32 devices in a mesh: seq: 16 (over z, y, core), blk: 2 (over x).
Axes of the slice: x: 2, y: 2, z: 4, core: 2. Of those that a mesh axis runs over, the one named last changes fastest.
Arguments:
- hidden: bfloat16 [32, 1024, 768], P('seq', 'blk'), may hold values from -6 to 6
- segments: int32 [32, 1024], P('seq', 'blk'), may hold values from 0 to 1023, as said below
- query_matrix: bfloat16 [768, 768], replicated, may hold values from -0.21875 to 0.21875
- query_bias: bfloat16 [768], replicated, may hold values from -3 to 3
- key_matrix: bfloat16 [768, 768], replicated, may hold values from -0.21875 to 0.21875
- value_matrix: bfloat16 [768, 768], replicated, may hold values from -0.21875 to 0.21875
- value_bias: bfloat16 [768], replicated, may hold values from -3 to 3
- output_matrix: bfloat16 [768, 768], replicated, may hold values from -0.875 to 0.875
- output_bias: bfloat16 [768], replicated, may hold values from -3 to 3
- first_gain: bfloat16 [768], replicated, may hold values from 0.5 to 1.5
- first_shift: bfloat16 [768], replicated, may hold values from -3 to 3
- inner_matrix: bfloat16 [768, 3072], replicated, may hold values from -0.21875 to 0.21875
- inner_bias: bfloat16 [3072], replicated, may hold values from -3 to 3
- outer_matrix: bfloat16 [3072, 768], replicated, may hold values from -0.109375 to 0.109375
- outer_bias: bfloat16 [768], replicated, may hold values from -3 to 3
- second_gain: bfloat16 [768], replicated, may hold values from 0.5 to 1.5
- second_shift: bfloat16 [768], replicated, may hold values from -3 to 3
- cotangent: bfloat16 [32, 1024, 768], P('seq', 'blk'), may hold values from -6 to 6
Outputs:
- layer_out: bfloat16 [32, 1024, 768], P('seq', 'blk')
- hidden_grad: float32 [32, 1024, 768], P('seq', 'blk')
- query_weight_grad: float32 [768, 768], P('seq', 'blk')
- query_bias_grad: float32 [768], replicated
- key_matrix_gradient: float32 [768, 768], P('seq', 'blk')
- value_weight_grad: float32 [768, 768], P('seq', 'blk')
- value_bias_grad: float32 [768], replicated
- output_weight_grad: float32 [768, 768], P('seq', 'blk')
- output_bias_grad: float32 [768], replicated
- first_gain_grad: float32 [768], replicated
- first_shift_grad: float32 [768], replicated
- inner_weight_grad: float32 [768, 3072], P('seq', 'blk')
- inner_bias_grad: float32 [3072], replicated
- outer_weight_grad: float32 [3072, 768], P('seq', 'blk')
- outer_bias_grad: float32 [768], replicated
- second_gain_grad: float32 [768], replicated
- second_shift_grad: float32 [768], replicated
The draws below stay inside these ranges and needn't reach their ends.
Inputs may be any that keep to these rules, and one draw needn't show every extreme that they name: `segments`: each position's id is the first position of its word-region pair in the sequence, so ids never fall and equal ids mark one pair; the last position starts a pair of its own. Of the 2 sequences on one index of seq, one holds a pair that reaches from the positions of the first index of blk to those of the last.
All inputs are finite; a program needn't handle non-finite values.
Results may differ from the reference program's by a relative error of at most 0.014.
Values may be sent and summed in bfloat16 or wider, within the bound.
No kernel may reach another device: no remote copies, remote signals or barrier semaphores. Data moves between devices by JAX's collectives and lax.ppermute only.
A program may use at most 256 MiB of HBM per device.

```python
import math
import jax
import jax.numpy as jnp
from jax import lax

D = 768
HEADS = 12
HEAD = 64
FF = 3072
SEQS_DEV = 2
LEN_DEV = 512
SEG_GAP = 128
SEQS = 32
LEN = 1024


def draw_segments(key, part):
    first_key, second_key = jax.random.split(key)
    marks = (jax.random.randint(first_key, (SEQS, LEN), 0, SEG_GAP) == 0).astype(jnp.int32)
    position = jnp.arange(LEN, dtype=jnp.int32)[None, :]
    chosen = jax.random.randint(second_key, (SEQS // SEQS_DEV,), 0, SEQS_DEV)
    seq_index = jnp.arange(SEQS, dtype=jnp.int32)
    picked = (seq_index % SEQS_DEV == jnp.repeat(chosen, SEQS_DEV))[:, None]
    inside = (position >= LEN_DEV // 2) & (position < LEN - LEN_DEV // 2)
    marks = jnp.where(picked & inside, 0, marks)
    marks = jnp.where(position == 0, 1, marks)
    marks = jnp.where(position == LEN - 1, 1, marks)
    starts = jnp.where(marks == 1, position, jnp.zeros_like(position)).astype(jnp.int32)
    return lax.cummax(starts, axis=1).astype(jnp.int32)


def block_levels(stream_key, extent, shards, smallest, high):
    loudness, own = 1.0, jax.random.fold_in(stream_key, 6)
    for axis_at, parts in shards:
        heights = jnp.exp(jax.random.uniform(jax.random.fold_in(own, axis_at), (parts,), jnp.float32, smallest / len(shards), high / len(shards)))
        loudness = loudness * jnp.repeat(heights, extent[axis_at] // parts).reshape([-1 if axis == axis_at else 1 for axis in range(len(extent))])
    return loudness


def bell_draw(key, extent, width, reach, shards=(), kind=jnp.bfloat16):
    entries = width * jax.random.normal(key, extent, jnp.float32)
    if shards:
        entries = entries * block_levels(key, extent, shards, -0.22, 0.18)
    return jnp.clip(entries, -reach, reach).astype(kind)


def setup_inputs(seed: int = 0) -> dict:
    arg_keys = jax.random.split(jax.random.key(seed), 19)
    hidden = bell_draw(arg_keys[0], (SEQS, LEN, D), 1.0, 6.0, ((0, 16), (1, 2)))
    segments = draw_segments(jax.random.fold_in(arg_keys[18], 71), 0)
    query_matrix = bell_draw(arg_keys[2], (D, D), D ** -0.5, 0.21875)
    query_bias = bell_draw(arg_keys[3], (D,), 0.5, 3.0)
    key_matrix = bell_draw(arg_keys[4], (D, D), D ** -0.5, 0.21875)
    value_matrix = bell_draw(arg_keys[5], (D, D), D ** -0.5, 0.21875)
    value_bias = bell_draw(arg_keys[6], (D,), 0.5, 3.0)
    output_matrix = bell_draw(arg_keys[7], (D, D), (D // 16) ** -0.5, 0.875)
    output_bias = bell_draw(arg_keys[8], (D,), 0.5, 3.0)
    first_gain = jnp.clip(1.0 + 0.1 * jax.random.normal(arg_keys[9], (D,), jnp.float32), 0.5, 1.5).astype(jnp.bfloat16)
    first_shift = bell_draw(arg_keys[10], (D,), 0.5, 3.0)
    inner_matrix = bell_draw(arg_keys[11], (D, FF), D ** -0.5, 0.21875)
    inner_bias = bell_draw(arg_keys[12], (FF,), 0.5, 3.0)
    outer_matrix = bell_draw(arg_keys[13], (FF, D), FF ** -0.5, 0.109375)
    outer_bias = bell_draw(arg_keys[14], (D,), 0.5, 3.0)
    second_gain = jnp.clip(1.0 + 0.1 * jax.random.normal(arg_keys[15], (D,), jnp.float32), 0.5, 1.5).astype(jnp.bfloat16)
    second_shift = bell_draw(arg_keys[16], (D,), 0.5, 3.0)
    cotangent = bell_draw(arg_keys[17], (SEQS, LEN, D), 1.0, 6.0, ((0, 16), (1, 2)))
    return {"hidden": hidden, "segments": segments, "query_matrix": query_matrix, "query_bias": query_bias, "key_matrix": key_matrix, "value_matrix": value_matrix, "value_bias": value_bias, "output_matrix": output_matrix, "output_bias": output_bias, "first_gain": first_gain, "first_shift": first_shift, "inner_matrix": inner_matrix, "inner_bias": inner_bias, "outer_matrix": outer_matrix, "outer_bias": outer_bias, "second_gain": second_gain, "second_shift": second_shift, "cotangent": cotangent}


@jax.custom_vjp
def low(v):
    return lax.optimization_barrier(v.astype(jnp.bfloat16)).astype(jnp.float32)

@jax.custom_vjp
def low_back(v):
    return v

def low_keep(v):
    return (low(v), None)

def low_pass(kept, grad):
    return (grad,)

def back_keep(v):
    return (v, None)

def back_low(kept, grad):
    return (low(grad),)
low.defvjp(low_keep, low_pass)
low_back.defvjp(back_keep, back_low)
NEGATIVE = -1e+30
EPSILON = 1e-12
HIGHEST = lax.Precision.HIGHEST

def matmul(operand, matrix):
    return jnp.dot(operand, matrix, precision=HIGHEST, preferred_element_type=jnp.float32)

def layer_norm(values, norm_gain, norm_shift):
    centre = values - lax.optimization_barrier(jnp.mean(values, axis=-1, keepdims=True))
    spread = lax.optimization_barrier(jnp.mean(centre * centre, axis=-1, keepdims=True))
    return centre * lax.rsqrt(spread + EPSILON) * norm_gain + norm_shift

def attention(queries, key_proj, value_proj, segment):
    length = queries.shape[0]
    block_size = math.gcd(length, 512)
    block_count = length // block_size
    key_heads = key_proj.reshape(length, HEADS, HEAD)
    value_heads = value_proj.reshape(length, HEADS, HEAD)

    def one_block(sequence):
        query_block, seg_block = sequence
        scores = jnp.einsum('qhd,khd->hqk', query_block, key_heads, precision=HIGHEST) * HEAD ** (-0.5)
        scores = low_back(scores)
        same_doc = (seg_block[:, None] == segment[None, :])[None]
        masked = jnp.where(same_doc, scores, NEGATIVE)
        row_max = lax.optimization_barrier(jnp.max(masked, axis=-1, keepdims=True))
        log_total = row_max + jnp.log(lax.optimization_barrier(jnp.sum(jnp.exp(masked - row_max), axis=-1, keepdims=True)))
        attn_probs = low(jnp.exp(masked - log_total))
        return jnp.einsum('hqk,khd->qhd', attn_probs, value_heads, precision=HIGHEST)
    blocks = lax.map(jax.checkpoint(one_block), (queries.reshape(block_count, block_size, HEADS, HEAD), segment.reshape(block_count, block_size)))
    return blocks.reshape(length, HEADS * HEAD)

def layer(inputs, segment, query_matrix, query_bias, key_matrix, value_matrix, value_bias, output_matrix, output_bias, first_gain, first_shift, inner_matrix, inner_bias, outer_matrix, outer_bias, second_gain, second_shift):
    queries = low(low_back(matmul(inputs, query_matrix) + query_bias))
    key_proj = low(low_back(matmul(inputs, key_matrix)))
    value_proj = low(low_back(matmul(inputs, value_matrix) + value_bias))
    context = low(low_back(attention(queries, key_proj, value_proj, segment)))
    attn_out = low_back(matmul(context, output_matrix) + output_bias)
    first_norm = layer_norm(inputs + attn_out, first_gain, first_shift)
    inner = low_back(matmul(low(first_norm), inner_matrix) + inner_bias)
    activation_reduced = low(jax.nn.gelu(inner, approximate=False))
    outer = low_back(matmul(activation_reduced, outer_matrix) + outer_bias)
    return layer_norm(first_norm + outer, second_gain, second_shift)

def reference(hidden, segments, query_matrix, query_bias, key_matrix, value_matrix, value_bias, output_matrix, output_bias, first_gain, first_shift, inner_matrix, inner_bias, outer_matrix, outer_bias, second_gain, second_shift, cotangent):
    params = tuple((weight.astype(jnp.float32) for weight in (query_matrix, query_bias, key_matrix, value_matrix, value_bias, output_matrix, output_bias, first_gain, first_shift, inner_matrix, inner_bias, outer_matrix, outer_bias, second_gain, second_shift)))

    def step(totals, sequence):
        row_in, row_seg, row_cot = sequence

        def forward(inputs, *weights):
            return layer(inputs, row_seg, *weights)
        output, pullback = jax.vjp(forward, row_in, *params)
        gradients = pullback(row_cot)
        totals = tuple((summed + extra for summed, extra in zip(totals, gradients[1:])))
        return (totals, (output.astype(jnp.bfloat16), gradients[0]))
    start_sums = tuple((jnp.zeros_like(weight) for weight in params))
    totals, outputs = lax.scan(step, start_sums, (hidden.astype(jnp.float32), segments, cotangent.astype(jnp.float32)))
    return (outputs[0], outputs[1], totals[0], totals[1], totals[2], totals[3], totals[4], totals[5], totals[6], totals[7], totals[8], totals[9], totals[10], totals[11], totals[12], totals[13], totals[14])
```

```python
import functools
import math

import jax
import jax.numpy as jnp
from jax import lax
from jax.experimental import pallas as pl
from jax.experimental.pallas import tpu as pltpu
from jax.sharding import PartitionSpec as P

HEADS = 12
HEAD = 64


NEGATIVE = -1e30
EPSILON = 1e-12


def layer_norm(values, norm_gain, norm_shift):
    centre = values - jnp.mean(values, axis=-1, keepdims=True)
    spread = jnp.mean(centre * centre, axis=-1, keepdims=True)
    return centre * lax.rsqrt(spread + EPSILON) * norm_gain + norm_shift


def gelu_exact(values):
    return jax.nn.gelu(values, approximate=False)


def linear(operand, matrix):
    return jnp.dot(operand, matrix, preferred_element_type=jnp.float32)


def split_heads(values):
    return values.reshape(values.shape[0], values.shape[1], HEADS, HEAD)


def block_scores(query_block, key_block, score_scale):
    return (
        jnp.einsum("sqhd,skhd->shqk", query_block, key_block, preferred_element_type=jnp.float32)
        * score_scale
    )


def attention_grads(
    query_block, key_block, value_block, dctx_block, same_doc, log_total, row_delta, score_scale
):
    attn_probs = jnp.where(
        same_doc,
        jnp.exp(block_scores(query_block, key_block, score_scale) - log_total[..., None]),
        0.0,
    )
    slopes = jnp.einsum(
        "sqhd,skhd->shqk", dctx_block, value_block, preferred_element_type=jnp.float32
    )
    return (attn_probs, (attn_probs * (slopes - row_delta[..., None])).astype(jnp.bfloat16))


def over_blocks(length, step, initial):
    block_size = math.gcd(length, 512)

    def scan_step(carried, block_index):
        return (step(carried, block_index * block_size, block_size), None)

    result, unused = lax.scan(scan_step, initial, jnp.arange(length // block_size, dtype=jnp.int32))
    return result


def general(
    hidden,
    segments,
    query_matrix,
    query_bias,
    key_matrix,
    value_matrix,
    value_bias,
    output_matrix,
    output_bias,
    first_gain,
    first_shift,
    inner_matrix,
    inner_bias,
    outer_matrix,
    outer_bias,
    second_gain,
    second_shift,
    cotangent,
):
    seq_count, row_count, model_width = hidden.shape
    score_scale = HEAD ** (-0.5)
    single_float = jnp.float32
    bf16 = jnp.bfloat16
    queries = (linear(hidden, query_matrix) + query_bias.astype(single_float)).astype(bf16)
    key_proj = linear(hidden, key_matrix).astype(bf16)
    value_proj = (linear(hidden, value_matrix) + value_bias.astype(single_float)).astype(bf16)
    seg_all = lax.all_gather(segments, "blk", axis=1, tiled=True)
    keys_all, values_all = (
        lax.all_gather(key_proj, "blk", axis=1, tiled=True),
        lax.all_gather(value_proj, "blk", axis=1, tiled=True),
    )
    length = seg_all.shape[1]
    query_heads = split_heads(queries)
    key_heads = split_heads(keys_all)
    value_heads = split_heads(values_all)

    def key_slices(offset, block_size):
        key_segs = lax.dynamic_slice_in_dim(seg_all, offset, block_size, 1)
        same_doc = (segments[:, :, None] == key_segs[:, None, :])[:, None]
        key_block = lax.dynamic_slice_in_dim(key_heads, offset, block_size, 1)
        value_block = lax.dynamic_slice_in_dim(value_heads, offset, block_size, 1)
        return (same_doc, key_block, value_block)

    def stats_step(carried, offset, block_size):
        same_doc, key_block, value_block = key_slices(offset, block_size)
        running_max, running_sum = carried
        scores = jnp.where(same_doc, block_scores(query_heads, key_block, score_scale), NEGATIVE)
        higher = jnp.maximum(running_max, jnp.max(scores, axis=-1))
        weights = jnp.where(same_doc, jnp.exp(scores - higher[..., None]), 0.0)
        return (higher, running_sum * jnp.exp(running_max - higher) + jnp.sum(weights, axis=-1))

    stat_shape = (seq_count, HEADS, row_count)
    running_max, running_sum = over_blocks(
        length,
        stats_step,
        (jnp.full(stat_shape, NEGATIVE, single_float), jnp.zeros(stat_shape, single_float)),
    )
    log_total = running_max + jnp.log(running_sum)

    def context_step(carried, offset, block_size):
        same_doc, key_block, value_block = key_slices(offset, block_size)
        attn_probs = jnp.where(
            same_doc,
            jnp.exp(block_scores(query_heads, key_block, score_scale) - log_total[..., None]),
            0.0,
        )
        return carried + jnp.einsum(
            "shqk,skhd->sqhd",
            attn_probs.astype(bf16),
            value_block,
            preferred_element_type=single_float,
        )

    head_zeros = jnp.zeros((seq_count, row_count, HEADS, HEAD), single_float)
    context = over_blocks(length, context_step, head_zeros)
    context_reduced = context.reshape(seq_count, row_count, model_width).astype(bf16)
    attn_out = linear(context_reduced, output_matrix) + output_bias.astype(single_float)
    first_pre = hidden.astype(single_float) + attn_out
    first_norm, first_back = jax.vjp(
        layer_norm, first_pre, first_gain.astype(single_float), first_shift.astype(single_float)
    )
    first_reduced = first_norm.astype(bf16)
    inner = linear(first_reduced, inner_matrix) + inner_bias.astype(single_float)
    act_full, gelu_back = jax.vjp(gelu_exact, inner)
    activation_reduced = act_full.astype(bf16)
    outer = linear(activation_reduced, outer_matrix) + outer_bias.astype(single_float)
    layer_full, second_back = jax.vjp(
        layer_norm,
        first_norm + outer,
        second_gain.astype(single_float),
        second_shift.astype(single_float),
    )
    layer_out = layer_full.astype(bf16)
    second_pre_grad, second_gain_grad, second_shift_grad = second_back(
        cotangent.astype(single_float)
    )
    outer_gradient_reduced = second_pre_grad.astype(bf16)
    outer_weight_grad = jnp.einsum(
        "gvx,gvm->xm",
        activation_reduced,
        outer_gradient_reduced,
        preferred_element_type=single_float,
    )
    outer_bias_grad = jnp.sum(outer_gradient_reduced.astype(single_float), axis=(0, 1))
    activation_gradient = jnp.einsum(
        "rzo,uo->rzu", outer_gradient_reduced, outer_matrix, preferred_element_type=single_float
    )
    inner_gradient_reduced = gelu_back(activation_gradient)[0].astype(bf16)
    inner_weight_grad = jnp.einsum(
        "ret,reu->tu", first_reduced, inner_gradient_reduced, preferred_element_type=single_float
    )
    inner_bias_grad = jnp.sum(inner_gradient_reduced.astype(single_float), axis=(0, 1))
    first_norm_grad = second_pre_grad + jnp.einsum(
        "aoi,ni->aon", inner_gradient_reduced, inner_matrix, preferred_element_type=single_float
    )
    first_pre_grad, first_gain_grad, first_shift_grad = first_back(first_norm_grad)
    attention_gradient_reduced = first_pre_grad.astype(bf16)
    output_weight_grad = jnp.einsum(
        "tfm,tfc->mc",
        context_reduced,
        attention_gradient_reduced,
        preferred_element_type=single_float,
    )
    output_bias_grad = jnp.sum(attention_gradient_reduced.astype(single_float), axis=(0, 1))
    dctx_low = jnp.einsum(
        "upx,cx->upc",
        attention_gradient_reduced,
        output_matrix,
        preferred_element_type=single_float,
    ).astype(bf16)
    dctx_heads = split_heads(dctx_low)
    row_delta = jnp.transpose(
        jnp.sum(dctx_heads.astype(single_float) * context, axis=-1), (0, 2, 1)
    )

    def query_step(carried, offset, block_size):
        same_doc, key_block, value_block = key_slices(offset, block_size)
        attn_probs, dscores = attention_grads(
            query_heads,
            key_block,
            value_block,
            dctx_heads,
            same_doc,
            log_total,
            row_delta,
            score_scale,
        )
        return carried + score_scale * jnp.einsum(
            "shqk,skhd->sqhd", dscores, key_block, preferred_element_type=single_float
        )

    query_grad = over_blocks(length, query_step, head_zeros)
    query_all, dctx_all = (
        lax.all_gather(queries, "blk", axis=1, tiled=True),
        lax.all_gather(dctx_low, "blk", axis=1, tiled=True),
    )
    lse_all, delta_all = (
        lax.all_gather(log_total, "blk", axis=2, tiled=True),
        lax.all_gather(row_delta, "blk", axis=2, tiled=True),
    )
    query_all_heads = split_heads(query_all)
    dctx_all_heads = split_heads(dctx_all)
    own_keys = split_heads(key_proj)
    own_values = split_heads(value_proj)

    def key_step(carried, offset, block_size):
        query_segs = lax.dynamic_slice_in_dim(seg_all, offset, block_size, 1)
        same_doc = (query_segs[:, :, None] == segments[:, None, :])[:, None]
        query_block = lax.dynamic_slice_in_dim(query_all_heads, offset, block_size, 1)
        dctx_block = lax.dynamic_slice_in_dim(dctx_all_heads, offset, block_size, 1)
        lse_block = lax.dynamic_slice_in_dim(lse_all, offset, block_size, 2)
        delta_block = lax.dynamic_slice_in_dim(delta_all, offset, block_size, 2)
        key_sum, value_sum = carried
        attn_probs, dscores = attention_grads(
            query_block,
            own_keys,
            own_values,
            dctx_block,
            same_doc,
            lse_block,
            delta_block,
            score_scale,
        )
        key_sum = key_sum + score_scale * jnp.einsum(
            "shqk,sqhd->skhd", dscores, query_block, preferred_element_type=single_float
        )
        value_sum = value_sum + jnp.einsum(
            "shqk,sqhd->skhd",
            attn_probs.astype(bf16),
            dctx_block,
            preferred_element_type=single_float,
        )
        return (key_sum, value_sum)

    key_grad, value_grad = over_blocks(length, key_step, (head_zeros, head_zeros))
    query_gradient_reduced = query_grad.reshape(seq_count, row_count, model_width).astype(bf16)
    key_gradient_reduced = key_grad.reshape(seq_count, row_count, model_width).astype(bf16)
    value_gradient_reduced = value_grad.reshape(seq_count, row_count, model_width).astype(bf16)
    query_weight_grad = jnp.einsum(
        "tfm,tfc->mc", hidden, query_gradient_reduced, preferred_element_type=single_float
    )
    query_bias_grad = jnp.sum(query_gradient_reduced.astype(single_float), axis=(0, 1))
    key_matrix_gradient = jnp.einsum(
        "tfm,tfc->mc", hidden, key_gradient_reduced, preferred_element_type=single_float
    )
    value_weight_grad = jnp.einsum(
        "tfm,tfc->mc", hidden, value_gradient_reduced, preferred_element_type=single_float
    )
    value_bias_grad = jnp.sum(value_gradient_reduced.astype(single_float), axis=(0, 1))
    hidden_grad = first_pre_grad + jnp.einsum(
        "upx,cx->upc", query_gradient_reduced, query_matrix, preferred_element_type=single_float
    )
    hidden_grad = hidden_grad + jnp.einsum(
        "upx,cx->upc", key_gradient_reduced, key_matrix, preferred_element_type=single_float
    )
    hidden_grad = hidden_grad + jnp.einsum(
        "upx,cx->upc", value_gradient_reduced, value_matrix, preferred_element_type=single_float
    )
    partial_sums = (
        lax.psum_scatter(query_weight_grad, "seq", scatter_dimension=0, tiled=True),
        lax.psum_scatter(key_matrix_gradient, "seq", scatter_dimension=0, tiled=True),
        lax.psum_scatter(value_weight_grad, "seq", scatter_dimension=0, tiled=True),
        lax.psum_scatter(output_weight_grad, "seq", scatter_dimension=0, tiled=True),
        lax.psum_scatter(inner_weight_grad, "seq", scatter_dimension=0, tiled=True),
        lax.psum_scatter(outer_weight_grad, "seq", scatter_dimension=0, tiled=True),
    )
    matrices = lax.psum_scatter(tuple(partial_sums), "blk", scatter_dimension=1, tiled=True)
    vectors = lax.psum(
        (
            query_bias_grad,
            value_bias_grad,
            output_bias_grad,
            first_gain_grad,
            first_shift_grad,
            inner_bias_grad,
            outer_bias_grad,
            second_gain_grad,
            second_shift_grad,
        ),
        ("seq", "blk"),
    )
    return (
        layer_out,
        hidden_grad,
        matrices[0],
        vectors[0],
        matrices[1],
        matrices[2],
        vectors[1],
        matrices[3],
        vectors[2],
        vectors[3],
        vectors[4],
        matrices[4],
        vectors[5],
        matrices[5],
        vectors[6],
        vectors[7],
        vectors[8],
    )


BF16 = jnp.bfloat16
F32 = jnp.float32
NN = ((1,), (0,))
NT = ((1,), (1,))
TN = ((0,), (0,))
GROUP = 256
PER_GROUP = GROUP // HEAD
TILE = 256
VMEM_LIMIT = 60 * 2**20


def mm(a, b, dims):
    return lax.dot_general(a, b, (dims, ((), ())), preferred_element_type=F32)


def fixed(shape):
    return pl.BlockSpec(shape, lambda *_: (0,) * len(shape), pipeline_mode=pl.Buffered(1))


def params(dimensions):
    return pltpu.CompilerParams(
        vmem_limit_bytes=VMEM_LIMIT, dimension_semantics=("arbitrary",) * dimensions
    )


def cost(flops, moved):
    return pl.CostEstimate(flops=int(flops), bytes_accessed=int(moved), transcendentals=0)


def head_lanes(shape, head):
    lane = lax.broadcasted_iota(jnp.int32, shape, 1)
    return (lane >= head * HEAD) & (lane < (head + 1) * HEAD)


def attention_forward_kernel(
    h_ref,
    wq_ref,
    wk_ref,
    wv_ref,
    bq_ref,
    bv_ref,
    segc_ref,
    segr_ref,
    q_ref,
    k_ref,
    v_ref,
    ctx_ref,
    lse_ref,
    mask_ref,
    vaug_ref,
):
    length = h_ref.shape[0]

    @pl.when(pl.program_id(0) == 0)
    def _():
        mask_ref[...] = jnp.where(segc_ref[...] == segr_ref[...], 0.0, NEGATIVE)

    h = h_ref[...]
    q_ref[...] = (mm(h, wq_ref[...], NN) + bq_ref[...]).astype(BF16)
    k_ref[...] = mm(h, wk_ref[...], NN).astype(BF16)
    v = (mm(h, wv_ref[...], NN) + bv_ref[...]).astype(BF16)
    v_ref[...] = v
    lane = lax.broadcasted_iota(jnp.int32, v.shape, 1)
    for head in range(PER_GROUP):
        other = (lane // 128) != (head // 2)
        filler = jnp.where(other, 1.0, 0.0).astype(BF16)
        vaug_ref[head] = jnp.where(head_lanes(v.shape, head), v, filler)

    def block(i, carry):
        rows = pl.ds(pl.multiple_of(i * TILE, TILE), TILE)
        qb = q_ref[rows, :] * BF16(HEAD**-0.5)
        halves = [None, None]
        stat_lane = lax.broadcasted_iota(jnp.int32, (TILE, 128), 1)
        stats = jnp.zeros((TILE, 128), F32)
        for head in range(PER_GROUP):
            qm = jnp.where(head_lanes(qb.shape, head), qb, BF16(0))
            s = mm(qm, k_ref[...], NT) + mask_ref[rows, :]
            top = jnp.max(s, axis=1, keepdims=True)
            e = jnp.exp(s - top).astype(BF16)
            o = mm(e, vaug_ref[head], NN)
            t = head // 2
            total = o[:, (1 - t) * 128 : (2 - t) * 128]
            part = o[:, t * 128 : (t + 1) * 128] / total
            halves[t] = part if halves[t] is None else halves[t] + part
            stats = jnp.where(stat_lane == head, top + jnp.log(total), stats)
        ctx_ref[rows, 0:128] = halves[0].astype(BF16)
        ctx_ref[rows, 128:256] = halves[1].astype(BF16)
        lse_ref[:, rows] = jnp.transpose(stats)[0:8]
        return carry

    lax.fori_loop(0, length // TILE, block, 0)


def attention_forward(h, wq, wk, wv, bq, bv, segc, segr):
    length, width = h.shape
    groups = width // GROUP
    column = pl.BlockSpec((width, GROUP), lambda g: (0, g))
    bias = pl.BlockSpec((1, GROUP), lambda g: (0, g))
    rows = pl.BlockSpec((length, GROUP), lambda g: (0, g))
    wide = jax.ShapeDtypeStruct((length, width), BF16)
    return pl.pallas_call(
        attention_forward_kernel,
        grid=(groups,),
        out_shape=(wide, wide, wide, wide, jax.ShapeDtypeStruct((8 * groups, length), F32)),
        in_specs=[
            fixed((length, width)),
            column,
            column,
            column,
            bias,
            bias,
            fixed((length, 1)),
            fixed((1, length)),
        ],
        out_specs=(rows, rows, rows, rows, pl.BlockSpec((8, length), lambda g: (g, 0))),
        scratch_shapes=[
            pltpu.VMEM((length, length), F32),
            pltpu.VMEM((PER_GROUP, length, GROUP), BF16),
        ],
        compiler_params=params(1),
        cost_estimate=cost(20e9, 12e6),
        name="attention_forward",
    )(h, wq, wk, wv, bq, bv, segc, segr)


def gelu_pair(u):
    z = jnp.abs(u) * 0.7071067811865476
    t = 1.0 / (1.0 + 0.3275911 * z)
    bell = jnp.exp(-z * z)
    poly = t * (
        0.127414796 + t * (-0.142248368 + t * (0.7107068705 + t * (-0.7265760135 + t * 0.5307027145)))
    )
    tail = poly * bell
    phi = jnp.where(u < 0, tail, 1.0 - tail)
    return (u * phi, phi + u * bell * 0.3989422804014327)


def normed(x):
    centre = x - jnp.mean(x, axis=1, keepdims=True)
    scale = lax.rsqrt(jnp.mean(centre * centre, axis=1, keepdims=True) + EPSILON)
    return (centre * scale, scale)


def norm_back(u, n, scale):
    return scale * (u - jnp.mean(u, axis=1, keepdims=True) - n * jnp.mean(u * n, axis=1, keepdims=True))


def row_sum(x):
    return jnp.sum(x, axis=0, keepdims=True)


def token_kernel(
    h_ref,
    ctx_ref,
    cot_ref,
    wo_ref,
    wi_ref,
    wp_ref,
    bi_ref,
    vec_ref,
    out_ref,
    first_ref,
    act_ref,
    og_ref,
    ig_ref,
    fp_ref,
    ag_ref,
    dctx_ref,
    sums_ref,
    isum_ref,
    slope_ref,
):
    @pl.when(pl.program_id(0) == 0)
    def _():
        sums_ref[...] = jnp.zeros_like(sums_ref)
        isum_ref[...] = jnp.zeros_like(isum_ref)

    ff = wi_ref.shape[1]
    chunk = 512
    output_bias, gain1, shift1 = vec_ref[0:1, :], vec_ref[1:2, :], vec_ref[2:3, :]
    outer_bias, gain2, shift2 = vec_ref[3:4, :], vec_ref[4:5, :], vec_ref[5:6, :]
    n1, r1 = normed(h_ref[...].astype(F32) + mm(ctx_ref[...], wo_ref[...], NN) + output_bias)
    fn = n1 * gain1 + shift1
    first = fn.astype(BF16)
    first_ref[...] = first
    for c in range(0, ff, chunk):
        act, slope = gelu_pair(mm(first, wi_ref[:, c : c + chunk], NN) + bi_ref[:, c : c + chunk])
        act_ref[:, c : c + chunk] = act.astype(BF16)
        slope_ref[:, c : c + chunk] = slope
    n2, r2 = normed(fn + mm(act_ref[...], wp_ref[...], NN) + outer_bias)
    out_ref[...] = (n2 * gain2 + shift2).astype(BF16)
    e = cot_ref[...].astype(F32)
    sums_ref[0:1, :] += row_sum(e * n2)
    sums_ref[1:2, :] += row_sum(e)
    sp = norm_back(e * gain2, n2, r2)
    og = sp.astype(BF16)
    og_ref[...] = og
    sums_ref[2:3, :] += row_sum(og.astype(F32))
    for c in range(0, ff, chunk):
        ig = (mm(og, wp_ref[c : c + chunk, :], NT) * slope_ref[:, c : c + chunk]).astype(BF16)
        ig_ref[:, c : c + chunk] = ig
        isum_ref[:, c : c + chunk] += row_sum(ig.astype(F32))
    d = sp + mm(ig_ref[...], wi_ref[...], NT)
    sums_ref[3:4, :] += row_sum(d * n1)
    sums_ref[4:5, :] += row_sum(d)
    fp = norm_back(d * gain1, n1, r1)
    fp_ref[...] = fp
    ag = fp.astype(BF16)
    ag_ref[...] = ag
    sums_ref[5:6, :] += row_sum(ag.astype(F32))
    dctx_ref[...] = mm(ag, wo_ref[...], NT).astype(BF16)


def token_pass(h, ctx, cot, wo, wi, wp, bi, vec):
    length, width = h.shape
    ff = wi.shape[1]
    rows = pl.BlockSpec((TILE, width), lambda i: (i, 0))
    wide_rows = pl.BlockSpec((TILE, ff), lambda i: (i, 0))
    low = jax.ShapeDtypeStruct((length, width), BF16)
    low_ff = jax.ShapeDtypeStruct((length, ff), BF16)
    return pl.pallas_call(
        token_kernel,
        grid=(length // TILE,),
        out_shape=(
            low,
            low,
            low_ff,
            low,
            low_ff,
            jax.ShapeDtypeStruct((length, width), F32),
            low,
            low,
            jax.ShapeDtypeStruct((8, width), F32),
            jax.ShapeDtypeStruct((1, ff), F32),
        ),
        in_specs=[
            rows,
            rows,
            rows,
            fixed((width, width)),
            fixed((width, ff)),
            fixed((ff, width)),
            fixed((1, ff)),
            fixed((8, width)),
        ],
        out_specs=(
            rows,
            rows,
            wide_rows,
            rows,
            wide_rows,
            rows,
            rows,
            rows,
            pl.BlockSpec((8, width), lambda i: (0, 0)),
            pl.BlockSpec((1, ff), lambda i: (0, 0)),
        ),
        scratch_shapes=[pltpu.VMEM((TILE, ff), F32)],
        compiler_params=params(1),
        cost_estimate=cost(21.7e9, 30e6),
        name="token_pass",
    )(h, ctx, cot, wo, wi, wp, bi, vec)


def product_kernel(a_ref, b_ref, out_ref):
    out_ref[...] = mm(a_ref[...], b_ref[...], TN).astype(out_ref.dtype)


def weight_grad(a, b, rows, columns, kind):
    length, height = a.shape
    width = b.shape[1]
    a_spec = pl.BlockSpec((length, rows), lambda i, j: (0, i))
    b_spec = pl.BlockSpec((length, columns), lambda i, j: (0, j))
    return pl.pallas_call(
        product_kernel,
        grid=(height // rows, width // columns),
        out_shape=jax.ShapeDtypeStruct((height, width), kind),
        in_specs=[a_spec, b_spec],
        out_specs=pl.BlockSpec((rows, columns), lambda i, j: (i, j)),
        compiler_params=params(2),
        cost_estimate=cost(2 * length * height * width, 2 * length * (height + width) + 2 * height * width),
        name="weight_grad",
    )(a, b)


def attention_backward_kernel(
    q_ref,
    k_ref,
    v_ref,
    dctx_ref,
    ctx_ref,
    lse_ref,
    segc_ref,
    segr_ref,
    dq_ref,
    dk_ref,
    dv_ref,
    sums_ref,
    delta_ref,
    total_ref,
    ds_ref,
    km_ref,
):
    length = q_ref.shape[0]
    prod = dctx_ref[...].astype(F32) * ctx_ref[...].astype(F32)
    high = prod.astype(BF16)
    rest = (prod - high.astype(F32)).astype(BF16)
    lane = lax.broadcasted_iota(jnp.int32, (8, GROUP), 1)
    head_of = lax.broadcasted_iota(jnp.int32, (8, GROUP), 0)
    chooser = jnp.where(lane // HEAD == head_of, 1.0, 0.0).astype(BF16)
    delta_ref[...] = mm(chooser, high, NT) + mm(chooser, rest, NT)
    total_ref[...] = jnp.zeros_like(total_ref)

    def block(j, carry):
        rows = pl.ds(pl.multiple_of(j * TILE, TILE), TILE)
        kb = k_ref[rows, :]
        vb = v_ref[rows, :]
        mask = jnp.where(segc_ref[rows, :] == segr_ref[...], 0.0, NEGATIVE)
        dk = jnp.zeros((TILE, GROUP), F32)
        dv = jnp.zeros((TILE, GROUP), F32)
        for head in range(PER_GROUP):
            mine = head_lanes((TILE, GROUP), head)
            km = jnp.where(mine, kb, BF16(0)) * BF16(HEAD**-0.5)
            vm = jnp.where(mine, vb, BF16(0))
            s = mm(km, q_ref[...], NT) + mask
            p = jnp.exp(s - lse_ref[head : head + 1, :])
            dp = mm(vm, dctx_ref[...], NT)
            ds = (p * (dp - delta_ref[head : head + 1, :])).astype(BF16)
            dv = jnp.where(mine, mm(p.astype(BF16), dctx_ref[...], NN), dv)
            dk = jnp.where(mine, mm(ds, q_ref[...], NN), dk)
            ds_ref[head * TILE : (head + 1) * TILE, :] = ds
            km_ref[head * TILE : (head + 1) * TILE, :] = km
        dkb = (dk * HEAD**-0.5).astype(BF16)
        dvb = dv.astype(BF16)
        dk_ref[rows, :] = dkb
        dv_ref[rows, :] = dvb
        total_ref[...] += mm(ds_ref[...], km_ref[...], TN)
        return carry + row_sum(dvb.astype(F32))

    dv_sum = lax.fori_loop(0, length // TILE, block, jnp.zeros((1, GROUP), F32))
    dq = total_ref[...].astype(BF16)
    dq_ref[...] = dq
    sums_ref[...] = jnp.zeros_like(sums_ref)
    sums_ref[0:1, :] = row_sum(dq.astype(F32))
    sums_ref[1:2, :] = dv_sum


def attention_backward(q, k, v, dctx, ctx, lse, segc, segr):
    length, width = q.shape
    groups = width // GROUP
    rows = pl.BlockSpec((length, GROUP), lambda g: (0, g))
    wide = jax.ShapeDtypeStruct((length, width), BF16)
    return pl.pallas_call(
        attention_backward_kernel,
        grid=(groups,),
        out_shape=(wide, wide, wide, jax.ShapeDtypeStruct((8, width), F32)),
        in_specs=[
            rows,
            rows,
            rows,
            rows,
            rows,
            pl.BlockSpec((8, length), lambda g: (g, 0)),
            fixed((length, 1)),
            fixed((1, length)),
        ],
        out_specs=(rows, rows, rows, pl.BlockSpec((8, GROUP), lambda g: (0, g))),
        scratch_shapes=[
            pltpu.VMEM((8, length), F32),
            pltpu.VMEM((length, GROUP), F32),
            pltpu.VMEM((PER_GROUP * TILE, length), BF16),
            pltpu.VMEM((PER_GROUP * TILE, GROUP), BF16),
        ],
        compiler_params=params(1),
        cost_estimate=cost(40e9, 14e6),
        name="attention_backward",
    )(q, k, v, dctx, ctx, lse, segc, segr)


def hidden_grad_kernel(fp_ref, dq_ref, dk_ref, dv_ref, wq_ref, wk_ref, wv_ref, out_ref):
    total = fp_ref[...] + mm(dq_ref[...], wq_ref[...], NT)
    total = total + mm(dk_ref[...], wk_ref[...], NT)
    out_ref[...] = (total + mm(dv_ref[...], wv_ref[...], NT)).astype(out_ref.dtype)


def hidden_grad_part(fp, dq, dk, dv, wq, wk, wv, part, kind):
    length, width = dq.shape
    half = length // 2
    steps = half // TILE
    rows = pl.BlockSpec((TILE, width), lambda i: (i + part * steps, 0))
    return pl.pallas_call(
        hidden_grad_kernel,
        grid=(steps,),
        out_shape=jax.ShapeDtypeStruct((half, width), kind),
        in_specs=[rows, rows, rows, rows] + [fixed((width, width))] * 3,
        out_specs=pl.BlockSpec((TILE, width), lambda i: (i, 0)),
        compiler_params=params(1),
        cost_estimate=cost(6 * half * width * width, 8e6),
        name="hidden_grad",
    )(fp, dq, dk, dv, wq, wk, wv)


def fast(
    hidden,
    segments,
    query_matrix,
    query_bias,
    key_matrix,
    value_matrix,
    value_bias,
    output_matrix,
    output_bias,
    first_gain,
    first_shift,
    inner_matrix,
    inner_bias,
    outer_matrix,
    outer_bias,
    second_gain,
    second_shift,
    cotangent,
):
    here = lax.axis_index("blk")
    swap = [(0, 1), (1, 0)]

    def own(x):
        return lax.dynamic_index_in_dim(x, here, 0, keepdims=False)

    def other(x):
        return lax.dynamic_index_in_dim(x, 1 - here, 0, keepdims=False)

    def trade(x):
        return lax.ppermute(x, "blk", swap)

    def whole(x):
        return jnp.concatenate([own(x), trade(other(x))], axis=0)

    def back(mine, received):
        first = jnp.where(here == 0, mine, received)
        second = jnp.where(here == 0, received, mine)
        return jnp.stack([first, second], axis=0)

    def row(x):
        return x.astype(F32)[None, :]

    h = whole(hidden)
    seg = whole(segments)
    cot = whole(cotangent)
    length, width = h.shape
    half = length // 2
    segc, segr = seg[:, None], seg[None, :]
    q, k, v, ctx, lse = attention_forward(
        h, query_matrix, key_matrix, value_matrix, row(query_bias), row(value_bias), segc, segr
    )
    empty = jnp.zeros((1, width), F32)
    vec = jnp.concatenate(
        [
            row(output_bias),
            row(first_gain),
            row(first_shift),
            row(outer_bias),
            row(second_gain),
            row(second_shift),
            empty,
            empty,
        ],
        axis=0,
    )
    out, first, act, og, ig, fp, ag, dctx, sums, isum = token_pass(
        h, ctx, cot, output_matrix, inner_matrix, outer_matrix, row(inner_bias), vec
    )
    layer_out = back(out[:half], trade(out[half:]))
    outer_grad = weight_grad(act, og, 512, width, BF16)
    inner_grad = weight_grad(first, ig, width, 512, BF16)
    output_grad = weight_grad(ctx, ag, width, width, BF16)
    dq, dk, dv, sums2 = attention_backward(q, k, v, dctx, ctx, lse, segc, segr)
    args = (fp, dq, dk, dv, query_matrix, key_matrix, value_matrix)
    away = hidden_grad_part(*args, 1, BF16)
    came = trade(away)
    home = hidden_grad_part(*args, 0, F32)
    query_grad = weight_grad(h, dq, width, width, BF16)
    key_grad = weight_grad(h, dk, width, width, BF16)
    value_grad = weight_grad(h, dv, width, width, BF16)
    hidden_grad = back(home, came.astype(F32))

    def scatter(x):
        y = lax.psum_scatter(x, "seq", scatter_dimension=0, tiled=True)
        return lax.psum_scatter(y, "blk", scatter_dimension=1, tiled=True).astype(F32)

    vectors = lax.psum((sums, isum[0], sums2), ("seq", "blk"))
    sums, isum, sums2 = vectors
    return (
        layer_out,
        hidden_grad,
        scatter(query_grad),
        sums2[0],
        scatter(key_grad),
        scatter(value_grad),
        sums2[1],
        scatter(output_grad),
        sums[5],
        sums[3],
        sums[4],
        scatter(inner_grad),
        isum,
        scatter(outer_grad),
        sums[2],
        sums[0],
        sums[1],
    )


def choose(sizes, *args):
    seq_count, row_count, width = args[0].shape
    whole_here = sizes[1] == 2 and seq_count == 2 and row_count % TILE == 0 and width % GROUP == 0
    return fast(*args) if whole_here and sizes[0] == 16 else general(*args)


def solution(mesh):
    sizes = (mesh.shape["seq"], mesh.shape["blk"])
    return jax.shard_map(
        functools.partial(choose, sizes),
        mesh=mesh,
        in_specs=(
            P("seq", "blk", None),
            P("seq", "blk"),
            P(),
            P(),
            P(),
            P(),
            P(),
            P(),
            P(),
            P(),
            P(),
            P(),
            P(),
            P(),
            P(),
            P(),
            P(),
            P("seq", "blk", None),
        ),
        out_specs=(
            P("seq", "blk", None),
            P("seq", "blk", None),
            P("seq", "blk"),
            P(),
            P("seq", "blk"),
            P("seq", "blk"),
            P(),
            P("seq", "blk"),
            P(),
            P(),
            P(),
            P("seq", "blk"),
            P(),
            P("seq", "blk"),
            P(),
            P(),
            P(),
        ),
        check_vma=False,
    )
```

```python
import functools
import math

import jax
import jax.numpy as jnp
from jax import lax
from jax.experimental import pallas as pl
from jax.experimental.pallas import tpu as pltpu
from jax.sharding import PartitionSpec as P

HEADS = 12
HEAD = 64


NEGATIVE = -1e30
EPSILON = 1e-12


def layer_norm(values, norm_gain, norm_shift):
    centre = values - jnp.mean(values, axis=-1, keepdims=True)
    spread = jnp.mean(centre * centre, axis=-1, keepdims=True)
    return centre * lax.rsqrt(spread + EPSILON) * norm_gain + norm_shift


def gelu_exact(values):
    return jax.nn.gelu(values, approximate=False)


def linear(operand, matrix):
    return jnp.dot(operand, matrix, preferred_element_type=jnp.float32)


def split_heads(values):
    return values.reshape(values.shape[0], values.shape[1], HEADS, HEAD)


def block_scores(query_block, key_block, score_scale):
    return (
        jnp.einsum("sqhd,skhd->shqk", query_block, key_block, preferred_element_type=jnp.float32)
        * score_scale
    )


def attention_grads(
    query_block, key_block, value_block, dctx_block, same_doc, log_total, row_delta, score_scale
):
    attn_probs = jnp.where(
        same_doc,
        jnp.exp(block_scores(query_block, key_block, score_scale) - log_total[..., None]),
        0.0,
    )
    slopes = jnp.einsum(
        "sqhd,skhd->shqk", dctx_block, value_block, preferred_element_type=jnp.float32
    )
    return (attn_probs, (attn_probs * (slopes - row_delta[..., None])).astype(jnp.bfloat16))


def over_blocks(length, step, initial):
    block_size = math.gcd(length, 512)

    def scan_step(carried, block_index):
        return (step(carried, block_index * block_size, block_size), None)

    result, unused = lax.scan(scan_step, initial, jnp.arange(length // block_size, dtype=jnp.int32))
    return result


def general(
    hidden,
    segments,
    query_matrix,
    query_bias,
    key_matrix,
    value_matrix,
    value_bias,
    output_matrix,
    output_bias,
    first_gain,
    first_shift,
    inner_matrix,
    inner_bias,
    outer_matrix,
    outer_bias,
    second_gain,
    second_shift,
    cotangent,
):
    seq_count, row_count, model_width = hidden.shape
    score_scale = HEAD ** (-0.5)
    single_float = jnp.float32
    bf16 = jnp.bfloat16
    queries = (linear(hidden, query_matrix) + query_bias.astype(single_float)).astype(bf16)
    key_proj = linear(hidden, key_matrix).astype(bf16)
    value_proj = (linear(hidden, value_matrix) + value_bias.astype(single_float)).astype(bf16)
    seg_all = lax.all_gather(segments, "blk", axis=1, tiled=True)
    keys_all, values_all = (
        lax.all_gather(key_proj, "blk", axis=1, tiled=True),
        lax.all_gather(value_proj, "blk", axis=1, tiled=True),
    )
    length = seg_all.shape[1]
    query_heads = split_heads(queries)
    key_heads = split_heads(keys_all)
    value_heads = split_heads(values_all)

    def key_slices(offset, block_size):
        key_segs = lax.dynamic_slice_in_dim(seg_all, offset, block_size, 1)
        same_doc = (segments[:, :, None] == key_segs[:, None, :])[:, None]
        key_block = lax.dynamic_slice_in_dim(key_heads, offset, block_size, 1)
        value_block = lax.dynamic_slice_in_dim(value_heads, offset, block_size, 1)
        return (same_doc, key_block, value_block)

    def stats_step(carried, offset, block_size):
        same_doc, key_block, value_block = key_slices(offset, block_size)
        running_max, running_sum = carried
        scores = jnp.where(same_doc, block_scores(query_heads, key_block, score_scale), NEGATIVE)
        higher = jnp.maximum(running_max, jnp.max(scores, axis=-1))
        weights = jnp.where(same_doc, jnp.exp(scores - higher[..., None]), 0.0)
        return (higher, running_sum * jnp.exp(running_max - higher) + jnp.sum(weights, axis=-1))

    stat_shape = (seq_count, HEADS, row_count)
    running_max, running_sum = over_blocks(
        length,
        stats_step,
        (jnp.full(stat_shape, NEGATIVE, single_float), jnp.zeros(stat_shape, single_float)),
    )
    log_total = running_max + jnp.log(running_sum)

    def context_step(carried, offset, block_size):
        same_doc, key_block, value_block = key_slices(offset, block_size)
        attn_probs = jnp.where(
            same_doc,
            jnp.exp(block_scores(query_heads, key_block, score_scale) - log_total[..., None]),
            0.0,
        )
        return carried + jnp.einsum(
            "shqk,skhd->sqhd",
            attn_probs.astype(bf16),
            value_block,
            preferred_element_type=single_float,
        )

    head_zeros = jnp.zeros((seq_count, row_count, HEADS, HEAD), single_float)
    context = over_blocks(length, context_step, head_zeros)
    context_reduced = context.reshape(seq_count, row_count, model_width).astype(bf16)
    attn_out = linear(context_reduced, output_matrix) + output_bias.astype(single_float)
    first_pre = hidden.astype(single_float) + attn_out
    first_norm, first_back = jax.vjp(
        layer_norm, first_pre, first_gain.astype(single_float), first_shift.astype(single_float)
    )
    first_reduced = first_norm.astype(bf16)
    inner = linear(first_reduced, inner_matrix) + inner_bias.astype(single_float)
    act_full, gelu_back = jax.vjp(gelu_exact, inner)
    activation_reduced = act_full.astype(bf16)
    outer = linear(activation_reduced, outer_matrix) + outer_bias.astype(single_float)
    layer_full, second_back = jax.vjp(
        layer_norm,
        first_norm + outer,
        second_gain.astype(single_float),
        second_shift.astype(single_float),
    )
    layer_out = layer_full.astype(bf16)
    second_pre_grad, second_gain_grad, second_shift_grad = second_back(
        cotangent.astype(single_float)
    )
    outer_gradient_reduced = second_pre_grad.astype(bf16)
    outer_weight_grad = jnp.einsum(
        "gvx,gvm->xm",
        activation_reduced,
        outer_gradient_reduced,
        preferred_element_type=single_float,
    )
    outer_bias_grad = jnp.sum(outer_gradient_reduced.astype(single_float), axis=(0, 1))
    activation_gradient = jnp.einsum(
        "rzo,uo->rzu", outer_gradient_reduced, outer_matrix, preferred_element_type=single_float
    )
    inner_gradient_reduced = gelu_back(activation_gradient)[0].astype(bf16)
    inner_weight_grad = jnp.einsum(
        "ret,reu->tu", first_reduced, inner_gradient_reduced, preferred_element_type=single_float
    )
    inner_bias_grad = jnp.sum(inner_gradient_reduced.astype(single_float), axis=(0, 1))
    first_norm_grad = second_pre_grad + jnp.einsum(
        "aoi,ni->aon", inner_gradient_reduced, inner_matrix, preferred_element_type=single_float
    )
    first_pre_grad, first_gain_grad, first_shift_grad = first_back(first_norm_grad)
    attention_gradient_reduced = first_pre_grad.astype(bf16)
    output_weight_grad = jnp.einsum(
        "tfm,tfc->mc",
        context_reduced,
        attention_gradient_reduced,
        preferred_element_type=single_float,
    )
    output_bias_grad = jnp.sum(attention_gradient_reduced.astype(single_float), axis=(0, 1))
    dctx_low = jnp.einsum(
        "upx,cx->upc",
        attention_gradient_reduced,
        output_matrix,
        preferred_element_type=single_float,
    ).astype(bf16)
    dctx_heads = split_heads(dctx_low)
    row_delta = jnp.transpose(
        jnp.sum(dctx_heads.astype(single_float) * context, axis=-1), (0, 2, 1)
    )

    def query_step(carried, offset, block_size):
        same_doc, key_block, value_block = key_slices(offset, block_size)
        attn_probs, dscores = attention_grads(
            query_heads,
            key_block,
            value_block,
            dctx_heads,
            same_doc,
            log_total,
            row_delta,
            score_scale,
        )
        return carried + score_scale * jnp.einsum(
            "shqk,skhd->sqhd", dscores, key_block, preferred_element_type=single_float
        )

    query_grad = over_blocks(length, query_step, head_zeros)
    query_all, dctx_all = (
        lax.all_gather(queries, "blk", axis=1, tiled=True),
        lax.all_gather(dctx_low, "blk", axis=1, tiled=True),
    )
    lse_all, delta_all = (
        lax.all_gather(log_total, "blk", axis=2, tiled=True),
        lax.all_gather(row_delta, "blk", axis=2, tiled=True),
    )
    query_all_heads = split_heads(query_all)
    dctx_all_heads = split_heads(dctx_all)
    own_keys = split_heads(key_proj)
    own_values = split_heads(value_proj)

    def key_step(carried, offset, block_size):
        query_segs = lax.dynamic_slice_in_dim(seg_all, offset, block_size, 1)
        same_doc = (query_segs[:, :, None] == segments[:, None, :])[:, None]
        query_block = lax.dynamic_slice_in_dim(query_all_heads, offset, block_size, 1)
        dctx_block = lax.dynamic_slice_in_dim(dctx_all_heads, offset, block_size, 1)
        lse_block = lax.dynamic_slice_in_dim(lse_all, offset, block_size, 2)
        delta_block = lax.dynamic_slice_in_dim(delta_all, offset, block_size, 2)
        key_sum, value_sum = carried
        attn_probs, dscores = attention_grads(
            query_block,
            own_keys,
            own_values,
            dctx_block,
            same_doc,
            lse_block,
            delta_block,
            score_scale,
        )
        key_sum = key_sum + score_scale * jnp.einsum(
            "shqk,sqhd->skhd", dscores, query_block, preferred_element_type=single_float
        )
        value_sum = value_sum + jnp.einsum(
            "shqk,sqhd->skhd",
            attn_probs.astype(bf16),
            dctx_block,
            preferred_element_type=single_float,
        )
        return (key_sum, value_sum)

    key_grad, value_grad = over_blocks(length, key_step, (head_zeros, head_zeros))
    query_gradient_reduced = query_grad.reshape(seq_count, row_count, model_width).astype(bf16)
    key_gradient_reduced = key_grad.reshape(seq_count, row_count, model_width).astype(bf16)
    value_gradient_reduced = value_grad.reshape(seq_count, row_count, model_width).astype(bf16)
    query_weight_grad = jnp.einsum(
        "tfm,tfc->mc", hidden, query_gradient_reduced, preferred_element_type=single_float
    )
    query_bias_grad = jnp.sum(query_gradient_reduced.astype(single_float), axis=(0, 1))
    key_matrix_gradient = jnp.einsum(
        "tfm,tfc->mc", hidden, key_gradient_reduced, preferred_element_type=single_float
    )
    value_weight_grad = jnp.einsum(
        "tfm,tfc->mc", hidden, value_gradient_reduced, preferred_element_type=single_float
    )
    value_bias_grad = jnp.sum(value_gradient_reduced.astype(single_float), axis=(0, 1))
    hidden_grad = first_pre_grad + jnp.einsum(
        "upx,cx->upc", query_gradient_reduced, query_matrix, preferred_element_type=single_float
    )
    hidden_grad = hidden_grad + jnp.einsum(
        "upx,cx->upc", key_gradient_reduced, key_matrix, preferred_element_type=single_float
    )
    hidden_grad = hidden_grad + jnp.einsum(
        "upx,cx->upc", value_gradient_reduced, value_matrix, preferred_element_type=single_float
    )
    partial_sums = (
        lax.psum_scatter(query_weight_grad, "seq", scatter_dimension=0, tiled=True),
        lax.psum_scatter(key_matrix_gradient, "seq", scatter_dimension=0, tiled=True),
        lax.psum_scatter(value_weight_grad, "seq", scatter_dimension=0, tiled=True),
        lax.psum_scatter(output_weight_grad, "seq", scatter_dimension=0, tiled=True),
        lax.psum_scatter(inner_weight_grad, "seq", scatter_dimension=0, tiled=True),
        lax.psum_scatter(outer_weight_grad, "seq", scatter_dimension=0, tiled=True),
    )
    matrices = lax.psum_scatter(tuple(partial_sums), "blk", scatter_dimension=1, tiled=True)
    vectors = lax.psum(
        (
            query_bias_grad,
            value_bias_grad,
            output_bias_grad,
            first_gain_grad,
            first_shift_grad,
            inner_bias_grad,
            outer_bias_grad,
            second_gain_grad,
            second_shift_grad,
        ),
        ("seq", "blk"),
    )
    return (
        layer_out,
        hidden_grad,
        matrices[0],
        vectors[0],
        matrices[1],
        matrices[2],
        vectors[1],
        matrices[3],
        vectors[2],
        vectors[3],
        vectors[4],
        matrices[4],
        vectors[5],
        matrices[5],
        vectors[6],
        vectors[7],
        vectors[8],
    )


BF16 = jnp.bfloat16
F32 = jnp.float32
NN = ((1,), (0,))
NT = ((1,), (1,))
TN = ((0,), (0,))
GROUP = 256
PER_GROUP = GROUP // HEAD
TILE = 256
VMEM_LIMIT = 60 * 2**20


def mm(a, b, dims):
    return lax.dot_general(a, b, (dims, ((), ())), preferred_element_type=F32)


def fixed(shape):
    return pl.BlockSpec(shape, lambda *_: (0,) * len(shape), pipeline_mode=pl.Buffered(1))


def params(dimensions):
    return pltpu.CompilerParams(
        vmem_limit_bytes=VMEM_LIMIT, dimension_semantics=("arbitrary",) * dimensions
    )


def cost(flops, moved):
    return pl.CostEstimate(flops=int(flops), bytes_accessed=int(moved), transcendentals=0)


def head_lanes(shape, head):
    lane = lax.broadcasted_iota(jnp.int32, shape, 1)
    return (lane >= head * HEAD) & (lane < (head + 1) * HEAD)


def attention_forward_kernel(
    h_ref,
    wq_ref,
    wk_ref,
    wv_ref,
    bq_ref,
    bv_ref,
    segc_ref,
    segr_ref,
    q_ref,
    k_ref,
    v_ref,
    ctx_ref,
    lse_ref,
    mask_ref,
    vaug_ref,
):
    length = h_ref.shape[0]

    @pl.when(pl.program_id(0) == 0)
    def _():
        mask_ref[...] = jnp.where(segc_ref[...] == segr_ref[...], 0.0, NEGATIVE)

    h = h_ref[...]
    q_ref[...] = (mm(h, wq_ref[...], NN) + bq_ref[...]).astype(BF16)
    k_ref[...] = mm(h, wk_ref[...], NN).astype(BF16)
    v = (mm(h, wv_ref[...], NN) + bv_ref[...]).astype(BF16)
    v_ref[...] = v
    lane = lax.broadcasted_iota(jnp.int32, v.shape, 1)
    for head in range(PER_GROUP):
        other = (lane // 128) != (head // 2)
        filler = jnp.where(other, 1.0, 0.0).astype(BF16)
        vaug_ref[head] = jnp.where(head_lanes(v.shape, head), v, filler)

    def block(i, carry):
        rows = pl.ds(pl.multiple_of(i * TILE, TILE), TILE)
        qb = q_ref[rows, :] * BF16(HEAD**-0.5)
        halves = [None, None]
        stat_lane = lax.broadcasted_iota(jnp.int32, (TILE, 128), 1)
        stats = jnp.zeros((TILE, 128), F32)
        for head in range(PER_GROUP):
            qm = jnp.where(head_lanes(qb.shape, head), qb, BF16(0))
            s = mm(qm, k_ref[...], NT) + mask_ref[rows, :]
            top = jnp.max(s, axis=1, keepdims=True)
            e = jnp.exp(s - top).astype(BF16)
            o = mm(e, vaug_ref[head], NN)
            t = head // 2
            total = o[:, (1 - t) * 128 : (2 - t) * 128]
            part = o[:, t * 128 : (t + 1) * 128] / total
            halves[t] = part if halves[t] is None else halves[t] + part
            stats = jnp.where(stat_lane == head, top + jnp.log(total), stats)
        ctx_ref[rows, 0:128] = halves[0].astype(BF16)
        ctx_ref[rows, 128:256] = halves[1].astype(BF16)
        lse_ref[:, rows] = jnp.transpose(stats)[0:8]
        return carry

    lax.fori_loop(0, length // TILE, block, 0)


def attention_forward(h, wq, wk, wv, bq, bv, segc, segr):
    length, width = h.shape
    groups = width // GROUP
    column = pl.BlockSpec((width, GROUP), lambda g: (0, g))
    bias = pl.BlockSpec((1, GROUP), lambda g: (0, g))
    rows = pl.BlockSpec((length, GROUP), lambda g: (0, g))
    wide = jax.ShapeDtypeStruct((length, width), BF16)
    return pl.pallas_call(
        attention_forward_kernel,
        grid=(groups,),
        out_shape=(wide, wide, wide, wide, jax.ShapeDtypeStruct((8 * groups, length), F32)),
        in_specs=[
            fixed((length, width)),
            column,
            column,
            column,
            bias,
            bias,
            fixed((length, 1)),
            fixed((1, length)),
        ],
        out_specs=(rows, rows, rows, rows, pl.BlockSpec((8, length), lambda g: (g, 0))),
        scratch_shapes=[
            pltpu.VMEM((length, length), F32),
            pltpu.VMEM((PER_GROUP, length, GROUP), BF16),
        ],
        compiler_params=params(1),
        cost_estimate=cost(20e9, 12e6),
        name="attention_forward",
    )(h, wq, wk, wv, bq, bv, segc, segr)


def gelu_pair(u):
    z = jnp.abs(u) * 0.7071067811865476
    t = 1.0 / (1.0 + 0.3275911 * z)
    bell = jnp.exp(-z * z)
    poly = t * (
        0.127414796 + t * (-0.142248368 + t * (0.7107068705 + t * (-0.7265760135 + t * 0.5307027145)))
    )
    tail = poly * bell
    phi = jnp.where(u < 0, tail, 1.0 - tail)
    return (u * phi, phi + u * bell * 0.3989422804014327)


def normed(x):
    centre = x - jnp.mean(x, axis=1, keepdims=True)
    scale = lax.rsqrt(jnp.mean(centre * centre, axis=1, keepdims=True) + EPSILON)
    return (centre * scale, scale)


def norm_back(u, n, scale):
    return scale * (u - jnp.mean(u, axis=1, keepdims=True) - n * jnp.mean(u * n, axis=1, keepdims=True))


def row_sum(x):
    return jnp.sum(x, axis=0, keepdims=True)


def token_kernel(
    h_ref,
    ctx_ref,
    cot_ref,
    wo_ref,
    wi_ref,
    wp_ref,
    bi_ref,
    vec_ref,
    out_ref,
    first_ref,
    act_ref,
    og_ref,
    ig_ref,
    fp_ref,
    ag_ref,
    dctx_ref,
    sums_ref,
    isum_ref,
    slope_ref,
):
    @pl.when(pl.program_id(0) == 0)
    def _():
        sums_ref[...] = jnp.zeros_like(sums_ref)
        isum_ref[...] = jnp.zeros_like(isum_ref)

    ff = wi_ref.shape[1]
    chunk = 512
    output_bias, gain1, shift1 = vec_ref[0:1, :], vec_ref[1:2, :], vec_ref[2:3, :]
    outer_bias, gain2, shift2 = vec_ref[3:4, :], vec_ref[4:5, :], vec_ref[5:6, :]
    n1, r1 = normed(h_ref[...].astype(F32) + mm(ctx_ref[...], wo_ref[...], NN) + output_bias)
    fn = n1 * gain1 + shift1
    first = fn.astype(BF16)
    first_ref[...] = first
    for c in range(0, ff, chunk):
        act, slope = gelu_pair(mm(first, wi_ref[:, c : c + chunk], NN) + bi_ref[:, c : c + chunk])
        act_ref[:, c : c + chunk] = act.astype(BF16)
        slope_ref[:, c : c + chunk] = slope
    n2, r2 = normed(fn + mm(act_ref[...], wp_ref[...], NN) + outer_bias)
    out_ref[...] = (n2 * gain2 + shift2).astype(BF16)
    e = cot_ref[...].astype(F32)
    sums_ref[0:1, :] += row_sum(e * n2)
    sums_ref[1:2, :] += row_sum(e)
    sp = norm_back(e * gain2, n2, r2)
    og = sp.astype(BF16)
    og_ref[...] = og
    sums_ref[2:3, :] += row_sum(og.astype(F32))
    for c in range(0, ff, chunk):
        ig = (mm(og, wp_ref[c : c + chunk, :], NT) * slope_ref[:, c : c + chunk]).astype(BF16)
        ig_ref[:, c : c + chunk] = ig
        isum_ref[:, c : c + chunk] += row_sum(ig.astype(F32))
    d = sp + mm(ig_ref[...], wi_ref[...], NT)
    sums_ref[3:4, :] += row_sum(d * n1)
    sums_ref[4:5, :] += row_sum(d)
    fp = norm_back(d * gain1, n1, r1)
    fp_ref[...] = fp
    ag = fp.astype(BF16)
    ag_ref[...] = ag
    sums_ref[5:6, :] += row_sum(ag.astype(F32))
    dctx_ref[...] = mm(ag, wo_ref[...], NT).astype(BF16)


def token_pass(h, ctx, cot, wo, wi, wp, bi, vec):
    length, width = h.shape
    ff = wi.shape[1]
    rows = pl.BlockSpec((TILE, width), lambda i: (i, 0))
    wide_rows = pl.BlockSpec((TILE, ff), lambda i: (i, 0))
    low = jax.ShapeDtypeStruct((length, width), BF16)
    low_ff = jax.ShapeDtypeStruct((length, ff), BF16)
    return pl.pallas_call(
        token_kernel,
        grid=(length // TILE,),
        out_shape=(
            low,
            low,
            low_ff,
            low,
            low_ff,
            jax.ShapeDtypeStruct((length, width), F32),
            low,
            low,
            jax.ShapeDtypeStruct((8, width), F32),
            jax.ShapeDtypeStruct((1, ff), F32),
        ),
        in_specs=[
            rows,
            rows,
            rows,
            fixed((width, width)),
            fixed((width, ff)),
            fixed((ff, width)),
            fixed((1, ff)),
            fixed((8, width)),
        ],
        out_specs=(
            rows,
            rows,
            wide_rows,
            rows,
            wide_rows,
            rows,
            rows,
            rows,
            pl.BlockSpec((8, width), lambda i: (0, 0)),
            pl.BlockSpec((1, ff), lambda i: (0, 0)),
        ),
        scratch_shapes=[pltpu.VMEM((TILE, ff), F32)],
        compiler_params=params(1),
        cost_estimate=cost(21.7e9, 30e6),
        name="token_pass",
    )(h, ctx, cot, wo, wi, wp, bi, vec)


def put_pairs(res, core_ref, keep_ref, send_ref, place):
    even = core_ref[0] == 0
    for at, (low_part, high_part) in place:
        zero, one = res[low_part], res[high_part]
        keep_ref[at] = jnp.where(even, zero, one)
        send_ref[at] = jnp.where(even, one, zero).astype(BF16)


def blocks_of(rows, y_first):
    columns = [slice(0, 384), slice(384, 768)]
    places = []
    for z in range(4):
        for y in range(2):
            for x in range(2):
                base = (z * 2 + y) * 2 * rows
                lead = (y, x) if y_first else (x, y)
                places.append(
                    (
                        lead + (z, 0),
                        (
                            (slice(base, base + rows), columns[x]),
                            (slice(base + rows, base + 2 * rows), columns[x]),
                        ),
                    )
                )
    return places


def outer_grad_kernel(core_ref, act_ref, og_ref, keep_ref, send_ref):
    res = mm(act_ref[...], og_ref[...], TN)
    rows = keep_ref.shape[3]
    places = [(at[:2] + (0,), pair) for at, pair in blocks_of(rows, False)[:4]]
    put_pairs(res, core_ref, keep_ref, send_ref, places)


SCALAR = pl.BlockSpec(memory_space=pltpu.SMEM)


def outer_grad_call(core, act, og):
    length, ff = act.shape
    width = og.shape[1]
    shape = (2, 2, 4, ff // 16, width // 2)
    spec = pl.BlockSpec((2, 2, 1) + shape[3:], lambda z: (0, 0, z, 0, 0))
    return pl.pallas_call(
        outer_grad_kernel,
        grid=(4,),
        out_shape=(jax.ShapeDtypeStruct(shape, F32), jax.ShapeDtypeStruct(shape, BF16)),
        in_specs=[
            SCALAR,
            pl.BlockSpec((length, ff // 4), lambda z: (0, z)),
            fixed((length, width)),
        ],
        out_specs=(spec, spec),
        compiler_params=params(1),
        cost_estimate=cost(8e9, 16e6),
        name="outer_grad",
    )(core, act, og)


def inner_grad_kernel(core_ref, first_ref, low_ref, high_ref, ctx_ref, ag_ref, keep_ref, send_ref):
    step = pl.program_id(0)
    places = blocks_of(keep_ref.shape[4], True)

    @pl.when(step < 4)
    def _():
        both = jnp.concatenate([low_ref[...], high_ref[...]], axis=1)
        put_pairs(mm(first_ref[...], both, TN), core_ref, keep_ref, send_ref, places)

    @pl.when(step == 4)
    def _():
        put_pairs(mm(ctx_ref[...], ag_ref[...], TN), core_ref, keep_ref, send_ref, places)


def inner_grad_call(core, first, ig, ctx, ag):
    length, width = first.shape
    shape = (2, 2, 4, 5, width // 16, width // 2)
    spec = pl.BlockSpec((2, 2, 4, 1) + shape[4:], lambda s: (0, 0, 0, s, 0, 0))
    return pl.pallas_call(
        inner_grad_kernel,
        grid=(5,),
        out_shape=(jax.ShapeDtypeStruct(shape, F32), jax.ShapeDtypeStruct(shape, BF16)),
        in_specs=[
            SCALAR,
            fixed((length, width)),
            pl.BlockSpec((length, width // 2), lambda s: (0, jnp.minimum(s, 3))),
            pl.BlockSpec((length, width // 2), lambda s: (0, 4 + jnp.minimum(s, 3))),
            fixed((length, width)),
            fixed((length, width)),
        ],
        out_specs=(spec, spec),
        compiler_params=params(1),
        cost_estimate=cost(9e9, 20e6),
        name="inner_grad",
    )(core, first, ig, ig, ctx, ag)


def projection_grad_kernel(core_ref, h_ref, d_ref, keep_ref, send_ref):
    res = mm(h_ref[...], d_ref[0], TN)
    put_pairs(res, core_ref, keep_ref, send_ref, blocks_of(keep_ref.shape[4], True))


def projection_grad_call(core, h, dqkv):
    length, width = h.shape
    shape = (2, 2, 4, 3, width // 16, width // 2)
    spec = pl.BlockSpec((2, 2, 4, 1) + shape[4:], lambda s: (0, 0, 0, s, 0, 0))
    return pl.pallas_call(
        projection_grad_kernel,
        grid=(3,),
        out_shape=(jax.ShapeDtypeStruct(shape, F32), jax.ShapeDtypeStruct(shape, BF16)),
        in_specs=[
            SCALAR,
            fixed((length, width)),
            pl.BlockSpec((1, length, width), lambda s: (s, 0, 0)),
        ],
        out_specs=(spec, spec),
        compiler_params=params(1),
        cost_estimate=cost(6e9, 14e6),
        name="projection_grad",
    )(core, h, dqkv)


def attention_backward_kernel(
    q_ref,
    k_ref,
    v_ref,
    dctx_ref,
    ctx_ref,
    lse_ref,
    segc_ref,
    segr_ref,
    *rest_refs,
):
    grads_ref, sums_ref, delta_ref, total_ref, ds_ref, km_ref = rest_refs[-6:]
    length = q_ref.shape[0]

    prod = dctx_ref[...].astype(F32) * ctx_ref[...].astype(F32)
    high = prod.astype(BF16)
    rest = (prod - high.astype(F32)).astype(BF16)
    lane = lax.broadcasted_iota(jnp.int32, (8, GROUP), 1)
    head_of = lax.broadcasted_iota(jnp.int32, (8, GROUP), 0)
    chooser = jnp.where(lane // HEAD == head_of, 1.0, 0.0).astype(BF16)
    delta_ref[...] = mm(chooser, high, NT) + mm(chooser, rest, NT)
    total_ref[...] = jnp.zeros_like(total_ref)

    def block(j, carry):
        rows = pl.ds(pl.multiple_of(j * TILE, TILE), TILE)
        kb = k_ref[rows, :]
        vb = v_ref[rows, :]
        mask = jnp.where(segc_ref[rows, :] == segr_ref[...], 0.0, NEGATIVE)
        dk = jnp.zeros((TILE, GROUP), F32)
        dv = jnp.zeros((TILE, GROUP), F32)
        for head in range(PER_GROUP):
            mine = head_lanes((TILE, GROUP), head)
            km = jnp.where(mine, kb, BF16(0)) * BF16(HEAD**-0.5)
            vm = jnp.where(mine, vb, BF16(0))
            s = mm(km, q_ref[...], NT) + mask
            p = jnp.exp(s - lse_ref[head : head + 1, :])
            dp = mm(vm, dctx_ref[...], NT)
            ds = (p * (dp - delta_ref[head : head + 1, :])).astype(BF16)
            dv = jnp.where(mine, mm(p.astype(BF16), dctx_ref[...], NN), dv)
            dk = jnp.where(mine, mm(ds, q_ref[...], NN), dk)
            ds_ref[head * TILE : (head + 1) * TILE, :] = ds
            km_ref[head * TILE : (head + 1) * TILE, :] = km
        dkb = (dk * HEAD**-0.5).astype(BF16)
        dvb = dv.astype(BF16)
        grads_ref[1, rows, :] = dkb
        grads_ref[2, rows, :] = dvb
        total_ref[...] += mm(ds_ref[...], km_ref[...], TN)
        return carry + row_sum(dvb.astype(F32))

    dv_sum = lax.fori_loop(0, length // TILE, block, jnp.zeros((1, GROUP), F32))
    dq = total_ref[...].astype(BF16)
    grads_ref[0] = dq
    sums_ref[...] = jnp.zeros_like(sums_ref)
    sums_ref[0:1, :] = row_sum(dq.astype(F32))
    sums_ref[1:2, :] = dv_sum


ANY = pl.BlockSpec(memory_space=pl.ANY)


def attention_backward(g, q, k, v, dctx, ctx, lse, segc, segr, held, after):
    length, width = q.shape
    rows = pl.BlockSpec((length, GROUP), lambda i: (0, g))
    grads = jax.ShapeDtypeStruct((3, length, width), BF16)
    sums = jax.ShapeDtypeStruct((8, width), F32)
    return pl.pallas_call(
        attention_backward_kernel,
        grid=(1,),
        out_shape=(grads, sums),
        in_specs=[
            rows,
            rows,
            rows,
            rows,
            rows,
            pl.BlockSpec((8, length), lambda i: (g, 0)),
            fixed((length, 1)),
            fixed((1, length)),
        ]
        + [ANY] * (len(held) + len(after)),
        out_specs=(
            pl.BlockSpec((3, length, GROUP), lambda i: (0, 0, g)),
            pl.BlockSpec((8, GROUP), lambda i: (0, g)),
        ),
        scratch_shapes=[
            pltpu.VMEM((8, length), F32),
            pltpu.VMEM((length, GROUP), F32),
            pltpu.VMEM((PER_GROUP * TILE, length), BF16),
            pltpu.VMEM((PER_GROUP * TILE, GROUP), BF16),
        ],
        input_output_aliases={8 + i: i for i in range(len(held))},
        compiler_params=params(1),
        cost_estimate=cost(12e9, 6e6),
        name="attention_backward",
    )(q, k, v, dctx, ctx, lse, segc, segr, *held, *after)


def hidden_grad_kernel(fp_ref, d_ref, wq_ref, wk_ref, wv_ref, out_ref):
    total = fp_ref[...] + mm(d_ref[0], wq_ref[...], NT)
    total = total + mm(d_ref[1], wk_ref[...], NT)
    out_ref[...] = (total + mm(d_ref[2], wv_ref[...], NT)).astype(out_ref.dtype)


def hidden_grad_part(fp, dqkv, wq, wk, wv, part, kind):
    length, width = fp.shape
    half = length // 2
    steps = half // TILE
    rows = pl.BlockSpec((TILE, width), lambda i: (i + part * steps, 0))
    return pl.pallas_call(
        hidden_grad_kernel,
        grid=(steps,),
        out_shape=jax.ShapeDtypeStruct((half, width), kind),
        in_specs=[rows, pl.BlockSpec((3, TILE, width), lambda i: (0, i + part * steps, 0))]
        + [fixed((width, width))] * 3,
        out_specs=pl.BlockSpec((TILE, width), lambda i: (i, 0)),
        compiler_params=params(1),
        cost_estimate=cost(6 * half * width * width, 8e6),
        name="hidden_grad",
    )(fp, dqkv, wq, wk, wv)


def fast(
    hidden,
    segments,
    query_matrix,
    query_bias,
    key_matrix,
    value_matrix,
    value_bias,
    output_matrix,
    output_bias,
    first_gain,
    first_shift,
    inner_matrix,
    inner_bias,
    outer_matrix,
    outer_bias,
    second_gain,
    second_shift,
    cotangent,
):
    here = lax.axis_index("blk")
    swap = [(0, 1), (1, 0)]

    def own(x):
        return lax.dynamic_index_in_dim(x, here, 0, keepdims=False)

    def other(x):
        return lax.dynamic_index_in_dim(x, 1 - here, 0, keepdims=False)

    def trade(x):
        return lax.ppermute(x, "blk", swap)

    def whole(x):
        return jnp.concatenate([own(x), trade(other(x))], axis=0)

    def back(mine, received):
        first = jnp.where(here == 0, mine, received)
        second = jnp.where(here == 0, received, mine)
        return jnp.stack([first, second], axis=0)

    def row(x):
        return x.astype(F32)[None, :]

    h = whole(hidden)
    seg = whole(segments)
    cot = whole(cotangent)
    length, width = h.shape
    half = length // 2
    segc, segr = seg[:, None], seg[None, :]
    q, k, v, ctx, lse = attention_forward(
        h, query_matrix, key_matrix, value_matrix, row(query_bias), row(value_bias), segc, segr
    )
    empty = jnp.zeros((1, width), F32)
    vec = jnp.concatenate(
        [
            row(output_bias),
            row(first_gain),
            row(first_shift),
            row(outer_bias),
            row(second_gain),
            row(second_shift),
            empty,
            empty,
        ],
        axis=0,
    )
    out, first, act, og, ig, fp, ag, dctx, sums, isum = token_pass(
        h, ctx, cot, output_matrix, inner_matrix, outer_matrix, row(inner_bias), vec
    )
    layer_out = back(out[:half], trade(out[half:]))
    place = lax.axis_index("seq")
    core, y_at, z_at = place % 2, (place // 2) % 2, place // 4
    core_id = core.astype(jnp.int32)[None]

    def seq_swap(x, bit):
        return lax.ppermute(x, "seq", [(i, i ^ bit) for i in range(16)])

    def pick(x, at):
        return lax.dynamic_index_in_dim(x, at, 0, keepdims=False)

    def exchange(keep, came, at, send):
        away = (pick(keep, 1 - at) + pick(came, 1 - at).astype(F32)).astype(BF16)
        mine = pick(keep, at) + pick(came, at).astype(F32)
        return (mine, send(away), away)

    def exchange_x(keep, came):
        return exchange(keep, came, here, trade)

    def exchange_y(keep, came):
        return exchange(keep, came, y_at, lambda x: seq_swap(x, 2))

    def exchange_z(keep, came):
        total = keep + came.astype(F32)
        low = total.astype(BF16)
        parts = [seq_swap(pick(low, z_at ^ d), 4 * d) for d in (1, 2, 3)]
        return (pick(total, z_at), parts, low)

    def finish(state):
        mine, parts, _ = state
        return mine + (parts[0].astype(F32) + parts[1].astype(F32) + parts[2].astype(F32))

    outer_keep, outer_send = outer_grad_call(core_id, act, og)
    outer_came = seq_swap(outer_send, 1)
    inner_keep, inner_send = inner_grad_call(core_id, first, ig, ctx, ag)
    inner_came = seq_swap(inner_send, 1)
    state_a = exchange_x(outer_keep, outer_came)
    bwd = (q, k, v, dctx, ctx, lse, segc, segr)
    dqkv, sums2 = attention_backward(0, *bwd, (), (state_a[2], inner_send))
    state_b = exchange_y(inner_keep, inner_came)
    dqkv, sums2 = attention_backward(1, *bwd, (dqkv, sums2), (state_b[2],))
    state_a = exchange_y(*state_a[:2])
    state_b = exchange_x(*state_b[:2])
    dqkv, sums2 = attention_backward(2, *bwd, (dqkv, sums2), (state_a[2], state_b[2]))
    late_keep, late_send = projection_grad_call(core_id, h, dqkv)
    late_came = seq_swap(late_send, 1)
    state_a = exchange_z(*state_a[:2])
    state_b = exchange_z(*state_b[:2])
    args = (fp, dqkv, query_matrix, key_matrix, value_matrix)
    away = hidden_grad_part(*args, 1, BF16)
    came = trade(away)
    state_c = exchange_y(late_keep, late_came)
    home = hidden_grad_part(*args, 0, F32)
    state_c = exchange_x(*state_c[:2])
    state_c = exchange_z(*state_c[:2])
    hidden_grad = back(home, came.astype(F32))
    outer_grad = finish(state_a)
    inner_all = finish(state_b)
    late_all = finish(state_c)
    output_grad = inner_all[4]
    inner_grad = jnp.transpose(inner_all[:4], (1, 0, 2)).reshape(width // 16, -1)

    vectors = jnp.concatenate([sums[:6], isum.reshape(-1, width), sums2[:2]], axis=0)
    vectors = vectors + seq_swap(vectors, 1)
    vectors = vectors + seq_swap(vectors, 2)
    vectors = vectors + trade(vectors)
    near, far, across = (seq_swap(vectors, 4 * d) for d in (1, 2, 3))
    vectors = (vectors + near) + (far + across)
    return (
        layer_out,
        hidden_grad,
        late_all[0],
        vectors[10],
        late_all[1],
        late_all[2],
        vectors[11],
        output_grad,
        vectors[5],
        vectors[3],
        vectors[4],
        inner_grad,
        vectors[6:10].reshape(-1),
        outer_grad,
        vectors[2],
        vectors[0],
        vectors[1],
    )


def choose(sizes, *args):
    seq_count, row_count, width = args[0].shape
    whole_here = sizes[1] == 2 and seq_count == 2 and row_count % TILE == 0 and width % GROUP == 0
    return fast(*args) if whole_here and sizes[0] == 16 else general(*args)


def solution(mesh):
    sizes = (mesh.shape["seq"], mesh.shape["blk"])
    return jax.shard_map(
        functools.partial(choose, sizes),
        mesh=mesh,
        in_specs=(
            P("seq", "blk", None),
            P("seq", "blk"),
            P(),
            P(),
            P(),
            P(),
            P(),
            P(),
            P(),
            P(),
            P(),
            P(),
            P(),
            P(),
            P(),
            P(),
            P(),
            P("seq", "blk", None),
        ),
        out_specs=(
            P("seq", "blk", None),
            P("seq", "blk", None),
            P("seq", "blk"),
            P(),
            P("seq", "blk"),
            P("seq", "blk"),
            P(),
            P("seq", "blk"),
            P(),
            P(),
            P(),
            P("seq", "blk"),
            P(),
            P("seq", "blk"),
            P(),
            P(),
            P(),
        ),
        check_vma=False,
    )
```

```python
import functools
import math

import jax
import jax.numpy as jnp
from jax import lax
from jax.experimental import pallas as pl
from jax.experimental.pallas import tpu as pltpu
from jax.sharding import PartitionSpec as P

HEADS = 12
HEAD = 64


NEGATIVE = -1e30
EPSILON = 1e-12


def layer_norm(values, norm_gain, norm_shift):
    centre = values - jnp.mean(values, axis=-1, keepdims=True)
    spread = jnp.mean(centre * centre, axis=-1, keepdims=True)
    return centre * lax.rsqrt(spread + EPSILON) * norm_gain + norm_shift


def gelu_exact(values):
    return jax.nn.gelu(values, approximate=False)


def linear(operand, matrix):
    return jnp.dot(operand, matrix, preferred_element_type=jnp.float32)


def split_heads(values):
    return values.reshape(values.shape[0], values.shape[1], HEADS, HEAD)


def block_scores(query_block, key_block, score_scale):
    return (
        jnp.einsum("sqhd,skhd->shqk", query_block, key_block, preferred_element_type=jnp.float32)
        * score_scale
    )


def attention_grads(
    query_block, key_block, value_block, dctx_block, same_doc, log_total, row_delta, score_scale
):
    attn_probs = jnp.where(
        same_doc,
        jnp.exp(block_scores(query_block, key_block, score_scale) - log_total[..., None]),
        0.0,
    )
    slopes = jnp.einsum(
        "sqhd,skhd->shqk", dctx_block, value_block, preferred_element_type=jnp.float32
    )
    return (attn_probs, (attn_probs * (slopes - row_delta[..., None])).astype(jnp.bfloat16))


def over_blocks(length, step, initial):
    block_size = math.gcd(length, 512)

    def scan_step(carried, block_index):
        return (step(carried, block_index * block_size, block_size), None)

    result, unused = lax.scan(scan_step, initial, jnp.arange(length // block_size, dtype=jnp.int32))
    return result


def general(
    hidden,
    segments,
    query_matrix,
    query_bias,
    key_matrix,
    value_matrix,
    value_bias,
    output_matrix,
    output_bias,
    first_gain,
    first_shift,
    inner_matrix,
    inner_bias,
    outer_matrix,
    outer_bias,
    second_gain,
    second_shift,
    cotangent,
):
    seq_count, row_count, model_width = hidden.shape
    score_scale = HEAD ** (-0.5)
    single_float = jnp.float32
    bf16 = jnp.bfloat16
    queries = (linear(hidden, query_matrix) + query_bias.astype(single_float)).astype(bf16)
    key_proj = linear(hidden, key_matrix).astype(bf16)
    value_proj = (linear(hidden, value_matrix) + value_bias.astype(single_float)).astype(bf16)
    seg_all = lax.all_gather(segments, "blk", axis=1, tiled=True)
    keys_all, values_all = (
        lax.all_gather(key_proj, "blk", axis=1, tiled=True),
        lax.all_gather(value_proj, "blk", axis=1, tiled=True),
    )
    length = seg_all.shape[1]
    query_heads = split_heads(queries)
    key_heads = split_heads(keys_all)
    value_heads = split_heads(values_all)

    def key_slices(offset, block_size):
        key_segs = lax.dynamic_slice_in_dim(seg_all, offset, block_size, 1)
        same_doc = (segments[:, :, None] == key_segs[:, None, :])[:, None]
        key_block = lax.dynamic_slice_in_dim(key_heads, offset, block_size, 1)
        value_block = lax.dynamic_slice_in_dim(value_heads, offset, block_size, 1)
        return (same_doc, key_block, value_block)

    def stats_step(carried, offset, block_size):
        same_doc, key_block, value_block = key_slices(offset, block_size)
        running_max, running_sum = carried
        scores = jnp.where(same_doc, block_scores(query_heads, key_block, score_scale), NEGATIVE)
        higher = jnp.maximum(running_max, jnp.max(scores, axis=-1))
        weights = jnp.where(same_doc, jnp.exp(scores - higher[..., None]), 0.0)
        return (higher, running_sum * jnp.exp(running_max - higher) + jnp.sum(weights, axis=-1))

    stat_shape = (seq_count, HEADS, row_count)
    running_max, running_sum = over_blocks(
        length,
        stats_step,
        (jnp.full(stat_shape, NEGATIVE, single_float), jnp.zeros(stat_shape, single_float)),
    )
    log_total = running_max + jnp.log(running_sum)

    def context_step(carried, offset, block_size):
        same_doc, key_block, value_block = key_slices(offset, block_size)
        attn_probs = jnp.where(
            same_doc,
            jnp.exp(block_scores(query_heads, key_block, score_scale) - log_total[..., None]),
            0.0,
        )
        return carried + jnp.einsum(
            "shqk,skhd->sqhd",
            attn_probs.astype(bf16),
            value_block,
            preferred_element_type=single_float,
        )

    head_zeros = jnp.zeros((seq_count, row_count, HEADS, HEAD), single_float)
    context = over_blocks(length, context_step, head_zeros)
    context_reduced = context.reshape(seq_count, row_count, model_width).astype(bf16)
    attn_out = linear(context_reduced, output_matrix) + output_bias.astype(single_float)
    first_pre = hidden.astype(single_float) + attn_out
    first_norm, first_back = jax.vjp(
        layer_norm, first_pre, first_gain.astype(single_float), first_shift.astype(single_float)
    )
    first_reduced = first_norm.astype(bf16)
    inner = linear(first_reduced, inner_matrix) + inner_bias.astype(single_float)
    act_full, gelu_back = jax.vjp(gelu_exact, inner)
    activation_reduced = act_full.astype(bf16)
    outer = linear(activation_reduced, outer_matrix) + outer_bias.astype(single_float)
    layer_full, second_back = jax.vjp(
        layer_norm,
        first_norm + outer,
        second_gain.astype(single_float),
        second_shift.astype(single_float),
    )
    layer_out = layer_full.astype(bf16)
    second_pre_grad, second_gain_grad, second_shift_grad = second_back(
        cotangent.astype(single_float)
    )
    outer_gradient_reduced = second_pre_grad.astype(bf16)
    outer_weight_grad = jnp.einsum(
        "gvx,gvm->xm",
        activation_reduced,
        outer_gradient_reduced,
        preferred_element_type=single_float,
    )
    outer_bias_grad = jnp.sum(outer_gradient_reduced.astype(single_float), axis=(0, 1))
    activation_gradient = jnp.einsum(
        "rzo,uo->rzu", outer_gradient_reduced, outer_matrix, preferred_element_type=single_float
    )
    inner_gradient_reduced = gelu_back(activation_gradient)[0].astype(bf16)
    inner_weight_grad = jnp.einsum(
        "ret,reu->tu", first_reduced, inner_gradient_reduced, preferred_element_type=single_float
    )
    inner_bias_grad = jnp.sum(inner_gradient_reduced.astype(single_float), axis=(0, 1))
    first_norm_grad = second_pre_grad + jnp.einsum(
        "aoi,ni->aon", inner_gradient_reduced, inner_matrix, preferred_element_type=single_float
    )
    first_pre_grad, first_gain_grad, first_shift_grad = first_back(first_norm_grad)
    attention_gradient_reduced = first_pre_grad.astype(bf16)
    output_weight_grad = jnp.einsum(
        "tfm,tfc->mc",
        context_reduced,
        attention_gradient_reduced,
        preferred_element_type=single_float,
    )
    output_bias_grad = jnp.sum(attention_gradient_reduced.astype(single_float), axis=(0, 1))
    dctx_low = jnp.einsum(
        "upx,cx->upc",
        attention_gradient_reduced,
        output_matrix,
        preferred_element_type=single_float,
    ).astype(bf16)
    dctx_heads = split_heads(dctx_low)
    row_delta = jnp.transpose(
        jnp.sum(dctx_heads.astype(single_float) * context, axis=-1), (0, 2, 1)
    )

    def query_step(carried, offset, block_size):
        same_doc, key_block, value_block = key_slices(offset, block_size)
        attn_probs, dscores = attention_grads(
            query_heads,
            key_block,
            value_block,
            dctx_heads,
            same_doc,
            log_total,
            row_delta,
            score_scale,
        )
        return carried + score_scale * jnp.einsum(
            "shqk,skhd->sqhd", dscores, key_block, preferred_element_type=single_float
        )

    query_grad = over_blocks(length, query_step, head_zeros)
    query_all, dctx_all = (
        lax.all_gather(queries, "blk", axis=1, tiled=True),
        lax.all_gather(dctx_low, "blk", axis=1, tiled=True),
    )
    lse_all, delta_all = (
        lax.all_gather(log_total, "blk", axis=2, tiled=True),
        lax.all_gather(row_delta, "blk", axis=2, tiled=True),
    )
    query_all_heads = split_heads(query_all)
    dctx_all_heads = split_heads(dctx_all)
    own_keys = split_heads(key_proj)
    own_values = split_heads(value_proj)

    def key_step(carried, offset, block_size):
        query_segs = lax.dynamic_slice_in_dim(seg_all, offset, block_size, 1)
        same_doc = (query_segs[:, :, None] == segments[:, None, :])[:, None]
        query_block = lax.dynamic_slice_in_dim(query_all_heads, offset, block_size, 1)
        dctx_block = lax.dynamic_slice_in_dim(dctx_all_heads, offset, block_size, 1)
        lse_block = lax.dynamic_slice_in_dim(lse_all, offset, block_size, 2)
        delta_block = lax.dynamic_slice_in_dim(delta_all, offset, block_size, 2)
        key_sum, value_sum = carried
        attn_probs, dscores = attention_grads(
            query_block,
            own_keys,
            own_values,
            dctx_block,
            same_doc,
            lse_block,
            delta_block,
            score_scale,
        )
        key_sum = key_sum + score_scale * jnp.einsum(
            "shqk,sqhd->skhd", dscores, query_block, preferred_element_type=single_float
        )
        value_sum = value_sum + jnp.einsum(
            "shqk,sqhd->skhd",
            attn_probs.astype(bf16),
            dctx_block,
            preferred_element_type=single_float,
        )
        return (key_sum, value_sum)

    key_grad, value_grad = over_blocks(length, key_step, (head_zeros, head_zeros))
    query_gradient_reduced = query_grad.reshape(seq_count, row_count, model_width).astype(bf16)
    key_gradient_reduced = key_grad.reshape(seq_count, row_count, model_width).astype(bf16)
    value_gradient_reduced = value_grad.reshape(seq_count, row_count, model_width).astype(bf16)
    query_weight_grad = jnp.einsum(
        "tfm,tfc->mc", hidden, query_gradient_reduced, preferred_element_type=single_float
    )
    query_bias_grad = jnp.sum(query_gradient_reduced.astype(single_float), axis=(0, 1))
    key_matrix_gradient = jnp.einsum(
        "tfm,tfc->mc", hidden, key_gradient_reduced, preferred_element_type=single_float
    )
    value_weight_grad = jnp.einsum(
        "tfm,tfc->mc", hidden, value_gradient_reduced, preferred_element_type=single_float
    )
    value_bias_grad = jnp.sum(value_gradient_reduced.astype(single_float), axis=(0, 1))
    hidden_grad = first_pre_grad + jnp.einsum(
        "upx,cx->upc", query_gradient_reduced, query_matrix, preferred_element_type=single_float
    )
    hidden_grad = hidden_grad + jnp.einsum(
        "upx,cx->upc", key_gradient_reduced, key_matrix, preferred_element_type=single_float
    )
    hidden_grad = hidden_grad + jnp.einsum(
        "upx,cx->upc", value_gradient_reduced, value_matrix, preferred_element_type=single_float
    )
    partial_sums = (
        lax.psum_scatter(query_weight_grad, "seq", scatter_dimension=0, tiled=True),
        lax.psum_scatter(key_matrix_gradient, "seq", scatter_dimension=0, tiled=True),
        lax.psum_scatter(value_weight_grad, "seq", scatter_dimension=0, tiled=True),
        lax.psum_scatter(output_weight_grad, "seq", scatter_dimension=0, tiled=True),
        lax.psum_scatter(inner_weight_grad, "seq", scatter_dimension=0, tiled=True),
        lax.psum_scatter(outer_weight_grad, "seq", scatter_dimension=0, tiled=True),
    )
    matrices = lax.psum_scatter(tuple(partial_sums), "blk", scatter_dimension=1, tiled=True)
    vectors = lax.psum(
        (
            query_bias_grad,
            value_bias_grad,
            output_bias_grad,
            first_gain_grad,
            first_shift_grad,
            inner_bias_grad,
            outer_bias_grad,
            second_gain_grad,
            second_shift_grad,
        ),
        ("seq", "blk"),
    )
    return (
        layer_out,
        hidden_grad,
        matrices[0],
        vectors[0],
        matrices[1],
        matrices[2],
        vectors[1],
        matrices[3],
        vectors[2],
        vectors[3],
        vectors[4],
        matrices[4],
        vectors[5],
        matrices[5],
        vectors[6],
        vectors[7],
        vectors[8],
    )


BF16 = jnp.bfloat16
F32 = jnp.float32
NN = ((1,), (0,))
NT = ((1,), (1,))
TN = ((0,), (0,))
UNIT = 128
GROUP = 256
PER_GROUP = GROUP // HEAD
TILE = 256
TOKENS = 512
VMEM_LIMIT = 60 * 2**20
SCALAR = pl.BlockSpec(memory_space=pltpu.SMEM)
ANY = pl.BlockSpec(memory_space=pl.ANY)


def mm(a, b, dims):
    return lax.dot_general(a, b, (dims, ((), ())), preferred_element_type=F32)


def fixed(shape):
    return pl.BlockSpec(shape, lambda *_: (0,) * len(shape), pipeline_mode=pl.Buffered(1))


def run(
    kernel,
    name,
    grid,
    operands,
    in_specs,
    out_shape,
    out_specs,
    scratch=(),
    scalars=0,
    held=None,
    passes=(),
    after=(),
    micros=1,
):
    held = held or {}
    out_shape, out_specs = list(out_shape), list(out_specs)
    n_in, n_out, n_held, n_pass = len(operands), len(out_shape), len(held), len(passes)
    aliases = {n_in + i: at for i, at in enumerate(held)}
    aliases |= {n_in + n_held + i: n_out + i for i in range(n_pass)}

    def body(*refs):
        outs = n_in + n_held + n_pass + len(after)
        kernel(*refs[:n_in], *refs[outs : outs + n_out], *refs[outs + n_out + n_pass :])

    result = pl.pallas_call(
        body,
        grid_spec=pltpu.PrefetchScalarGridSpec(
            num_scalar_prefetch=scalars,
            grid=grid,
            in_specs=list(in_specs) + [ANY] * (n_held + n_pass + len(after)),
            out_specs=out_specs + [ANY] * n_pass,
            scratch_shapes=list(scratch),
        ),
        out_shape=out_shape + [jax.ShapeDtypeStruct(x.shape, x.dtype) for x in passes],
        input_output_aliases=aliases,
        compiler_params=pltpu.CompilerParams(
            vmem_limit_bytes=VMEM_LIMIT, dimension_semantics=("arbitrary",) * len(grid)
        ),
        cost_estimate=pl.CostEstimate(
            flops=int(micros * 1e7), bytes_accessed=0, transcendentals=0
        ),
        name=name,
    )(*operands, *held.values(), *passes, *after)
    return result


def head_lanes(shape, head):
    lane = lax.broadcasted_iota(jnp.int32, shape, 1)
    return (lane >= head * HEAD) & (lane < (head + 1) * HEAD)


def lanes(*parts):
    return jnp.concatenate(parts, axis=1)


def column_of(row):
    return jnp.transpose(jnp.broadcast_to(row.astype(F32), (UNIT, row.shape[1])))[:, 0:1]


def same_pair(row, column, rows):
    return jnp.where(column[rows] == row, 0.0, NEGATIVE)


def attention_forward_kernel(
    here_ref,
    own_ref,
    far_ref,
    wq0_ref,
    wq1_ref,
    wk0_ref,
    wk1_ref,
    wv0_ref,
    wv1_ref,
    bq0_ref,
    bq1_ref,
    bv0_ref,
    bv1_ref,
    seg_ref,
    q_ref,
    k_ref,
    v_ref,
    ctx_ref,
    lse_ref,
    h_ref,
    mask_ref,
    vaug_ref,
):
    half = far_ref.shape[0]
    length = 2 * half

    @pl.when(pl.program_id(0) == 0)
    def _():
        segr = seg_ref[...].astype(F32)
        mask_ref[...] = jnp.where(column_of(segr) == segr, 0.0, NEGATIVE)
        h_ref[0:half, :] = own_ref[0]
        h_ref[half:, :] = far_ref[...]

    h = h_ref[...]
    bias_q = lanes(bq0_ref[...], bq1_ref[...])
    bias_v = lanes(bv0_ref[...], bv1_ref[...])
    q_ref[...] = (mm(h, lanes(wq0_ref[...], wq1_ref[...]), NN) + bias_q).astype(BF16)
    k_ref[...] = mm(h, lanes(wk0_ref[...], wk1_ref[...]), NN).astype(BF16)
    v = (mm(h, lanes(wv0_ref[...], wv1_ref[...]), NN) + bias_v).astype(BF16)
    v_ref[...] = v
    lane = lax.broadcasted_iota(jnp.int32, v.shape, 1)
    for head in range(PER_GROUP):
        other = (lane // UNIT) != (head // 2)
        filler = jnp.where(other, 1.0, 0.0).astype(BF16)
        vaug_ref[head] = jnp.where(head_lanes(v.shape, head), v, filler)

    def block(i, carry):
        rows = pl.ds(pl.multiple_of(i * TILE, TILE), TILE)
        qb = q_ref[rows, :] * BF16(HEAD**-0.5)
        halves = [None, None]
        stat_lane = lax.broadcasted_iota(jnp.int32, (TILE, UNIT), 1)
        stats = jnp.zeros((TILE, UNIT), F32)
        for head in range(PER_GROUP):
            qm = jnp.where(head_lanes(qb.shape, head), qb, BF16(0))
            s = mm(qm, k_ref[...], NT) + mask_ref[rows, :]
            top = jnp.max(s, axis=1, keepdims=True)
            e = jnp.exp(s - top).astype(BF16)
            o = mm(e, vaug_ref[head], NN)
            t = head // 2
            total = o[:, (1 - t) * UNIT : (2 - t) * UNIT]
            part = o[:, t * UNIT : (t + 1) * UNIT] / total
            halves[t] = part if halves[t] is None else halves[t] + part
            stats = jnp.where(stat_lane == head, top + jnp.log(total), stats)
        ctx_ref[0, rows, :] = halves[0].astype(BF16)
        ctx_ref[1, rows, :] = halves[1].astype(BF16)
        lse_ref[:, rows] = jnp.transpose(stats)[0:8]
        return carry

    lax.fori_loop(0, length // TILE, block, 0, unroll=True)


def attention_forward(here, hidden, far, wq, wk, wv, bq, bv, seg):
    half, width = far.shape
    length = 2 * half
    groups = width // GROUP
    left = pl.BlockSpec((width, UNIT), lambda g, h: (0, g))
    right = pl.BlockSpec((width, UNIT), lambda g, h: (0, groups + g))
    bias_left = pl.BlockSpec((1, UNIT), lambda g, h: (0, g))
    bias_right = pl.BlockSpec((1, UNIT), lambda g, h: (0, groups + g))
    rows = pl.BlockSpec((length, GROUP), lambda g, h: (0, g))
    wide = jax.ShapeDtypeStruct((length, width), BF16)
    own = pl.BlockSpec((1, half, width), lambda g, h: (h[0], 0, 0), pipeline_mode=pl.Buffered(1))
    return run(
        attention_forward_kernel,
        "attention_forward",
        (groups,),
        (here, hidden, far, wq, wq, wk, wk, wv, wv, bq, bq, bv, bv, seg),
        [own, fixed((half, width))]
        + [left, right] * 3
        + [bias_left, bias_right] * 2
        + [fixed((1, length))],
        (
            wide,
            wide,
            wide,
            jax.ShapeDtypeStruct((2, length, width // 2), BF16),
            jax.ShapeDtypeStruct((8 * groups, length), F32),
            wide,
        ),
        (
            rows,
            rows,
            rows,
            pl.BlockSpec((2, length, UNIT), lambda g, h: (0, 0, g)),
            pl.BlockSpec((8, length), lambda g, h: (g, 0)),
            pl.BlockSpec((length, width), lambda g, h: (0, 0)),
        ),
        [pltpu.VMEM((length, length), F32), pltpu.VMEM((PER_GROUP, length, GROUP), BF16)],
        scalars=1,
        micros=16,
    )


def gelu_pair(u):
    phi = 0.5 + 0.5 * lax.erf(u * 0.7071067811865476)
    bell = jnp.exp2(u * u * -0.7213475204444817)
    return (u * phi, phi + u * bell * 0.3989422804014327)


def normed(x):
    centre = x - jnp.mean(x, axis=1, keepdims=True)
    scale = lax.rsqrt(jnp.mean(centre * centre, axis=1, keepdims=True) + EPSILON)
    return (centre * scale, scale)


def norm_back(u, n, scale):
    return scale * (u - jnp.mean(u, axis=1, keepdims=True) - n * jnp.mean(u * n, axis=1, keepdims=True))


def row_sum(x):
    return jnp.sum(x, axis=0, keepdims=True)


def token_kernel(
    here_ref,
    h_ref,
    ctx_ref,
    cot_own_ref,
    cot_far_ref,
    wo_ref,
    wi_ref,
    wp_ref,
    bi_ref,
    vec_ref,
    out_ref,
    far_ref,
    first_ref,
    act_ref,
    og_ref,
    ig_ref,
    fp_ref,
    ag_ref,
    dctx_ref,
    sums_ref,
    isum_ref,
    slope_ref,
):
    step = pl.program_id(0)
    steps = pl.num_programs(0)

    @pl.when(step == 0)
    def _():
        sums_ref[...] = jnp.zeros_like(sums_ref)
        isum_ref[...] = jnp.zeros_like(isum_ref)

    ff = wi_ref.shape[1]
    chunk = 512
    output_bias, gain1, shift1 = vec_ref[0:1, :], vec_ref[1:2, :], vec_ref[2:3, :]
    outer_bias, gain2, shift2 = vec_ref[3:4, :], vec_ref[4:5, :], vec_ref[5:6, :]
    middle = wo_ref.shape[0] // 2
    near = step < steps // 2

    def part(rows):
        ctx = lanes(ctx_ref[0, rows, :], ctx_ref[1, rows, :])
        x = h_ref[rows, :].astype(F32) + mm(ctx, wo_ref[...], NN) + output_bias
        yield
        n1, r1 = normed(x)
        fn = n1 * gain1 + shift1
        first = fn.astype(BF16)
        first_ref[rows, :] = first
        yield
        for c in range(0, ff, chunk):
            act, slope = gelu_pair(mm(first, wi_ref[:, c : c + chunk], NN) + bi_ref[:, c : c + chunk])
            act_ref[rows, c : c + chunk] = act.astype(BF16)
            slope_ref[rows, c : c + chunk] = slope
            yield
        x = fn + mm(act_ref[rows, :], wp_ref[...], NN) + outer_bias
        yield
        n2, r2 = normed(x)
        out = (n2 * gain2 + shift2).astype(BF16)

        @pl.when(near)
        def _():
            out_ref[0, rows, :] = out

        @pl.when(jnp.logical_not(near))
        def _():
            far_ref[rows, :] = out

        e = jnp.where(near, cot_own_ref[0, rows, :], cot_far_ref[rows, :]).astype(F32)
        sums_ref[0:1, :] += row_sum(e * n2)
        sums_ref[1:2, :] += row_sum(e)
        sp = norm_back(e * gain2, n2, r2)
        og = sp.astype(BF16)
        og_ref[rows, :] = og
        sums_ref[2:3, :] += row_sum(og.astype(F32))
        yield
        for c in range(0, ff, chunk):
            ig = (mm(og, wp_ref[c : c + chunk, :], NT) * slope_ref[rows, c : c + chunk]).astype(BF16)
            ig_ref[rows, c : c + chunk] = ig
            isum_ref[:, c : c + chunk] += row_sum(ig.astype(F32))
            yield
        d = sp + mm(ig_ref[rows, :], wi_ref[...], NT)
        yield
        sums_ref[3:4, :] += row_sum(d * n1)
        sums_ref[4:5, :] += row_sum(d)
        fp = norm_back(d * gain1, n1, r1)
        fp_ref[rows, :] = fp
        ag = fp.astype(BF16)
        ag_ref[rows, :] = ag
        sums_ref[5:6, :] += row_sum(ag.astype(F32))
        yield
        dctx = mm(ag, wo_ref[...], NT).astype(BF16)
        dctx_ref[0, rows, :] = dctx[:, :middle]
        dctx_ref[1, rows, :] = dctx[:, middle:]

    size = h_ref.shape[0]
    parts = [part(slice(r, r + TILE)) for r in range(0, size, TILE)]
    live, waiting = [], list(parts)
    while waiting or live:
        if waiting:
            live.append(waiting.pop(0))
        live = [p for p in live if next(p, 0) is None]


def token_pass(here, h, ctx, cot, cot_far, wo, wi, wp, bi, vec):
    length, width = h.shape
    half = length // 2
    ff = wi.shape[1]
    steps = length // TOKENS
    near = steps // 2
    rows = pl.BlockSpec((TOKENS, width), lambda i, b: (i, 0))
    split_rows = pl.BlockSpec((2, TOKENS, width // 2), lambda i, b: (0, i, 0))
    wide_rows = pl.BlockSpec((TOKENS, ff), lambda i, b: (i, 0))
    own_rows = pl.BlockSpec((1, TOKENS, width), lambda i, b: (b[0], jnp.minimum(i, near - 1), 0))
    far_rows = pl.BlockSpec((TOKENS, width), lambda i, b: (jnp.maximum(i - near, 0), 0))
    low = jax.ShapeDtypeStruct((length, width), BF16)
    low_ff = jax.ShapeDtypeStruct((length, ff), BF16)
    return run(
        token_kernel,
        "token_pass",
        (steps,),
        (here, h, ctx, cot, cot_far, wo, wi, wp, bi, vec),
        [
            rows,
            split_rows,
            own_rows,
            far_rows,
            fixed((width, width)),
            fixed((width, ff)),
            fixed((ff, width)),
            fixed((1, ff)),
            fixed((8, width)),
        ],
        (
            jax.ShapeDtypeStruct((2, half, width), BF16),
            jax.ShapeDtypeStruct((half, width), BF16),
            low,
            low_ff,
            low,
            low_ff,
            jax.ShapeDtypeStruct((length, width), F32),
            low,
            jax.ShapeDtypeStruct((2, length, width // 2), BF16),
            jax.ShapeDtypeStruct((8, width), F32),
            jax.ShapeDtypeStruct((1, ff), F32),
        ),
        (
            own_rows,
            far_rows,
            rows,
            wide_rows,
            rows,
            wide_rows,
            rows,
            rows,
            split_rows,
            pl.BlockSpec((8, width), lambda i, b: (0, 0)),
            pl.BlockSpec((1, ff), lambda i, b: (0, 0)),
        ),
        [pltpu.VMEM((TOKENS, ff), F32)],
        scalars=1,
        micros=23,
    )


def put_pairs(res, core_ref, keep_ref, send_ref, columns, rows, count):
    even = core_ref[0] == 0
    for z in range(count):
        for y in range(2):
            base = (z * 2 + y) * 2 * rows
            for x in range(2):
                zero = lanes(*[res[base : base + rows, c] for c in columns[x]])
                one = lanes(*[res[base + rows : base + 2 * rows, c] for c in columns[x]])
                keep_ref[y, x, z, 0] = jnp.where(even, zero, one).astype(BF16)
                send_ref[y, x, z, 0] = jnp.where(even, one, zero).astype(BF16)


HALVES = ((slice(0, 384),), (slice(384, 768),))
VECTOR_ROWS = 32
BIAS_ROWS = 16


def outer_grad_kernel(core_ref, act_ref, og_ref, sums_ref, isum_ref, keep_ref, send_ref, rows_ref):
    res = mm(act_ref[...], og_ref[...], TN)
    middle = res.shape[1] // 2
    rows = res.shape[0] // 4
    even = core_ref[0] == 0
    rows_ref[...] = jnp.zeros_like(rows_ref)
    at = 0
    for r in range(6):
        for x in range(2):
            rows_ref[at : at + 1, :] = sums_ref[r : r + 1, x * middle : (x + 1) * middle]
            at += 1
    for r in range(isum_ref.shape[1] // middle):
        rows_ref[at : at + 1, :] = isum_ref[:, r * middle : (r + 1) * middle]
        at += 1
    extra = rows_ref[...].astype(BF16)
    for y in range(2):
        for x in range(2):
            columns = slice(x * middle, (x + 1) * middle)
            zero = res[2 * y * rows : (2 * y + 1) * rows, columns]
            one = res[(2 * y + 1) * rows : (2 * y + 2) * rows, columns]
            keep_ref[x, y, 0, 0:rows, :] = jnp.where(even, zero, one).astype(BF16)
            send_ref[x, y, 0, 0:rows, :] = jnp.where(even, one, zero).astype(BF16)
            keep_ref[x, y, 0, rows:, :] = extra
            send_ref[x, y, 0, rows:, :] = extra


def pair_out(shape, block, index):
    kind = jax.ShapeDtypeStruct(shape, BF16)
    spec = pl.BlockSpec(block, index)
    return ((kind, kind), (spec, spec))


def outer_grad_call(core, act, og, sums, isum):
    length, ff = act.shape
    width = og.shape[1]
    shape = (2, 2, 4, ff // 16 + VECTOR_ROWS, width // 2)
    kinds, specs = pair_out(shape, (2, 2, 1) + shape[3:], lambda z: (0, 0, z, 0, 0))
    return run(
        outer_grad_kernel,
        "outer_grad",
        (4,),
        (core, act, og, sums, isum),
        [
            SCALAR,
            pl.BlockSpec((length, ff // 4), lambda z: (0, z)),
            fixed((length, width)),
            fixed(sums.shape),
            fixed(isum.shape),
        ],
        kinds,
        specs,
        [pltpu.VMEM((VECTOR_ROWS, width // 2), F32)],
        micros=4.5,
    )


def inner_grad_kernel(
    core_ref, first_ref, low_ref, high_ref, ctx_ref, ag_ref, keep_ref, send_ref
):
    step = pl.program_id(0)
    rows = keep_ref.shape[4]

    @pl.when(step < 4)
    def _():
        res = mm(first_ref[...], lanes(low_ref[...], high_ref[...]), TN)
        put_pairs(res, core_ref, keep_ref, send_ref, HALVES, rows, 4)

    @pl.when(step == 4)
    def _():
        res = mm(lanes(ctx_ref[0], ctx_ref[1]), ag_ref[...], TN)
        put_pairs(res, core_ref, keep_ref, send_ref, HALVES, rows, 4)


def inner_grad_call(core, first, ig, ctx, ag, passes):
    length, width = first.shape
    shape = (2, 2, 4, 5, width // 16, width // 2)
    kinds, specs = pair_out(shape, shape[:3] + (1,) + shape[4:], lambda s: (0, 0, 0, s, 0, 0))
    return run(
        inner_grad_kernel,
        "inner_grad",
        (5,),
        (core, first, ig, ig, ctx, ag),
        [
            SCALAR,
            fixed((length, width)),
            pl.BlockSpec((length, width // 2), lambda s: (0, jnp.minimum(s, 3))),
            pl.BlockSpec((length, width // 2), lambda s: (0, 4 + jnp.minimum(s, 3))),
            fixed((2, length, width // 2)),
            fixed((length, width)),
        ],
        kinds,
        specs,
        passes=passes,
        micros=6,
    )


def projection_grad_kernel(with_sums, core_ref, h_ref, d_ref, sums_ref, keep_ref, send_ref):
    step = pl.program_id(0)
    res = mm(h_ref[...], d_ref[0], TN)
    rows = res.shape[0] // 16
    units = res.shape[1] // UNIT
    columns = [[slice(u * UNIT, (u + 1) * UNIT) for u in range(x, units, 2)] for x in range(2)]
    even = core_ref[0] == 0
    for s in range(3):

        @pl.when(step == s)
        def _(s=s):
            place = slice(s * rows, (s + 1) * rows)
            for z in range(4):
                for y in range(2):
                    base = (z * 2 + y) * 2 * rows
                    for x in range(2):
                        zero = lanes(*[res[base : base + rows, c] for c in columns[x]])
                        one = lanes(*[res[base + rows : base + 2 * rows, c] for c in columns[x]])
                        keep_ref[y, x, z, place, :] = jnp.where(even, zero, one).astype(BF16)
                        send_ref[y, x, z, place, :] = jnp.where(even, one, zero).astype(BF16)

    @pl.when(step == 0)
    def _():
        extra = jnp.zeros((BIAS_ROWS, keep_ref.shape[4]), F32)
        if with_sums:
            at = lax.broadcasted_iota(jnp.int32, extra.shape, 0)
            count = sums_ref.shape[1] // UNIT
            for r in range(2):
                for u in range(count):
                    part = sums_ref[r : r + 1, u * UNIT : (u + 1) * UNIT]
                    extra = jnp.where(at == r * count + u, part, extra)
        for z in range(4):
            for y in range(2):
                for x in range(2):
                    keep_ref[y, x, z, 3 * rows :, :] = extra.astype(BF16)
                    send_ref[y, x, z, 3 * rows :, :] = extra.astype(BF16)


def projection_grad_call(core, h, dqkv, sums, at, span, with_sums, passes, after):
    length, width = h.shape
    shape = (2, 2, 4, 3 * width // 16 + BIAS_ROWS, span // 2)
    kinds, specs = pair_out(shape, shape, lambda s: (0, 0, 0, 0, 0))
    return run(
        functools.partial(projection_grad_kernel, with_sums),
        "projection_grad",
        (3,),
        (core, h, dqkv, sums),
        [
            SCALAR,
            fixed((length, width)),
            pl.BlockSpec((1, length, span), lambda s: (s, 0, at)),
            fixed(sums.shape),
        ],
        kinds,
        specs,
        passes=passes,
        after=after,
        micros=2.5,
    )


def attention_backward_kernel(
    q_ref,
    k_ref,
    v_ref,
    dctx_pair_ref,
    ctx_pair_ref,
    lse_ref,
    seg_ref,
    grads_ref,
    sums_ref,
    delta_ref,
    total_ref,
    kt_ref,
    dctx_ref,
    segc_ref,
):
    length = q_ref.shape[0]
    dctx_ref[...] = lanes(dctx_pair_ref[0], dctx_pair_ref[1])
    ctx = lanes(ctx_pair_ref[0], ctx_pair_ref[1])
    segr = seg_ref[...].astype(F32)
    segc_ref[...] = column_of(segr)
    prod = dctx_ref[...].astype(F32) * ctx.astype(F32)
    high = prod.astype(BF16)
    rest = (prod - high.astype(F32)).astype(BF16)
    lane = lax.broadcasted_iota(jnp.int32, (8, GROUP), 1)
    head_of = lax.broadcasted_iota(jnp.int32, (8, GROUP), 0)
    chooser = jnp.where(lane // HEAD == head_of, 1.0, 0.0).astype(BF16)
    delta_ref[...] = mm(chooser, high, NT) + mm(chooser, rest, NT)
    total_ref[...] = jnp.zeros_like(total_ref)
    kt_ref[...] = jnp.transpose(k_ref[...])

    def block(j, carry):
        rows = pl.ds(pl.multiple_of(j * TILE, TILE), TILE)
        kb = k_ref[rows, :]
        vb = v_ref[rows, :]
        mask = jnp.where(segc_ref[rows, :] == segr, 0.0, NEGATIVE)
        dk = jnp.zeros((TILE, GROUP), F32)
        dv = jnp.zeros((TILE, GROUP), F32)
        for head in range(PER_GROUP):
            mine = head_lanes((TILE, GROUP), head)
            km = jnp.where(mine, kb, BF16(0)) * BF16(HEAD**-0.5)
            vm = jnp.where(mine, vb, BF16(0))
            s = mm(km, q_ref[...], NT) + mask
            p = jnp.exp(s - lse_ref[head : head + 1, :])
            dp = mm(vm, dctx_ref[...], NT)
            ds = (p * (dp - delta_ref[head : head + 1, :])).astype(BF16)
            dv = jnp.where(mine, mm(p.astype(BF16), dctx_ref[...], NN), dv)
            dk = jnp.where(mine, mm(ds, q_ref[...], NN), dk)
            columns = slice(head * HEAD, (head + 1) * HEAD)
            total_ref[columns, :] += mm(kt_ref[columns, rows], ds, NN)
        dkb = (dk * HEAD**-0.5).astype(BF16)
        dvb = dv.astype(BF16)
        grads_ref[1, rows, :] = dkb
        grads_ref[2, rows, :] = dvb
        return carry + row_sum(dvb.astype(F32))

    dv_sum = lax.fori_loop(0, length // TILE, block, jnp.zeros((1, GROUP), F32), unroll=True)
    dq = jnp.transpose(total_ref[...] * HEAD**-0.5).astype(BF16)
    grads_ref[0] = dq
    sums_ref[...] = jnp.zeros_like(sums_ref)
    sums_ref[0:1, :] = row_sum(dq.astype(F32))
    sums_ref[1:2, :] = dv_sum


def attention_backward(g, q, k, v, dctx, ctx, lse, seg, held, passes, after):
    length, width = q.shape
    rows = pl.BlockSpec((length, GROUP), lambda i: (0, g))
    pair_rows = pl.BlockSpec((2, length, UNIT), lambda i: (0, 0, g))
    return run(
        attention_backward_kernel,
        "attention_backward",
        (1,),
        (q, k, v, dctx, ctx, lse, seg),
        [
            rows,
            rows,
            rows,
            pair_rows,
            pair_rows,
            pl.BlockSpec((8, length), lambda i: (g, 0)),
            fixed((1, length)),
        ],
        (jax.ShapeDtypeStruct((3, length, width), BF16), jax.ShapeDtypeStruct((8, width), F32)),
        (
            pl.BlockSpec((3, length, GROUP), lambda i: (0, 0, g)),
            pl.BlockSpec((8, GROUP), lambda i: (0, g)),
        ),
        [
            pltpu.VMEM((8, length), F32),
            pltpu.VMEM((GROUP, length), F32),
            pltpu.VMEM((GROUP, length), BF16),
            pltpu.VMEM((length, GROUP), BF16),
            pltpu.VMEM((length, 1), F32),
        ],
        held=dict(enumerate(held)),
        passes=passes,
        after=after,
        micros=8,
    )


def hidden_total(fp_ref, d_ref, wq_ref, wk_ref, wv_ref):
    total = fp_ref[...]
    for at, w_ref in enumerate((wq_ref, wk_ref, wv_ref)):
        units = d_ref.shape[2] // UNIT
        order = list(range(0, units, 2)) + list(range(1, units, 2))
        d = lanes(*[d_ref[at, :, u * UNIT : (u + 1) * UNIT] for u in order])
        total = total + mm(d, w_ref[...], NT)
    return total


def hidden_away_kernel(fp_ref, d_ref, wq_ref, wk_ref, wv_ref, out_ref):
    out_ref[...] = hidden_total(fp_ref, d_ref, wq_ref, wk_ref, wv_ref).astype(BF16)


def hidden_home_kernel(
    here_ref, fp_ref, d_ref, wq_ref, wk_ref, wv_ref, came_ref, out_ref, layer_ref
):
    out_ref[0] = hidden_total(fp_ref, d_ref, wq_ref, wk_ref, wv_ref)
    layer_ref[0] = came_ref[...]


def hidden_away(fp, dqkv, wq, wk, wv, passes, after):
    length, width = fp.shape
    half = length // 2
    steps = half // TILE
    return run(
        hidden_away_kernel,
        "hidden_away",
        (steps,),
        (fp, dqkv, wq, wk, wv),
        [
            pl.BlockSpec((TILE, width), lambda i: (i + steps, 0)),
            pl.BlockSpec((3, TILE, width), lambda i: (0, i + steps, 0)),
        ]
        + [fixed((width, width))] * 3,
        (jax.ShapeDtypeStruct((half, width), BF16),),
        (pl.BlockSpec((TILE, width), lambda i: (i, 0)),),
        passes=passes,
        after=after,
        micros=3,
    )


def hidden_home(here, fp, dqkv, wq, wk, wv, came, layer, passes, after):
    length, width = fp.shape
    half = length // 2
    steps = half // TILE
    return run(
        hidden_home_kernel,
        "hidden_home",
        (steps,),
        (here, fp, dqkv, wq, wk, wv, came),
        [
            pl.BlockSpec((TILE, width), lambda i, b: (i, 0)),
            pl.BlockSpec((3, TILE, width), lambda i, b: (0, i, 0)),
        ]
        + [fixed((width, width))] * 3
        + [pl.BlockSpec((TILE, width), lambda i, b: (i, 0))],
        (
            jax.ShapeDtypeStruct((2, half, width), F32),
            jax.ShapeDtypeStruct((2, half, width), BF16),
        ),
        (
            pl.BlockSpec((1, TILE, width), lambda i, b: (b[0], i, 0)),
            pl.BlockSpec((1, TILE, width), lambda i, b: (1 - b[0], i, 0)),
        ),
        scalars=1,
        held={1: layer},
        passes=passes,
        after=after,
        micros=3,
    )


def place_kernel(here_ref, came_ref, out_ref):
    out_ref[0] = came_ref[...].astype(F32)


def place_far(here, came, grad, passes):
    half, width = came.shape
    return run(
        place_kernel,
        "place_far",
        (2,),
        (here, came),
        [pl.BlockSpec((half // 2, width), lambda i, b: (i, 0))],
        (jax.ShapeDtypeStruct((2, half, width), F32),),
        (pl.BlockSpec((1, half // 2, width), lambda i, b: (1 - b[0], i, 0)),),
        scalars=1,
        held={0: grad},
        passes=passes,
        micros=1,
    )


def fast(
    hidden,
    segments,
    query_matrix,
    query_bias,
    key_matrix,
    value_matrix,
    value_bias,
    output_matrix,
    output_bias,
    first_gain,
    first_shift,
    inner_matrix,
    inner_bias,
    outer_matrix,
    outer_bias,
    second_gain,
    second_shift,
    cotangent,
):
    here = lax.axis_index("blk")
    place = lax.axis_index("seq")
    core, y_at, z_at = place % 2, (place // 2) % 2, place // 4
    here_id = here.astype(jnp.int32)[None]
    core_id = core.astype(jnp.int32)[None]
    half, width = hidden.shape[1:]

    def pick(x, *at):
        start = at + (0,) * (x.ndim - len(at))
        size = (1,) * len(at) + x.shape[len(at) :]
        return lax.dynamic_slice(x, start, size).reshape(x.shape[len(at) :])

    def trade(x):
        return lax.ppermute(x, "blk", [(0, 1), (1, 0)])

    def seq_swap(x, bit):
        return lax.ppermute(x, "seq", [(i, i ^ bit) for i in range(16)])

    def row(x):
        return x.astype(F32)[None, :]

    def rounded(x):
        return lax.reduce_precision(x, 8, 7)

    def sum_0(state, *at):
        return rounded(pick(state[0], *at).astype(F32) + pick(state[1], *at).astype(F32))

    def sum_1(state, mine, *at):
        return rounded(sum_0(state, mine, *at) + pick(state[2], *at).astype(F32))

    def sum_2(state, mine, then, *at):
        return rounded(sum_1(state, mine, then, *at) + pick(state[3], *at).astype(F32))

    def send_z(parts):
        return [seq_swap(x, 4 * d) for d, x in zip((1, 2, 3), parts)]

    def add_z(total, parts):
        return (total + parts[0].astype(F32)) + (parts[1].astype(F32) + parts[2].astype(F32))

    seg = jnp.concatenate([pick(segments, here), trade(pick(segments, 1 - here))])[None, :]
    far = trade(pick(hidden, 1 - here))
    cot_far = trade(pick(cotangent, 1 - here + jnp.minimum(seg[0, -1], 0)))
    q, k, v, ctx, lse, h = attention_forward(
        here_id,
        hidden,
        far,
        query_matrix,
        key_matrix,
        value_matrix,
        row(query_bias),
        row(value_bias),
        seg,
    )
    empty = jnp.zeros((2, width), F32)
    vec = jnp.concatenate(
        [
            row(output_bias),
            row(first_gain),
            row(first_shift),
            row(outer_bias),
            row(second_gain),
            row(second_shift),
            empty,
        ],
        axis=0,
    )
    out, out_far, first, act, og, ig, fp, ag, dctx, sums, isum = token_pass(
        here_id, h, ctx, cotangent, cot_far, output_matrix, inner_matrix, outer_matrix, row(inner_bias), vec
    )
    out_came = trade(out_far)
    x_mine, x_away, y_mine, y_away = here, 1 - here, y_at, 1 - y_at
    a_keep, a_send = outer_grad_call(core_id, act, og, sums, isum)
    a0 = seq_swap(a_send, 1)
    b_keep, b_send, a_keep = inner_grad_call(core_id, first, ig, ctx, ag, (a_keep,))
    b0 = seq_swap(b_send, 1)
    a = (a_keep, a0)
    a_away = sum_0(a, x_away).astype(BF16)
    a1 = trade(a_away)
    b = (b_keep, b0)
    b_away = sum_0(b, y_away).astype(BF16)
    b1 = seq_swap(b_away, 2)
    bwd = (q, k, v, dctx, ctx, lse, seg)
    held = attention_backward(0, *bwd, (), (), (a_away, b_away))
    *held, a_keep, b_keep = attention_backward(1, *bwd, held, (a_keep, b_keep), ())
    a = (a_keep, a0, a1)
    a_away = sum_1(a, x_mine, y_away).astype(BF16)
    a2 = seq_swap(a_away, 2)
    c_keep, c_send, b_keep = projection_grad_call(
        core_id, h, held[0], sums, 0, 2 * GROUP, False, (b_keep,), (a_away,)
    )
    c0 = seq_swap(c_send, 1)
    b = (b_keep, b0, b1)
    b_away = sum_1(b, y_mine, x_away).astype(BF16)
    b2 = trade(b_away)
    dqkv, sums2, a_keep, b_keep, c_keep = attention_backward(
        2, *bwd, held, (a_keep, b_keep, c_keep), (c_send, b_away)
    )
    c = (c_keep, c0)
    c_away = sum_0(c, y_away).astype(BF16)
    c1 = seq_swap(c_away, 2)
    d_keep, d_send, a_keep, b_keep, out_came = projection_grad_call(
        core_id, h, dqkv, sums2, 2, GROUP, True, (a_keep, b_keep, out_came), (c_away,)
    )
    d0 = seq_swap(d_send, 1)
    a = (a_keep, a0, a1, a2)
    b = (b_keep, b0, b1, b2)

    def both(z):
        a_part = sum_2(a, x_mine, y_mine, z)
        b_part = sum_2(b, y_mine, x_mine, z)
        return jnp.concatenate([a_part, b_part.reshape(-1, width // 2)], axis=0)

    parts = [both(z_at ^ e).astype(BF16) for e in (1, 2, 3)]
    ab3 = send_z(parts)
    args = (fp, dqkv, query_matrix, key_matrix, value_matrix)
    far_grad, c_keep, d_keep = hidden_away(*args, (c_keep, d_keep), (parts[0],))
    came = trade(far_grad)
    d = (d_keep, d0)
    d_away = sum_0(d, y_away).astype(BF16)
    d1 = seq_swap(d_away, 2)
    hidden_grad, layer_out, a_keep, b_keep, c_keep, d_keep = hidden_home(
        here_id, *args, out_came, out, (a_keep, b_keep, c_keep, d_keep), (d_away,)
    )
    c = (c_keep, c0, c1)
    d = (d_keep, d0, d1)

    def late_1(*at):
        return lanes_of(sum_1(c, y_mine, *at), sum_1(d, y_mine, *at))

    def lanes_of(*parts):
        return jnp.concatenate(parts, axis=-1)

    e2 = trade(late_1(x_away).astype(BF16))

    def late_2(z):
        return rounded(late_1(x_mine, z) + pick(e2, z).astype(F32))

    e3 = send_z([late_2(z_at ^ e).astype(BF16) for e in (1, 2, 3)])
    hidden_grad, a_keep, b_keep = place_far(here_id, came, hidden_grad, (a_keep, b_keep))
    a = (a_keep, a0, a1, a2)
    b = (b_keep, b0, b1, b2)
    early = add_z(both(z_at), ab3)
    late = add_z(late_2(z_at), e3)
    rows = width // 16
    outer_rows = 4 * rows
    outer_grad = early[:outer_rows]
    vectors = early[outer_rows : outer_rows + VECTOR_ROWS].reshape(-1, width)
    inner_all = early[outer_rows + VECTOR_ROWS :].reshape(5, rows, width // 2)
    output_grad = inner_all[4]
    inner_grad = jnp.transpose(inner_all[:4], (1, 0, 2)).reshape(rows, -1)
    units = width // UNIT
    biases = late[3 * rows :, 2 * UNIT :][: 2 * units].reshape(2, units // 2, 2, UNIT)
    biases = jnp.transpose(biases, (0, 2, 1, 3)).reshape(2, width)
    return (
        layer_out,
        hidden_grad,
        late[:rows],
        biases[0],
        late[rows : 2 * rows],
        late[2 * rows : 3 * rows],
        biases[1],
        output_grad,
        vectors[5],
        vectors[3],
        vectors[4],
        inner_grad,
        vectors[6:10].reshape(-1),
        outer_grad,
        vectors[2],
        vectors[0],
        vectors[1],
    )


def choose(sizes, *args):
    seq_count, row_count, width = args[0].shape
    whole_here = sizes[1] == 2 and seq_count == 2 and row_count % TILE == 0 and width == 3 * GROUP
    return fast(*args) if whole_here and sizes[0] == 16 else general(*args)


def solution(mesh):
    sizes = (mesh.shape["seq"], mesh.shape["blk"])
    return jax.shard_map(
        functools.partial(choose, sizes),
        mesh=mesh,
        in_specs=(
            P("seq", "blk", None),
            P("seq", "blk"),
            P(),
            P(),
            P(),
            P(),
            P(),
            P(),
            P(),
            P(),
            P(),
            P(),
            P(),
            P(),
            P(),
            P(),
            P(),
            P("seq", "blk", None),
        ),
        out_specs=(
            P("seq", "blk", None),
            P("seq", "blk", None),
            P("seq", "blk"),
            P(),
            P("seq", "blk"),
            P("seq", "blk"),
            P(),
            P("seq", "blk"),
            P(),
            P(),
            P(),
            P("seq", "blk"),
            P(),
            P("seq", "blk"),
            P(),
            P(),
            P(),
        ),
        check_vma=False,
    )
```

```python
import functools
import math

import jax
import jax.numpy as jnp
from jax import lax
from jax.experimental import pallas as pl
from jax.experimental.pallas import tpu as pltpu
from jax.sharding import PartitionSpec as P

HEADS = 12
HEAD = 64


NEGATIVE = -1e30
EPSILON = 1e-12


def layer_norm(values, norm_gain, norm_shift):
    centre = values - jnp.mean(values, axis=-1, keepdims=True)
    spread = jnp.mean(centre * centre, axis=-1, keepdims=True)
    return centre * lax.rsqrt(spread + EPSILON) * norm_gain + norm_shift


def gelu_exact(values):
    return jax.nn.gelu(values, approximate=False)


def linear(operand, matrix):
    return jnp.dot(operand, matrix, preferred_element_type=jnp.float32)


def split_heads(values):
    return values.reshape(values.shape[0], values.shape[1], HEADS, HEAD)


def block_scores(query_block, key_block, score_scale):
    return (
        jnp.einsum("sqhd,skhd->shqk", query_block, key_block, preferred_element_type=jnp.float32)
        * score_scale
    )


def attention_grads(
    query_block, key_block, value_block, dctx_block, same_doc, log_total, row_delta, score_scale
):
    attn_probs = jnp.where(
        same_doc,
        jnp.exp(block_scores(query_block, key_block, score_scale) - log_total[..., None]),
        0.0,
    )
    slopes = jnp.einsum(
        "sqhd,skhd->shqk", dctx_block, value_block, preferred_element_type=jnp.float32
    )
    return (attn_probs, (attn_probs * (slopes - row_delta[..., None])).astype(jnp.bfloat16))


def over_blocks(length, step, initial):
    block_size = math.gcd(length, 512)

    def scan_step(carried, block_index):
        return (step(carried, block_index * block_size, block_size), None)

    result, unused = lax.scan(scan_step, initial, jnp.arange(length // block_size, dtype=jnp.int32))
    return result


def general(
    hidden,
    segments,
    query_matrix,
    query_bias,
    key_matrix,
    value_matrix,
    value_bias,
    output_matrix,
    output_bias,
    first_gain,
    first_shift,
    inner_matrix,
    inner_bias,
    outer_matrix,
    outer_bias,
    second_gain,
    second_shift,
    cotangent,
):
    seq_count, row_count, model_width = hidden.shape
    score_scale = HEAD ** (-0.5)
    single_float = jnp.float32
    bf16 = jnp.bfloat16
    queries = (linear(hidden, query_matrix) + query_bias.astype(single_float)).astype(bf16)
    key_proj = linear(hidden, key_matrix).astype(bf16)
    value_proj = (linear(hidden, value_matrix) + value_bias.astype(single_float)).astype(bf16)
    seg_all = lax.all_gather(segments, "blk", axis=1, tiled=True)
    keys_all, values_all = (
        lax.all_gather(key_proj, "blk", axis=1, tiled=True),
        lax.all_gather(value_proj, "blk", axis=1, tiled=True),
    )
    length = seg_all.shape[1]
    query_heads = split_heads(queries)
    key_heads = split_heads(keys_all)
    value_heads = split_heads(values_all)

    def key_slices(offset, block_size):
        key_segs = lax.dynamic_slice_in_dim(seg_all, offset, block_size, 1)
        same_doc = (segments[:, :, None] == key_segs[:, None, :])[:, None]
        key_block = lax.dynamic_slice_in_dim(key_heads, offset, block_size, 1)
        value_block = lax.dynamic_slice_in_dim(value_heads, offset, block_size, 1)
        return (same_doc, key_block, value_block)

    def stats_step(carried, offset, block_size):
        same_doc, key_block, value_block = key_slices(offset, block_size)
        running_max, running_sum = carried
        scores = jnp.where(same_doc, block_scores(query_heads, key_block, score_scale), NEGATIVE)
        higher = jnp.maximum(running_max, jnp.max(scores, axis=-1))
        weights = jnp.where(same_doc, jnp.exp(scores - higher[..., None]), 0.0)
        return (higher, running_sum * jnp.exp(running_max - higher) + jnp.sum(weights, axis=-1))

    stat_shape = (seq_count, HEADS, row_count)
    running_max, running_sum = over_blocks(
        length,
        stats_step,
        (jnp.full(stat_shape, NEGATIVE, single_float), jnp.zeros(stat_shape, single_float)),
    )
    log_total = running_max + jnp.log(running_sum)

    def context_step(carried, offset, block_size):
        same_doc, key_block, value_block = key_slices(offset, block_size)
        attn_probs = jnp.where(
            same_doc,
            jnp.exp(block_scores(query_heads, key_block, score_scale) - log_total[..., None]),
            0.0,
        )
        return carried + jnp.einsum(
            "shqk,skhd->sqhd",
            attn_probs.astype(bf16),
            value_block,
            preferred_element_type=single_float,
        )

    head_zeros = jnp.zeros((seq_count, row_count, HEADS, HEAD), single_float)
    context = over_blocks(length, context_step, head_zeros)
    context_reduced = context.reshape(seq_count, row_count, model_width).astype(bf16)
    attn_out = linear(context_reduced, output_matrix) + output_bias.astype(single_float)
    first_pre = hidden.astype(single_float) + attn_out
    first_norm, first_back = jax.vjp(
        layer_norm, first_pre, first_gain.astype(single_float), first_shift.astype(single_float)
    )
    first_reduced = first_norm.astype(bf16)
    inner = linear(first_reduced, inner_matrix) + inner_bias.astype(single_float)
    act_full, gelu_back = jax.vjp(gelu_exact, inner)
    activation_reduced = act_full.astype(bf16)
    outer = linear(activation_reduced, outer_matrix) + outer_bias.astype(single_float)
    layer_full, second_back = jax.vjp(
        layer_norm,
        first_norm + outer,
        second_gain.astype(single_float),
        second_shift.astype(single_float),
    )
    layer_out = layer_full.astype(bf16)
    second_pre_grad, second_gain_grad, second_shift_grad = second_back(
        cotangent.astype(single_float)
    )
    outer_gradient_reduced = second_pre_grad.astype(bf16)
    outer_weight_grad = jnp.einsum(
        "gvx,gvm->xm",
        activation_reduced,
        outer_gradient_reduced,
        preferred_element_type=single_float,
    )
    outer_bias_grad = jnp.sum(outer_gradient_reduced.astype(single_float), axis=(0, 1))
    activation_gradient = jnp.einsum(
        "rzo,uo->rzu", outer_gradient_reduced, outer_matrix, preferred_element_type=single_float
    )
    inner_gradient_reduced = gelu_back(activation_gradient)[0].astype(bf16)
    inner_weight_grad = jnp.einsum(
        "ret,reu->tu", first_reduced, inner_gradient_reduced, preferred_element_type=single_float
    )
    inner_bias_grad = jnp.sum(inner_gradient_reduced.astype(single_float), axis=(0, 1))
    first_norm_grad = second_pre_grad + jnp.einsum(
        "aoi,ni->aon", inner_gradient_reduced, inner_matrix, preferred_element_type=single_float
    )
    first_pre_grad, first_gain_grad, first_shift_grad = first_back(first_norm_grad)
    attention_gradient_reduced = first_pre_grad.astype(bf16)
    output_weight_grad = jnp.einsum(
        "tfm,tfc->mc",
        context_reduced,
        attention_gradient_reduced,
        preferred_element_type=single_float,
    )
    output_bias_grad = jnp.sum(attention_gradient_reduced.astype(single_float), axis=(0, 1))
    dctx_low = jnp.einsum(
        "upx,cx->upc",
        attention_gradient_reduced,
        output_matrix,
        preferred_element_type=single_float,
    ).astype(bf16)
    dctx_heads = split_heads(dctx_low)
    row_delta = jnp.transpose(
        jnp.sum(dctx_heads.astype(single_float) * context, axis=-1), (0, 2, 1)
    )

    def query_step(carried, offset, block_size):
        same_doc, key_block, value_block = key_slices(offset, block_size)
        attn_probs, dscores = attention_grads(
            query_heads,
            key_block,
            value_block,
            dctx_heads,
            same_doc,
            log_total,
            row_delta,
            score_scale,
        )
        return carried + score_scale * jnp.einsum(
            "shqk,skhd->sqhd", dscores, key_block, preferred_element_type=single_float
        )

    query_grad = over_blocks(length, query_step, head_zeros)
    query_all, dctx_all = (
        lax.all_gather(queries, "blk", axis=1, tiled=True),
        lax.all_gather(dctx_low, "blk", axis=1, tiled=True),
    )
    lse_all, delta_all = (
        lax.all_gather(log_total, "blk", axis=2, tiled=True),
        lax.all_gather(row_delta, "blk", axis=2, tiled=True),
    )
    query_all_heads = split_heads(query_all)
    dctx_all_heads = split_heads(dctx_all)
    own_keys = split_heads(key_proj)
    own_values = split_heads(value_proj)

    def key_step(carried, offset, block_size):
        query_segs = lax.dynamic_slice_in_dim(seg_all, offset, block_size, 1)
        same_doc = (query_segs[:, :, None] == segments[:, None, :])[:, None]
        query_block = lax.dynamic_slice_in_dim(query_all_heads, offset, block_size, 1)
        dctx_block = lax.dynamic_slice_in_dim(dctx_all_heads, offset, block_size, 1)
        lse_block = lax.dynamic_slice_in_dim(lse_all, offset, block_size, 2)
        delta_block = lax.dynamic_slice_in_dim(delta_all, offset, block_size, 2)
        key_sum, value_sum = carried
        attn_probs, dscores = attention_grads(
            query_block,
            own_keys,
            own_values,
            dctx_block,
            same_doc,
            lse_block,
            delta_block,
            score_scale,
        )
        key_sum = key_sum + score_scale * jnp.einsum(
            "shqk,sqhd->skhd", dscores, query_block, preferred_element_type=single_float
        )
        value_sum = value_sum + jnp.einsum(
            "shqk,sqhd->skhd",
            attn_probs.astype(bf16),
            dctx_block,
            preferred_element_type=single_float,
        )
        return (key_sum, value_sum)

    key_grad, value_grad = over_blocks(length, key_step, (head_zeros, head_zeros))
    query_gradient_reduced = query_grad.reshape(seq_count, row_count, model_width).astype(bf16)
    key_gradient_reduced = key_grad.reshape(seq_count, row_count, model_width).astype(bf16)
    value_gradient_reduced = value_grad.reshape(seq_count, row_count, model_width).astype(bf16)
    query_weight_grad = jnp.einsum(
        "tfm,tfc->mc", hidden, query_gradient_reduced, preferred_element_type=single_float
    )
    query_bias_grad = jnp.sum(query_gradient_reduced.astype(single_float), axis=(0, 1))
    key_matrix_gradient = jnp.einsum(
        "tfm,tfc->mc", hidden, key_gradient_reduced, preferred_element_type=single_float
    )
    value_weight_grad = jnp.einsum(
        "tfm,tfc->mc", hidden, value_gradient_reduced, preferred_element_type=single_float
    )
    value_bias_grad = jnp.sum(value_gradient_reduced.astype(single_float), axis=(0, 1))
    hidden_grad = first_pre_grad + jnp.einsum(
        "upx,cx->upc", query_gradient_reduced, query_matrix, preferred_element_type=single_float
    )
    hidden_grad = hidden_grad + jnp.einsum(
        "upx,cx->upc", key_gradient_reduced, key_matrix, preferred_element_type=single_float
    )
    hidden_grad = hidden_grad + jnp.einsum(
        "upx,cx->upc", value_gradient_reduced, value_matrix, preferred_element_type=single_float
    )
    partial_sums = (
        lax.psum_scatter(query_weight_grad, "seq", scatter_dimension=0, tiled=True),
        lax.psum_scatter(key_matrix_gradient, "seq", scatter_dimension=0, tiled=True),
        lax.psum_scatter(value_weight_grad, "seq", scatter_dimension=0, tiled=True),
        lax.psum_scatter(output_weight_grad, "seq", scatter_dimension=0, tiled=True),
        lax.psum_scatter(inner_weight_grad, "seq", scatter_dimension=0, tiled=True),
        lax.psum_scatter(outer_weight_grad, "seq", scatter_dimension=0, tiled=True),
    )
    matrices = lax.psum_scatter(tuple(partial_sums), "blk", scatter_dimension=1, tiled=True)
    vectors = lax.psum(
        (
            query_bias_grad,
            value_bias_grad,
            output_bias_grad,
            first_gain_grad,
            first_shift_grad,
            inner_bias_grad,
            outer_bias_grad,
            second_gain_grad,
            second_shift_grad,
        ),
        ("seq", "blk"),
    )
    return (
        layer_out,
        hidden_grad,
        matrices[0],
        vectors[0],
        matrices[1],
        matrices[2],
        vectors[1],
        matrices[3],
        vectors[2],
        vectors[3],
        vectors[4],
        matrices[4],
        vectors[5],
        matrices[5],
        vectors[6],
        vectors[7],
        vectors[8],
    )


BF16 = jnp.bfloat16
F32 = jnp.float32
NN = ((1,), (0,))
NT = ((1,), (1,))
TN = ((0,), (0,))
UNIT = 128
GROUP = 256
PER_GROUP = GROUP // HEAD
TILE = 256
TOKENS = 512
VMEM_LIMIT = 60 * 2**20
SCALAR = pl.BlockSpec(memory_space=pltpu.SMEM)
ANY = pl.BlockSpec(memory_space=pl.ANY)


def mm(a, b, dims):
    return lax.dot_general(a, b, (dims, ((), ())), preferred_element_type=F32)


def fixed(shape):
    return pl.BlockSpec(shape, lambda *_: (0,) * len(shape), pipeline_mode=pl.Buffered(1))


def run(
    kernel,
    name,
    grid,
    operands,
    in_specs,
    out_shape,
    out_specs,
    scratch=(),
    scalars=0,
    held=None,
    passes=(),
    after=(),
    micros=1,
):
    held = held or {}
    out_shape, out_specs = list(out_shape), list(out_specs)
    n_in, n_out, n_held, n_pass = len(operands), len(out_shape), len(held), len(passes)
    aliases = {n_in + i: at for i, at in enumerate(held)}
    aliases |= {n_in + n_held + i: n_out + i for i in range(n_pass)}

    def body(*refs):
        outs = n_in + n_held + n_pass + len(after)
        kernel(*refs[:n_in], *refs[outs : outs + n_out], *refs[outs + n_out + n_pass :])

    result = pl.pallas_call(
        body,
        grid_spec=pltpu.PrefetchScalarGridSpec(
            num_scalar_prefetch=scalars,
            grid=grid,
            in_specs=list(in_specs) + [ANY] * (n_held + n_pass + len(after)),
            out_specs=out_specs + [ANY] * n_pass,
            scratch_shapes=list(scratch),
        ),
        out_shape=out_shape + [jax.ShapeDtypeStruct(x.shape, x.dtype) for x in passes],
        input_output_aliases=aliases,
        compiler_params=pltpu.CompilerParams(
            vmem_limit_bytes=VMEM_LIMIT, dimension_semantics=("arbitrary",) * len(grid)
        ),
        cost_estimate=pl.CostEstimate(
            flops=int(micros * 1e7), bytes_accessed=0, transcendentals=0
        ),
        name=name,
    )(*operands, *held.values(), *passes, *after)
    return result


def head_lanes(shape, head):
    lane = lax.broadcasted_iota(jnp.int32, shape, 1)
    return (lane >= head * HEAD) & (lane < (head + 1) * HEAD)


def lanes(*parts):
    return jnp.concatenate(parts, axis=1)


def column_of(row):
    return jnp.transpose(jnp.broadcast_to(row.astype(F32), (UNIT, row.shape[1])))[:, 0:1]


def same_pair(row, column, rows):
    return jnp.where(column[rows] == row, 0.0, NEGATIVE)


def attention_forward_kernel(
    here_ref,
    own_ref,
    far_ref,
    wq0_ref,
    wq1_ref,
    wk0_ref,
    wk1_ref,
    wv0_ref,
    wv1_ref,
    bq0_ref,
    bq1_ref,
    bv0_ref,
    bv1_ref,
    seg_ref,
    q_ref,
    k_ref,
    v_ref,
    ctx_ref,
    lse_ref,
    h_ref,
    mask_ref,
    vaug_ref,
):
    half = far_ref.shape[0]
    length = 2 * half

    @pl.when(pl.program_id(0) == 0)
    def _():
        segr = seg_ref[...].astype(F32)
        mask_ref[...] = jnp.where(column_of(segr) == segr, 0.0, NEGATIVE)
        h_ref[0:half, :] = own_ref[0]
        h_ref[half:, :] = far_ref[...]

    h = h_ref[...]
    bias_q = lanes(bq0_ref[...], bq1_ref[...])
    bias_v = lanes(bv0_ref[...], bv1_ref[...])
    q_ref[...] = (mm(h, lanes(wq0_ref[...], wq1_ref[...]), NN) + bias_q).astype(BF16)
    k_ref[...] = mm(h, lanes(wk0_ref[...], wk1_ref[...]), NN).astype(BF16)
    v = (mm(h, lanes(wv0_ref[...], wv1_ref[...]), NN) + bias_v).astype(BF16)
    v_ref[...] = v
    lane = lax.broadcasted_iota(jnp.int32, v.shape, 1)
    for head in range(PER_GROUP):
        other = (lane // UNIT) != (head // 2)
        filler = jnp.where(other, 1.0, 0.0).astype(BF16)
        vaug_ref[head] = jnp.where(head_lanes(v.shape, head), v, filler)

    def block(i, carry):
        rows = pl.ds(pl.multiple_of(i * TILE, TILE), TILE)
        qb = q_ref[rows, :] * BF16(HEAD**-0.5)
        halves = [None, None]
        stat_lane = lax.broadcasted_iota(jnp.int32, (TILE, UNIT), 1)
        stats = jnp.zeros((TILE, UNIT), F32)
        for head in range(PER_GROUP):
            qm = jnp.where(head_lanes(qb.shape, head), qb, BF16(0))
            s = mm(qm, k_ref[...], NT) + mask_ref[rows, :]
            top = jnp.max(s, axis=1, keepdims=True)
            e = jnp.exp(s - top).astype(BF16)
            o = mm(e, vaug_ref[head], NN)
            t = head // 2
            total = o[:, (1 - t) * UNIT : (2 - t) * UNIT]
            part = o[:, t * UNIT : (t + 1) * UNIT] / total
            halves[t] = part if halves[t] is None else halves[t] + part
            stats = jnp.where(stat_lane == head, top + jnp.log(total), stats)
        ctx_ref[0, rows, :] = halves[0].astype(BF16)
        ctx_ref[1, rows, :] = halves[1].astype(BF16)
        lse_ref[:, rows] = jnp.transpose(stats)[0:8]
        return carry

    lax.fori_loop(0, length // TILE, block, 0, unroll=True)


def attention_forward(here, hidden, far, wq, wk, wv, bq, bv, seg):
    half, width = far.shape
    length = 2 * half
    groups = width // GROUP
    left = pl.BlockSpec((width, UNIT), lambda g, h: (0, g))
    right = pl.BlockSpec((width, UNIT), lambda g, h: (0, groups + g))
    bias_left = pl.BlockSpec((1, UNIT), lambda g, h: (0, g))
    bias_right = pl.BlockSpec((1, UNIT), lambda g, h: (0, groups + g))
    rows = pl.BlockSpec((length, GROUP), lambda g, h: (0, g))
    wide = jax.ShapeDtypeStruct((length, width), BF16)
    own = pl.BlockSpec((1, half, width), lambda g, h: (h[0], 0, 0), pipeline_mode=pl.Buffered(1))
    return run(
        attention_forward_kernel,
        "attention_forward",
        (groups,),
        (here, hidden, far, wq, wq, wk, wk, wv, wv, bq, bq, bv, bv, seg),
        [own, fixed((half, width))]
        + [left, right] * 3
        + [bias_left, bias_right] * 2
        + [fixed((1, length))],
        (
            wide,
            wide,
            wide,
            jax.ShapeDtypeStruct((2, length, width // 2), BF16),
            jax.ShapeDtypeStruct((8 * groups, length), F32),
            wide,
        ),
        (
            rows,
            rows,
            rows,
            pl.BlockSpec((2, length, UNIT), lambda g, h: (0, 0, g)),
            pl.BlockSpec((8, length), lambda g, h: (g, 0)),
            pl.BlockSpec((length, width), lambda g, h: (0, 0)),
        ),
        [pltpu.VMEM((length, length), F32), pltpu.VMEM((PER_GROUP, length, GROUP), BF16)],
        scalars=1,
        micros=16,
    )


def gelu_pair(u):
    phi = 0.5 + 0.5 * lax.erf(u * 0.7071067811865476)
    bell = jnp.exp2(u * u * -0.7213475204444817)
    return (u * phi, phi + u * bell * 0.3989422804014327)


def normed(x):
    centre = x - jnp.mean(x, axis=1, keepdims=True)
    scale = lax.rsqrt(jnp.mean(centre * centre, axis=1, keepdims=True) + EPSILON)
    return (centre * scale, scale)


def norm_back(u, n, scale):
    return scale * (u - jnp.mean(u, axis=1, keepdims=True) - n * jnp.mean(u * n, axis=1, keepdims=True))


def row_sum(x):
    return jnp.sum(x, axis=0, keepdims=True)


def token_kernel(
    here_ref,
    h_ref,
    ctx_ref,
    cot_own_ref,
    cot_far_ref,
    wo_ref,
    wi_ref,
    wp_ref,
    bi_ref,
    vec_ref,
    out_ref,
    far0_ref,
    far1_ref,
    first_ref,
    act_ref,
    og_ref,
    ig_ref,
    fp_ref,
    ag_ref,
    dctx_ref,
    sums_ref,
    isum_ref,
    slope_ref,
):
    step = pl.program_id(0)
    steps = pl.num_programs(0)

    @pl.when(step == 0)
    def _():
        sums_ref[...] = jnp.zeros_like(sums_ref)
        isum_ref[...] = jnp.zeros_like(isum_ref)

    ff = wi_ref.shape[1]
    chunk = 512
    output_bias, gain1, shift1 = vec_ref[0:1, :], vec_ref[1:2, :], vec_ref[2:3, :]
    outer_bias, gain2, shift2 = vec_ref[3:4, :], vec_ref[4:5, :], vec_ref[5:6, :]
    middle = wo_ref.shape[0] // 2
    near = step < steps // 2

    def part(rows):
        ctx = lanes(ctx_ref[0, rows, :], ctx_ref[1, rows, :])
        x = h_ref[rows, :].astype(F32) + mm(ctx, wo_ref[...], NN) + output_bias
        yield
        n1, r1 = normed(x)
        fn = n1 * gain1 + shift1
        first = fn.astype(BF16)
        first_ref[rows, :] = first
        yield
        for c in range(0, ff, chunk):
            act, slope = gelu_pair(mm(first, wi_ref[:, c : c + chunk], NN) + bi_ref[:, c : c + chunk])
            act_ref[rows, c : c + chunk] = act.astype(BF16)
            slope_ref[rows, c : c + chunk] = slope
            yield
        x = fn + mm(act_ref[rows, :], wp_ref[...], NN) + outer_bias
        yield
        n2, r2 = normed(x)
        out = (n2 * gain2 + shift2).astype(BF16)

        @pl.when(near)
        def _():
            out_ref[0, rows, :] = out

        @pl.when(jnp.logical_not(near))
        def _():
            (far1_ref if rows.start else far0_ref)[...] = out

        e = jnp.where(near, cot_own_ref[0, rows, :], cot_far_ref[rows, :]).astype(F32)
        sums_ref[0:1, :] += row_sum(e * n2)
        sums_ref[1:2, :] += row_sum(e)
        sp = norm_back(e * gain2, n2, r2)
        og = sp.astype(BF16)
        og_ref[rows, :] = og
        sums_ref[2:3, :] += row_sum(og.astype(F32))
        yield
        for c in range(0, ff, chunk):
            ig = (mm(og, wp_ref[c : c + chunk, :], NT) * slope_ref[rows, c : c + chunk]).astype(BF16)
            ig_ref[rows, c : c + chunk] = ig
            isum_ref[:, c : c + chunk] += row_sum(ig.astype(F32))
            yield
        d = sp + mm(ig_ref[rows, :], wi_ref[...], NT)
        yield
        sums_ref[3:4, :] += row_sum(d * n1)
        sums_ref[4:5, :] += row_sum(d)
        fp = norm_back(d * gain1, n1, r1)
        fp_ref[rows, :] = fp
        ag = fp.astype(BF16)
        ag_ref[rows, :] = ag
        sums_ref[5:6, :] += row_sum(ag.astype(F32))
        yield
        dctx = mm(ag, wo_ref[...], NT).astype(BF16)
        dctx_ref[0, rows, :] = dctx[:, :middle]
        dctx_ref[1, rows, :] = dctx[:, middle:]

    size = h_ref.shape[0]
    parts = [part(slice(r, r + TILE)) for r in range(0, size, TILE)]
    live, waiting = [], list(parts)
    while waiting or live:
        if waiting:
            live.append(waiting.pop(0))
        live = [p for p in live if next(p, 0) is None]


def token_pass(here, h, ctx, cot, cot_far, wo, wi, wp, bi, vec):
    length, width = h.shape
    half = length // 2
    ff = wi.shape[1]
    steps = length // TOKENS
    near = steps // 2
    rows = pl.BlockSpec((TOKENS, width), lambda i, b: (i, 0))
    split_rows = pl.BlockSpec((2, TOKENS, width // 2), lambda i, b: (0, i, 0))
    wide_rows = pl.BlockSpec((TOKENS, ff), lambda i, b: (i, 0))
    own_rows = pl.BlockSpec((1, TOKENS, width), lambda i, b: (b[0], jnp.minimum(i, near - 1), 0))
    far_rows = pl.BlockSpec((TOKENS, width), lambda i, b: (jnp.maximum(i - near, 0), 0))
    low = jax.ShapeDtypeStruct((length, width), BF16)
    low_ff = jax.ShapeDtypeStruct((length, ff), BF16)
    return run(
        token_kernel,
        "token_pass",
        (steps,),
        (here, h, ctx, cot, cot_far, wo, wi, wp, bi, vec),
        [
            rows,
            split_rows,
            own_rows,
            far_rows,
            fixed((width, width)),
            fixed((width, ff)),
            fixed((ff, width)),
            fixed((1, ff)),
            fixed((8, width)),
        ],
        (
            jax.ShapeDtypeStruct((2, half, width), BF16),
            jax.ShapeDtypeStruct((half // 2, width), BF16),
            jax.ShapeDtypeStruct((half // 2, width), BF16),
            low,
            low_ff,
            low,
            low_ff,
            jax.ShapeDtypeStruct((length, width), F32),
            low,
            jax.ShapeDtypeStruct((2, length, width // 2), BF16),
            jax.ShapeDtypeStruct((8, width), F32),
            jax.ShapeDtypeStruct((1, ff), F32),
        ),
        (
            own_rows,
            pl.BlockSpec((half // 2, width), lambda i, b: (0, 0)),
            pl.BlockSpec((half // 2, width), lambda i, b: (0, 0)),
            rows,
            wide_rows,
            rows,
            wide_rows,
            rows,
            rows,
            split_rows,
            pl.BlockSpec((8, width), lambda i, b: (0, 0)),
            pl.BlockSpec((1, ff), lambda i, b: (0, 0)),
        ),
        [pltpu.VMEM((TOKENS, ff), F32)],
        scalars=1,
        micros=23,
    )


def put_pairs(res, core_ref, keep_ref, send_ref, columns, rows, count):
    even = core_ref[0] == 0
    for z in range(count):
        for y in range(2):
            base = (z * 2 + y) * 2 * rows
            for x in range(2):
                zero = lanes(*[res[base : base + rows, c] for c in columns[x]])
                one = lanes(*[res[base + rows : base + 2 * rows, c] for c in columns[x]])
                keep_ref[x, y, z, 0] = jnp.where(even, zero, one).astype(BF16)
                send_ref[x, y, z, 0] = jnp.where(even, one, zero).astype(BF16)


HALVES = ((slice(0, 384),), (slice(384, 768),))
VECTOR_ROWS = 32
BIAS_ROWS = 16


def outer_grad_kernel(core_ref, act_ref, og_ref, sums_ref, isum_ref, keep_ref, send_ref, rows_ref):
    res = mm(act_ref[...], og_ref[...], TN)
    middle = res.shape[1] // 2
    rows = res.shape[0] // 4
    even = core_ref[0] == 0
    rows_ref[...] = jnp.zeros_like(rows_ref)
    at = 0
    for r in range(6):
        for x in range(2):
            rows_ref[at : at + 1, :] = sums_ref[r : r + 1, x * middle : (x + 1) * middle]
            at += 1
    for r in range(isum_ref.shape[1] // middle):
        rows_ref[at : at + 1, :] = isum_ref[:, r * middle : (r + 1) * middle]
        at += 1
    extra = rows_ref[...].astype(BF16)
    for y in range(2):
        for x in range(2):
            columns = slice(x * middle, (x + 1) * middle)
            zero = res[2 * y * rows : (2 * y + 1) * rows, columns]
            one = res[(2 * y + 1) * rows : (2 * y + 2) * rows, columns]
            keep_ref[y, x, 0, 0:rows, :] = jnp.where(even, zero, one).astype(BF16)
            send_ref[y, x, 0, 0:rows, :] = jnp.where(even, one, zero).astype(BF16)
            keep_ref[y, x, 0, rows:, :] = extra
            send_ref[y, x, 0, rows:, :] = extra


def pair_out(shape, block, index):
    kind = jax.ShapeDtypeStruct(shape, BF16)
    spec = pl.BlockSpec(block, index)
    return ((kind, kind), (spec, spec))


def outer_grad_call(core, act, og, sums, isum):
    length, ff = act.shape
    width = og.shape[1]
    shape = (2, 2, 4, ff // 16 + VECTOR_ROWS, width // 2)
    kinds, specs = pair_out(shape, (2, 2, 1) + shape[3:], lambda z: (0, 0, z, 0, 0))
    return run(
        outer_grad_kernel,
        "outer_grad",
        (4,),
        (core, act, og, sums, isum),
        [
            SCALAR,
            pl.BlockSpec((length, ff // 4), lambda z: (0, z)),
            fixed((length, width)),
            fixed(sums.shape),
            fixed(isum.shape),
        ],
        kinds,
        specs,
        [pltpu.VMEM((VECTOR_ROWS, width // 2), F32)],
        micros=4.5,
    )


def inner_grad_kernel(
    core_ref, first_ref, low_ref, high_ref, ctx_ref, ag_ref, keep_ref, send_ref
):
    step = pl.program_id(0)
    rows = keep_ref.shape[4]

    @pl.when(step < 4)
    def _():
        res = mm(first_ref[...], lanes(low_ref[...], high_ref[...]), TN)
        put_pairs(res, core_ref, keep_ref, send_ref, HALVES, rows, 4)

    @pl.when(step == 4)
    def _():
        res = mm(lanes(ctx_ref[0], ctx_ref[1]), ag_ref[...], TN)
        put_pairs(res, core_ref, keep_ref, send_ref, HALVES, rows, 4)


def inner_grad_call(core, first, ig, ctx, ag, passes):
    length, width = first.shape
    shape = (2, 2, 4, 5, width // 16, width // 2)
    kinds, specs = pair_out(shape, shape[:3] + (1,) + shape[4:], lambda s: (0, 0, 0, s, 0, 0))
    return run(
        inner_grad_kernel,
        "inner_grad",
        (5,),
        (core, first, ig, ig, ctx, ag),
        [
            SCALAR,
            fixed((length, width)),
            pl.BlockSpec((length, width // 2), lambda s: (0, jnp.minimum(s, 3))),
            pl.BlockSpec((length, width // 2), lambda s: (0, 4 + jnp.minimum(s, 3))),
            fixed((2, length, width // 2)),
            fixed((length, width)),
        ],
        kinds,
        specs,
        passes=passes,
        micros=6,
    )


def projection_grad_kernel(with_sums, core_ref, h_ref, d_ref, sums_ref, keep_ref, send_ref):
    step = pl.program_id(0)
    res = mm(h_ref[...], d_ref[0], TN)
    rows = res.shape[0] // 16
    units = res.shape[1] // UNIT
    columns = [[slice(u * UNIT, (u + 1) * UNIT) for u in range(x, units, 2)] for x in range(2)]
    even = core_ref[0] == 0
    for s in range(3):

        @pl.when(step == s)
        def _(s=s):
            place = slice(s * rows, (s + 1) * rows)
            for z in range(4):
                for y in range(2):
                    base = (z * 2 + y) * 2 * rows
                    for x in range(2):
                        zero = lanes(*[res[base : base + rows, c] for c in columns[x]])
                        one = lanes(*[res[base + rows : base + 2 * rows, c] for c in columns[x]])
                        keep_ref[y, x, z, place, :] = jnp.where(even, zero, one).astype(BF16)
                        send_ref[y, x, z, place, :] = jnp.where(even, one, zero).astype(BF16)

    @pl.when(step == 0)
    def _():
        extra = jnp.zeros((BIAS_ROWS, keep_ref.shape[4]), F32)
        if with_sums:
            at = lax.broadcasted_iota(jnp.int32, extra.shape, 0)
            count = sums_ref.shape[1] // UNIT
            for r in range(2):
                for u in range(count):
                    part = sums_ref[r : r + 1, u * UNIT : (u + 1) * UNIT]
                    extra = jnp.where(at == r * count + u, part, extra)
        for z in range(4):
            for y in range(2):
                for x in range(2):
                    keep_ref[y, x, z, 3 * rows :, :] = extra.astype(BF16)
                    send_ref[y, x, z, 3 * rows :, :] = extra.astype(BF16)


def projection_grad_call(core, h, dqkv, sums, at, span, with_sums, passes, after):
    length, width = h.shape
    shape = (2, 2, 4, 3 * width // 16 + BIAS_ROWS, span // 2)
    kinds, specs = pair_out(shape, shape, lambda s: (0, 0, 0, 0, 0))
    return run(
        functools.partial(projection_grad_kernel, with_sums),
        "projection_grad",
        (3,),
        (core, h, dqkv, sums),
        [
            SCALAR,
            fixed((length, width)),
            pl.BlockSpec((1, length, span), lambda s: (s, 0, at)),
            fixed(sums.shape),
        ],
        kinds,
        specs,
        passes=passes,
        after=after,
        micros=2.5,
    )


def attention_backward_kernel(
    q_ref,
    k_ref,
    v_ref,
    dctx_pair_ref,
    ctx_pair_ref,
    lse_ref,
    seg_ref,
    grads_ref,
    sums_ref,
    delta_ref,
    total_ref,
    kt_ref,
    dctx_ref,
    segc_ref,
):
    length = q_ref.shape[0]
    dctx_ref[...] = lanes(dctx_pair_ref[0], dctx_pair_ref[1])
    ctx = lanes(ctx_pair_ref[0], ctx_pair_ref[1])
    segr = seg_ref[...].astype(F32)
    segc_ref[...] = column_of(segr)
    prod = dctx_ref[...].astype(F32) * ctx.astype(F32)
    high = prod.astype(BF16)
    rest = (prod - high.astype(F32)).astype(BF16)
    lane = lax.broadcasted_iota(jnp.int32, (8, GROUP), 1)
    head_of = lax.broadcasted_iota(jnp.int32, (8, GROUP), 0)
    chooser = jnp.where(lane // HEAD == head_of, 1.0, 0.0).astype(BF16)
    delta_ref[...] = mm(chooser, high, NT) + mm(chooser, rest, NT)
    total_ref[...] = jnp.zeros_like(total_ref)
    kt_ref[...] = jnp.transpose(k_ref[...])

    def block(j, carry):
        rows = pl.ds(pl.multiple_of(j * TILE, TILE), TILE)
        kb = k_ref[rows, :]
        vb = v_ref[rows, :]
        mask = jnp.where(segc_ref[rows, :] == segr, 0.0, NEGATIVE)
        dk = jnp.zeros((TILE, GROUP), F32)
        dv = jnp.zeros((TILE, GROUP), F32)
        for head in range(PER_GROUP):
            mine = head_lanes((TILE, GROUP), head)
            km = jnp.where(mine, kb, BF16(0)) * BF16(HEAD**-0.5)
            vm = jnp.where(mine, vb, BF16(0))
            s = mm(km, q_ref[...], NT) + mask
            p = jnp.exp(s - lse_ref[head : head + 1, :])
            dp = mm(vm, dctx_ref[...], NT)
            ds = (p * (dp - delta_ref[head : head + 1, :])).astype(BF16)
            dv = jnp.where(mine, mm(p.astype(BF16), dctx_ref[...], NN), dv)
            dk = jnp.where(mine, mm(ds, q_ref[...], NN), dk)
            columns = slice(head * HEAD, (head + 1) * HEAD)
            total_ref[columns, :] += mm(kt_ref[columns, rows], ds, NN)
        dkb = (dk * HEAD**-0.5).astype(BF16)
        dvb = dv.astype(BF16)
        grads_ref[1, rows, :] = dkb
        grads_ref[2, rows, :] = dvb
        return carry + row_sum(dvb.astype(F32))

    dv_sum = lax.fori_loop(0, length // TILE, block, jnp.zeros((1, GROUP), F32), unroll=True)
    dq = jnp.transpose(total_ref[...] * HEAD**-0.5).astype(BF16)
    grads_ref[0] = dq
    sums_ref[...] = jnp.zeros_like(sums_ref)
    sums_ref[0:1, :] = row_sum(dq.astype(F32))
    sums_ref[1:2, :] = dv_sum


def attention_backward(g, q, k, v, dctx, ctx, lse, seg, held, passes, after):
    length, width = q.shape
    rows = pl.BlockSpec((length, GROUP), lambda i: (0, g))
    pair_rows = pl.BlockSpec((2, length, UNIT), lambda i: (0, 0, g))
    return run(
        attention_backward_kernel,
        "attention_backward",
        (1,),
        (q, k, v, dctx, ctx, lse, seg),
        [
            rows,
            rows,
            rows,
            pair_rows,
            pair_rows,
            pl.BlockSpec((8, length), lambda i: (g, 0)),
            fixed((1, length)),
        ],
        (jax.ShapeDtypeStruct((3, length, width), BF16), jax.ShapeDtypeStruct((8, width), F32)),
        (
            pl.BlockSpec((3, length, GROUP), lambda i: (0, 0, g)),
            pl.BlockSpec((8, GROUP), lambda i: (0, g)),
        ),
        [
            pltpu.VMEM((8, length), F32),
            pltpu.VMEM((GROUP, length), F32),
            pltpu.VMEM((GROUP, length), BF16),
            pltpu.VMEM((length, GROUP), BF16),
            pltpu.VMEM((length, 1), F32),
        ],
        held=dict(enumerate(held)),
        passes=passes,
        after=after,
        micros=8,
    )


def hidden_total(fp_ref, d_ref, wq_ref, wk_ref, wv_ref):
    total = fp_ref[...]
    for at, w_ref in enumerate((wq_ref, wk_ref, wv_ref)):
        units = d_ref.shape[2] // UNIT
        order = list(range(0, units, 2)) + list(range(1, units, 2))
        d = lanes(*[d_ref[at, :, u * UNIT : (u + 1) * UNIT] for u in order])
        total = total + mm(d, w_ref[...], NT)
    return total


def hidden_away_kernel(fp_ref, d_ref, wq_ref, wk_ref, wv_ref, out_ref):
    out_ref[...] = hidden_total(fp_ref, d_ref, wq_ref, wk_ref, wv_ref).astype(BF16)


def hidden_home_kernel(
    here_ref, fp_ref, d_ref, wq_ref, wk_ref, wv_ref, came0_ref, came1_ref, out_ref, layer_ref
):
    out_ref[0] = hidden_total(fp_ref, d_ref, wq_ref, wk_ref, wv_ref)
    layer_ref[0] = jnp.where(pl.program_id(0) == 0, came0_ref[...], came1_ref[...])


def hidden_away(fp, dqkv, wq, wk, wv, passes, after):
    length, width = fp.shape
    half = length // 2
    steps = half // TILE
    return run(
        hidden_away_kernel,
        "hidden_away",
        (steps,),
        (fp, dqkv, wq, wk, wv),
        [
            pl.BlockSpec((TILE, width), lambda i: (i + steps, 0)),
            pl.BlockSpec((3, TILE, width), lambda i: (0, i + steps, 0)),
        ]
        + [fixed((width, width))] * 3,
        (jax.ShapeDtypeStruct((half, width), BF16),),
        (pl.BlockSpec((TILE, width), lambda i: (i, 0)),),
        passes=passes,
        after=after,
        micros=3,
    )


def hidden_home(here, fp, dqkv, wq, wk, wv, came0, came1, layer, passes, after):
    length, width = fp.shape
    half = length // 2
    steps = half // TILE
    return run(
        hidden_home_kernel,
        "hidden_home",
        (steps,),
        (here, fp, dqkv, wq, wk, wv, came0, came1),
        [
            pl.BlockSpec((TILE, width), lambda i, b: (i, 0)),
            pl.BlockSpec((3, TILE, width), lambda i, b: (0, i, 0)),
        ]
        + [fixed((width, width))] * 3
        + [fixed((TILE, width))] * 2,
        (
            jax.ShapeDtypeStruct((2, half, width), F32),
            jax.ShapeDtypeStruct((2, half, width), BF16),
        ),
        (
            pl.BlockSpec((1, TILE, width), lambda i, b: (b[0], i, 0)),
            pl.BlockSpec((1, TILE, width), lambda i, b: (1 - b[0], i, 0)),
        ),
        scalars=1,
        held={1: layer},
        passes=passes,
        after=after,
        micros=3,
    )


def place_kernel(here_ref, came_ref, out_ref):
    out_ref[0] = came_ref[...].astype(F32)


def place_far(here, came, grad, passes):
    half, width = came.shape
    return run(
        place_kernel,
        "place_far",
        (2,),
        (here, came),
        [pl.BlockSpec((half // 2, width), lambda i, b: (i, 0))],
        (jax.ShapeDtypeStruct((2, half, width), F32),),
        (pl.BlockSpec((1, half // 2, width), lambda i, b: (1 - b[0], i, 0)),),
        scalars=1,
        held={0: grad},
        passes=passes,
        micros=1,
    )


def fast(
    hidden,
    segments,
    query_matrix,
    query_bias,
    key_matrix,
    value_matrix,
    value_bias,
    output_matrix,
    output_bias,
    first_gain,
    first_shift,
    inner_matrix,
    inner_bias,
    outer_matrix,
    outer_bias,
    second_gain,
    second_shift,
    cotangent,
):
    here = lax.axis_index("blk")
    place = lax.axis_index("seq")
    core, y_at, z_at = place % 2, (place // 2) % 2, place // 4
    here_id = here.astype(jnp.int32)[None]
    core_id = core.astype(jnp.int32)[None]
    half, width = hidden.shape[1:]

    def pick(x, *at):
        start = at + (0,) * (x.ndim - len(at))
        size = (1,) * len(at) + x.shape[len(at) :]
        return lax.dynamic_slice(x, start, size).reshape(x.shape[len(at) :])

    def trade(x):
        return lax.ppermute(x, "blk", [(0, 1), (1, 0)])

    def seq_swap(x, bit):
        return lax.ppermute(x, "seq", [(i, i ^ bit) for i in range(16)])

    def row(x):
        return x.astype(F32)[None, :]

    def rounded(x):
        return lax.reduce_precision(x, 8, 7)

    def sum_0(state, *at):
        return rounded(pick(state[0], *at).astype(F32) + pick(state[1], *at).astype(F32))

    def sum_1(state, mine, *at):
        return rounded(sum_0(state, mine, *at) + pick(state[2], *at).astype(F32))

    def sum_2(state, mine, then, *at):
        return rounded(sum_1(state, mine, then, *at) + pick(state[3], *at).astype(F32))

    def send_z(parts):
        return [seq_swap(x, 4 * d) for d, x in zip((1, 2, 3), parts)]

    def add_z(total, parts):
        return (total + parts[0].astype(F32)) + (parts[1].astype(F32) + parts[2].astype(F32))

    seg = jnp.concatenate([pick(segments, here), trade(pick(segments, 1 - here))])[None, :]
    far = trade(pick(hidden, 1 - here))
    cot_far = trade(pick(cotangent, 1 - here + jnp.minimum(seg[0, -1], 0)))
    q, k, v, ctx, lse, h = attention_forward(
        here_id,
        hidden,
        far,
        query_matrix,
        key_matrix,
        value_matrix,
        row(query_bias),
        row(value_bias),
        seg,
    )
    empty = jnp.zeros((2, width), F32)
    vec = jnp.concatenate(
        [
            row(output_bias),
            row(first_gain),
            row(first_shift),
            row(outer_bias),
            row(second_gain),
            row(second_shift),
            empty,
        ],
        axis=0,
    )
    out, out_far0, out_far1, first, act, og, ig, fp, ag, dctx, sums, isum = token_pass(
        here_id, h, ctx, cotangent, cot_far, output_matrix, inner_matrix, outer_matrix, row(inner_bias), vec
    )
    out_came0, out_came1 = trade(out_far0), trade(out_far1)
    x_mine, x_away, y_mine, y_away = here, 1 - here, y_at, 1 - y_at
    a_keep, a_send = outer_grad_call(core_id, act, og, sums, isum)
    a0 = seq_swap(a_send, 1)
    b_keep, b_send, a_keep = inner_grad_call(core_id, first, ig, ctx, ag, (a_keep,))
    b0 = seq_swap(b_send, 1)
    a = (a_keep, a0)
    a_away = sum_0(a, y_away).astype(BF16)
    a1 = seq_swap(a_away, 2)
    b = (b_keep, b0)
    b_away = sum_0(b, x_away).astype(BF16)
    b1 = trade(b_away)
    bwd = (q, k, v, dctx, ctx, lse, seg)
    held = attention_backward(0, *bwd, (), (), (a_away, b_away))
    *held, a_keep, b_keep = attention_backward(1, *bwd, held, (a_keep, b_keep), ())
    a = (a_keep, a0, a1)
    a_away = sum_1(a, y_mine, x_away).astype(BF16)
    a2 = trade(a_away)
    c_keep, c_send, b_keep, out_came0 = projection_grad_call(
        core_id, h, held[0], sums, 0, 2 * GROUP, False, (b_keep, out_came0), (a_away,)
    )
    c0 = seq_swap(c_send, 1)
    b = (b_keep, b0, b1)
    b_away = sum_1(b, x_mine, y_away).astype(BF16)
    b2 = seq_swap(b_away, 2)
    dqkv, sums2, a_keep, b_keep, c_keep = attention_backward(
        2, *bwd, held, (a_keep, b_keep, c_keep), (c_send, b_away)
    )
    c = (c_keep, c0)
    c_away = sum_0(c, y_away).astype(BF16)
    c1 = seq_swap(c_away, 2)
    d_keep, d_send, a_keep, b_keep, out_came1 = projection_grad_call(
        core_id, h, dqkv, sums2, 2, GROUP, True, (a_keep, b_keep, out_came1), (c_away,)
    )
    d0 = seq_swap(d_send, 1)
    a = (a_keep, a0, a1, a2)
    b = (b_keep, b0, b1, b2)

    def both(z):
        a_part = sum_2(a, y_mine, x_mine, z)
        b_part = sum_2(b, x_mine, y_mine, z)
        return jnp.concatenate([a_part, b_part.reshape(-1, width // 2)], axis=0)

    parts = [both(z_at ^ e).astype(BF16) for e in (1, 2, 3)]
    ab3 = send_z(parts)
    args = (fp, dqkv, query_matrix, key_matrix, value_matrix)
    d = (d_keep, d0)
    d_away = sum_0(d, y_away).astype(BF16)
    d1 = seq_swap(d_away, 2)
    hidden_grad, layer_out, a_keep, b_keep, c_keep, d_keep = hidden_home(
        here_id, *args, out_came0, out_came1, out, (a_keep, b_keep, c_keep, d_keep), (d_away, *parts)
    )
    c = (c_keep, c0, c1)
    d = (d_keep, d0, d1)

    def lanes_of(*parts):
        return jnp.concatenate(parts, axis=-1)

    def late_1(*at):
        return lanes_of(sum_1(c, y_mine, *at), sum_1(d, y_mine, *at))

    e_away = late_1(x_away).astype(BF16)
    e2 = trade(e_away)
    far_grad, a_keep, b_keep, c_keep, d_keep = hidden_away(
        *args, (a_keep, b_keep, c_keep, d_keep), (e_away,)
    )
    came = trade(far_grad)
    c = (c_keep, c0, c1)
    d = (d_keep, d0, d1)
    a = (a_keep, a0, a1, a2)
    b = (b_keep, b0, b1, b2)

    def late_2(z):
        return rounded(late_1(x_mine, z) + pick(e2, z).astype(F32))

    e3 = send_z([late_2(z_at ^ e).astype(BF16) for e in (1, 2, 3)])
    early = add_z(both(z_at), ab3)
    hidden_grad = place_far(here_id, came, hidden_grad, ())[0]
    late = add_z(late_2(z_at), e3)
    rows = width // 16
    outer_rows = 4 * rows
    outer_grad = early[:outer_rows]
    vectors = early[outer_rows : outer_rows + VECTOR_ROWS].reshape(-1, width)
    inner_all = early[outer_rows + VECTOR_ROWS :].reshape(5, rows, width // 2)
    output_grad = inner_all[4]
    inner_grad = jnp.transpose(inner_all[:4], (1, 0, 2)).reshape(rows, -1)
    units = width // UNIT
    biases = late[3 * rows :, 2 * UNIT :][: 2 * units].reshape(2, units // 2, 2, UNIT)
    biases = jnp.transpose(biases, (0, 2, 1, 3)).reshape(2, width)
    return (
        layer_out,
        hidden_grad,
        late[:rows],
        biases[0],
        late[rows : 2 * rows],
        late[2 * rows : 3 * rows],
        biases[1],
        output_grad,
        vectors[5],
        vectors[3],
        vectors[4],
        inner_grad,
        vectors[6:10].reshape(-1),
        outer_grad,
        vectors[2],
        vectors[0],
        vectors[1],
    )


def choose(sizes, *args):
    seq_count, row_count, width = args[0].shape
    whole_here = sizes[1] == 2 and seq_count == 2 and row_count == 2 * TILE and width == 3 * GROUP
    return fast(*args) if whole_here and sizes[0] == 16 else general(*args)


def solution(mesh):
    sizes = (mesh.shape["seq"], mesh.shape["blk"])
    return jax.shard_map(
        functools.partial(choose, sizes),
        mesh=mesh,
        in_specs=(
            P("seq", "blk", None),
            P("seq", "blk"),
            P(),
            P(),
            P(),
            P(),
            P(),
            P(),
            P(),
            P(),
            P(),
            P(),
            P(),
            P(),
            P(),
            P(),
            P(),
            P("seq", "blk", None),
        ),
        out_specs=(
            P("seq", "blk", None),
            P("seq", "blk", None),
            P("seq", "blk"),
            P(),
            P("seq", "blk"),
            P("seq", "blk"),
            P(),
            P("seq", "blk"),
            P(),
            P(),
            P(),
            P("seq", "blk"),
            P(),
            P("seq", "blk"),
            P(),
            P(),
            P(),
        ),
        check_vma=False,
    )
```

```python
import functools
import math

import jax
import jax.numpy as jnp
from jax import lax
from jax.experimental import pallas as pl
from jax.experimental.pallas import tpu as pltpu
from jax.sharding import PartitionSpec as P

HEADS = 12
HEAD = 64


NEGATIVE = -1e30
EPSILON = 1e-12


def layer_norm(values, norm_gain, norm_shift):
    centre = values - jnp.mean(values, axis=-1, keepdims=True)
    spread = jnp.mean(centre * centre, axis=-1, keepdims=True)
    return centre * lax.rsqrt(spread + EPSILON) * norm_gain + norm_shift


def gelu_exact(values):
    return jax.nn.gelu(values, approximate=False)


def linear(operand, matrix):
    return jnp.dot(operand, matrix, preferred_element_type=jnp.float32)


def split_heads(values):
    return values.reshape(values.shape[0], values.shape[1], HEADS, HEAD)


def block_scores(query_block, key_block, score_scale):
    return (
        jnp.einsum("sqhd,skhd->shqk", query_block, key_block, preferred_element_type=jnp.float32)
        * score_scale
    )


def attention_grads(
    query_block, key_block, value_block, dctx_block, same_doc, log_total, row_delta, score_scale
):
    attn_probs = jnp.where(
        same_doc,
        jnp.exp(block_scores(query_block, key_block, score_scale) - log_total[..., None]),
        0.0,
    )
    slopes = jnp.einsum(
        "sqhd,skhd->shqk", dctx_block, value_block, preferred_element_type=jnp.float32
    )
    return (attn_probs, (attn_probs * (slopes - row_delta[..., None])).astype(jnp.bfloat16))


def over_blocks(length, step, initial):
    block_size = math.gcd(length, 512)

    def scan_step(carried, block_index):
        return (step(carried, block_index * block_size, block_size), None)

    result, unused = lax.scan(scan_step, initial, jnp.arange(length // block_size, dtype=jnp.int32))
    return result


def general(
    hidden,
    segments,
    query_matrix,
    query_bias,
    key_matrix,
    value_matrix,
    value_bias,
    output_matrix,
    output_bias,
    first_gain,
    first_shift,
    inner_matrix,
    inner_bias,
    outer_matrix,
    outer_bias,
    second_gain,
    second_shift,
    cotangent,
):
    seq_count, row_count, model_width = hidden.shape
    score_scale = HEAD ** (-0.5)
    single_float = jnp.float32
    bf16 = jnp.bfloat16
    queries = (linear(hidden, query_matrix) + query_bias.astype(single_float)).astype(bf16)
    key_proj = linear(hidden, key_matrix).astype(bf16)
    value_proj = (linear(hidden, value_matrix) + value_bias.astype(single_float)).astype(bf16)
    seg_all = lax.all_gather(segments, "blk", axis=1, tiled=True)
    keys_all, values_all = (
        lax.all_gather(key_proj, "blk", axis=1, tiled=True),
        lax.all_gather(value_proj, "blk", axis=1, tiled=True),
    )
    length = seg_all.shape[1]
    query_heads = split_heads(queries)
    key_heads = split_heads(keys_all)
    value_heads = split_heads(values_all)

    def key_slices(offset, block_size):
        key_segs = lax.dynamic_slice_in_dim(seg_all, offset, block_size, 1)
        same_doc = (segments[:, :, None] == key_segs[:, None, :])[:, None]
        key_block = lax.dynamic_slice_in_dim(key_heads, offset, block_size, 1)
        value_block = lax.dynamic_slice_in_dim(value_heads, offset, block_size, 1)
        return (same_doc, key_block, value_block)

    def stats_step(carried, offset, block_size):
        same_doc, key_block, value_block = key_slices(offset, block_size)
        running_max, running_sum = carried
        scores = jnp.where(same_doc, block_scores(query_heads, key_block, score_scale), NEGATIVE)
        higher = jnp.maximum(running_max, jnp.max(scores, axis=-1))
        weights = jnp.where(same_doc, jnp.exp(scores - higher[..., None]), 0.0)
        return (higher, running_sum * jnp.exp(running_max - higher) + jnp.sum(weights, axis=-1))

    stat_shape = (seq_count, HEADS, row_count)
    running_max, running_sum = over_blocks(
        length,
        stats_step,
        (jnp.full(stat_shape, NEGATIVE, single_float), jnp.zeros(stat_shape, single_float)),
    )
    log_total = running_max + jnp.log(running_sum)

    def context_step(carried, offset, block_size):
        same_doc, key_block, value_block = key_slices(offset, block_size)
        attn_probs = jnp.where(
            same_doc,
            jnp.exp(block_scores(query_heads, key_block, score_scale) - log_total[..., None]),
            0.0,
        )
        return carried + jnp.einsum(
            "shqk,skhd->sqhd",
            attn_probs.astype(bf16),
            value_block,
            preferred_element_type=single_float,
        )

    head_zeros = jnp.zeros((seq_count, row_count, HEADS, HEAD), single_float)
    context = over_blocks(length, context_step, head_zeros)
    context_reduced = context.reshape(seq_count, row_count, model_width).astype(bf16)
    attn_out = linear(context_reduced, output_matrix) + output_bias.astype(single_float)
    first_pre = hidden.astype(single_float) + attn_out
    first_norm, first_back = jax.vjp(
        layer_norm, first_pre, first_gain.astype(single_float), first_shift.astype(single_float)
    )
    first_reduced = first_norm.astype(bf16)
    inner = linear(first_reduced, inner_matrix) + inner_bias.astype(single_float)
    act_full, gelu_back = jax.vjp(gelu_exact, inner)
    activation_reduced = act_full.astype(bf16)
    outer = linear(activation_reduced, outer_matrix) + outer_bias.astype(single_float)
    layer_full, second_back = jax.vjp(
        layer_norm,
        first_norm + outer,
        second_gain.astype(single_float),
        second_shift.astype(single_float),
    )
    layer_out = layer_full.astype(bf16)
    second_pre_grad, second_gain_grad, second_shift_grad = second_back(
        cotangent.astype(single_float)
    )
    outer_gradient_reduced = second_pre_grad.astype(bf16)
    outer_weight_grad = jnp.einsum(
        "gvx,gvm->xm",
        activation_reduced,
        outer_gradient_reduced,
        preferred_element_type=single_float,
    )
    outer_bias_grad = jnp.sum(outer_gradient_reduced.astype(single_float), axis=(0, 1))
    activation_gradient = jnp.einsum(
        "rzo,uo->rzu", outer_gradient_reduced, outer_matrix, preferred_element_type=single_float
    )
    inner_gradient_reduced = gelu_back(activation_gradient)[0].astype(bf16)
    inner_weight_grad = jnp.einsum(
        "ret,reu->tu", first_reduced, inner_gradient_reduced, preferred_element_type=single_float
    )
    inner_bias_grad = jnp.sum(inner_gradient_reduced.astype(single_float), axis=(0, 1))
    first_norm_grad = second_pre_grad + jnp.einsum(
        "aoi,ni->aon", inner_gradient_reduced, inner_matrix, preferred_element_type=single_float
    )
    first_pre_grad, first_gain_grad, first_shift_grad = first_back(first_norm_grad)
    attention_gradient_reduced = first_pre_grad.astype(bf16)
    output_weight_grad = jnp.einsum(
        "tfm,tfc->mc",
        context_reduced,
        attention_gradient_reduced,
        preferred_element_type=single_float,
    )
    output_bias_grad = jnp.sum(attention_gradient_reduced.astype(single_float), axis=(0, 1))
    dctx_low = jnp.einsum(
        "upx,cx->upc",
        attention_gradient_reduced,
        output_matrix,
        preferred_element_type=single_float,
    ).astype(bf16)
    dctx_heads = split_heads(dctx_low)
    row_delta = jnp.transpose(
        jnp.sum(dctx_heads.astype(single_float) * context, axis=-1), (0, 2, 1)
    )

    def query_step(carried, offset, block_size):
        same_doc, key_block, value_block = key_slices(offset, block_size)
        attn_probs, dscores = attention_grads(
            query_heads,
            key_block,
            value_block,
            dctx_heads,
            same_doc,
            log_total,
            row_delta,
            score_scale,
        )
        return carried + score_scale * jnp.einsum(
            "shqk,skhd->sqhd", dscores, key_block, preferred_element_type=single_float
        )

    query_grad = over_blocks(length, query_step, head_zeros)
    query_all, dctx_all = (
        lax.all_gather(queries, "blk", axis=1, tiled=True),
        lax.all_gather(dctx_low, "blk", axis=1, tiled=True),
    )
    lse_all, delta_all = (
        lax.all_gather(log_total, "blk", axis=2, tiled=True),
        lax.all_gather(row_delta, "blk", axis=2, tiled=True),
    )
    query_all_heads = split_heads(query_all)
    dctx_all_heads = split_heads(dctx_all)
    own_keys = split_heads(key_proj)
    own_values = split_heads(value_proj)

    def key_step(carried, offset, block_size):
        query_segs = lax.dynamic_slice_in_dim(seg_all, offset, block_size, 1)
        same_doc = (query_segs[:, :, None] == segments[:, None, :])[:, None]
        query_block = lax.dynamic_slice_in_dim(query_all_heads, offset, block_size, 1)
        dctx_block = lax.dynamic_slice_in_dim(dctx_all_heads, offset, block_size, 1)
        lse_block = lax.dynamic_slice_in_dim(lse_all, offset, block_size, 2)
        delta_block = lax.dynamic_slice_in_dim(delta_all, offset, block_size, 2)
        key_sum, value_sum = carried
        attn_probs, dscores = attention_grads(
            query_block,
            own_keys,
            own_values,
            dctx_block,
            same_doc,
            lse_block,
            delta_block,
            score_scale,
        )
        key_sum = key_sum + score_scale * jnp.einsum(
            "shqk,sqhd->skhd", dscores, query_block, preferred_element_type=single_float
        )
        value_sum = value_sum + jnp.einsum(
            "shqk,sqhd->skhd",
            attn_probs.astype(bf16),
            dctx_block,
            preferred_element_type=single_float,
        )
        return (key_sum, value_sum)

    key_grad, value_grad = over_blocks(length, key_step, (head_zeros, head_zeros))
    query_gradient_reduced = query_grad.reshape(seq_count, row_count, model_width).astype(bf16)
    key_gradient_reduced = key_grad.reshape(seq_count, row_count, model_width).astype(bf16)
    value_gradient_reduced = value_grad.reshape(seq_count, row_count, model_width).astype(bf16)
    query_weight_grad = jnp.einsum(
        "tfm,tfc->mc", hidden, query_gradient_reduced, preferred_element_type=single_float
    )
    query_bias_grad = jnp.sum(query_gradient_reduced.astype(single_float), axis=(0, 1))
    key_matrix_gradient = jnp.einsum(
        "tfm,tfc->mc", hidden, key_gradient_reduced, preferred_element_type=single_float
    )
    value_weight_grad = jnp.einsum(
        "tfm,tfc->mc", hidden, value_gradient_reduced, preferred_element_type=single_float
    )
    value_bias_grad = jnp.sum(value_gradient_reduced.astype(single_float), axis=(0, 1))
    hidden_grad = first_pre_grad + jnp.einsum(
        "upx,cx->upc", query_gradient_reduced, query_matrix, preferred_element_type=single_float
    )
    hidden_grad = hidden_grad + jnp.einsum(
        "upx,cx->upc", key_gradient_reduced, key_matrix, preferred_element_type=single_float
    )
    hidden_grad = hidden_grad + jnp.einsum(
        "upx,cx->upc", value_gradient_reduced, value_matrix, preferred_element_type=single_float
    )
    partial_sums = (
        lax.psum_scatter(query_weight_grad, "seq", scatter_dimension=0, tiled=True),
        lax.psum_scatter(key_matrix_gradient, "seq", scatter_dimension=0, tiled=True),
        lax.psum_scatter(value_weight_grad, "seq", scatter_dimension=0, tiled=True),
        lax.psum_scatter(output_weight_grad, "seq", scatter_dimension=0, tiled=True),
        lax.psum_scatter(inner_weight_grad, "seq", scatter_dimension=0, tiled=True),
        lax.psum_scatter(outer_weight_grad, "seq", scatter_dimension=0, tiled=True),
    )
    matrices = lax.psum_scatter(tuple(partial_sums), "blk", scatter_dimension=1, tiled=True)
    vectors = lax.psum(
        (
            query_bias_grad,
            value_bias_grad,
            output_bias_grad,
            first_gain_grad,
            first_shift_grad,
            inner_bias_grad,
            outer_bias_grad,
            second_gain_grad,
            second_shift_grad,
        ),
        ("seq", "blk"),
    )
    return (
        layer_out,
        hidden_grad,
        matrices[0],
        vectors[0],
        matrices[1],
        matrices[2],
        vectors[1],
        matrices[3],
        vectors[2],
        vectors[3],
        vectors[4],
        matrices[4],
        vectors[5],
        matrices[5],
        vectors[6],
        vectors[7],
        vectors[8],
    )


BF16 = jnp.bfloat16
F32 = jnp.float32
NN = ((1,), (0,))
NT = ((1,), (1,))
TN = ((0,), (0,))
UNIT = 128
GROUP = 256
PER_GROUP = GROUP // HEAD
TILE = 256
TOKENS = 512
VMEM_LIMIT = 60 * 2**20
SCALAR = pl.BlockSpec(memory_space=pltpu.SMEM)
ANY = pl.BlockSpec(memory_space=pl.ANY)


def mm(a, b, dims):
    return lax.dot_general(a, b, (dims, ((), ())), preferred_element_type=F32)


def fixed(shape):
    return pl.BlockSpec(shape, lambda *_: (0,) * len(shape), pipeline_mode=pl.Buffered(1))


def run(
    kernel,
    name,
    grid,
    operands,
    in_specs,
    out_shape,
    out_specs,
    scratch=(),
    scalars=0,
    held=None,
    passes=(),
    after=(),
    micros=1,
):
    held = held or {}
    out_shape, out_specs = list(out_shape), list(out_specs)
    n_in, n_out, n_held, n_pass = len(operands), len(out_shape), len(held), len(passes)
    aliases = {n_in + i: at for i, at in enumerate(held)}
    aliases |= {n_in + n_held + i: n_out + i for i in range(n_pass)}

    def body(*refs):
        outs = n_in + n_held + n_pass + len(after)
        kernel(*refs[:n_in], *refs[outs : outs + n_out], *refs[outs + n_out + n_pass :])

    result = pl.pallas_call(
        body,
        grid_spec=pltpu.PrefetchScalarGridSpec(
            num_scalar_prefetch=scalars,
            grid=grid,
            in_specs=list(in_specs) + [ANY] * (n_held + n_pass + len(after)),
            out_specs=out_specs + [ANY] * n_pass,
            scratch_shapes=list(scratch),
        ),
        out_shape=out_shape + [jax.ShapeDtypeStruct(x.shape, x.dtype) for x in passes],
        input_output_aliases=aliases,
        compiler_params=pltpu.CompilerParams(
            vmem_limit_bytes=VMEM_LIMIT, dimension_semantics=("arbitrary",) * len(grid)
        ),
        cost_estimate=pl.CostEstimate(
            flops=int(micros * 1e10), bytes_accessed=1, transcendentals=0
        ),
        name=name,
    )(*operands, *held.values(), *passes, *after)
    return result


def head_lanes(shape, head):
    lane = lax.broadcasted_iota(jnp.int32, shape, 1)
    return (lane >= head * HEAD) & (lane < (head + 1) * HEAD)


def lanes(*parts):
    return jnp.concatenate(parts, axis=1)


def column_of(row):
    return jnp.transpose(jnp.broadcast_to(row.astype(F32), (UNIT, row.shape[1])))[:, 0:1]


def same_pair(row, column, rows):
    return jnp.where(column[rows] == row, 0.0, NEGATIVE)


def attention_forward_kernel(
    here_ref,
    own_ref,
    far_ref,
    wq0_ref,
    wq1_ref,
    wk0_ref,
    wk1_ref,
    wv0_ref,
    wv1_ref,
    bq0_ref,
    bq1_ref,
    bv0_ref,
    bv1_ref,
    seg_ref,
    q_ref,
    k_ref,
    v_ref,
    ctx_ref,
    lse_ref,
    h_ref,
    mask_ref,
    vaug_ref,
):
    half = far_ref.shape[0]
    length = 2 * half

    @pl.when(pl.program_id(0) == 0)
    def _():
        segr = seg_ref[...].astype(F32)
        mask_ref[...] = jnp.where(column_of(segr) == segr, 0.0, NEGATIVE)
        h_ref[0:half, :] = own_ref[0]
        h_ref[half:, :] = far_ref[...]

    h = h_ref[...]
    bias_q = lanes(bq0_ref[...], bq1_ref[...])
    bias_v = lanes(bv0_ref[...], bv1_ref[...])
    q_ref[...] = (mm(h, lanes(wq0_ref[...], wq1_ref[...]), NN) + bias_q).astype(BF16)
    k_ref[...] = mm(h, lanes(wk0_ref[...], wk1_ref[...]), NN).astype(BF16)
    v = (mm(h, lanes(wv0_ref[...], wv1_ref[...]), NN) + bias_v).astype(BF16)
    v_ref[...] = v
    lane = lax.broadcasted_iota(jnp.int32, v.shape, 1)
    for head in range(PER_GROUP):
        other = (lane // UNIT) != (head // 2)
        filler = jnp.where(other, 1.0, 0.0).astype(BF16)
        vaug_ref[head] = jnp.where(head_lanes(v.shape, head), v, filler)

    def block(i, carry):
        rows = pl.ds(pl.multiple_of(i * TILE, TILE), TILE)
        qb = q_ref[rows, :] * BF16(HEAD**-0.5)
        halves = [None, None]
        stat_lane = lax.broadcasted_iota(jnp.int32, (TILE, UNIT), 1)
        stats = jnp.zeros((TILE, UNIT), F32)
        for head in range(PER_GROUP):
            qm = jnp.where(head_lanes(qb.shape, head), qb, BF16(0))
            s = mm(qm, k_ref[...], NT) + mask_ref[rows, :]
            top = jnp.max(s, axis=1, keepdims=True)
            e = jnp.exp(s - top).astype(BF16)
            o = mm(e, vaug_ref[head], NN)
            t = head // 2
            total = o[:, (1 - t) * UNIT : (2 - t) * UNIT]
            part = o[:, t * UNIT : (t + 1) * UNIT] / total
            halves[t] = part if halves[t] is None else halves[t] + part
            stats = jnp.where(stat_lane == head, top + jnp.log(total), stats)
        ctx_ref[0, rows, :] = halves[0].astype(BF16)
        ctx_ref[1, rows, :] = halves[1].astype(BF16)
        lse_ref[:, rows] = jnp.transpose(stats)[0:8]
        return carry

    lax.fori_loop(0, length // TILE, block, 0, unroll=True)


def attention_forward(here, hidden, far, wq, wk, wv, bq, bv, seg):
    half, width = far.shape
    length = 2 * half
    groups = width // GROUP
    left = pl.BlockSpec((width, UNIT), lambda g, h: (0, g))
    right = pl.BlockSpec((width, UNIT), lambda g, h: (0, groups + g))
    bias_left = pl.BlockSpec((1, UNIT), lambda g, h: (0, g))
    bias_right = pl.BlockSpec((1, UNIT), lambda g, h: (0, groups + g))
    rows = pl.BlockSpec((length, GROUP), lambda g, h: (0, g))
    wide = jax.ShapeDtypeStruct((length, width), BF16)
    own = pl.BlockSpec((1, half, width), lambda g, h: (h[0], 0, 0), pipeline_mode=pl.Buffered(1))
    return run(
        attention_forward_kernel,
        "attention_forward",
        (groups,),
        (here, hidden, far, wq, wq, wk, wk, wv, wv, bq, bq, bv, bv, seg),
        [own, fixed((half, width))]
        + [left, right] * 3
        + [bias_left, bias_right] * 2
        + [fixed((1, length))],
        (
            wide,
            wide,
            wide,
            jax.ShapeDtypeStruct((2, length, width // 2), BF16),
            jax.ShapeDtypeStruct((8 * groups, length), F32),
            wide,
        ),
        (
            rows,
            rows,
            rows,
            pl.BlockSpec((2, length, UNIT), lambda g, h: (0, 0, g)),
            pl.BlockSpec((8, length), lambda g, h: (g, 0)),
            pl.BlockSpec((length, width), lambda g, h: (0, 0)),
        ),
        [pltpu.VMEM((length, length), F32), pltpu.VMEM((PER_GROUP, length, GROUP), BF16)],
        scalars=1,
        micros=16,
    )


def gelu_pair(u):
    phi = 0.5 + 0.5 * lax.erf(u * 0.7071067811865476)
    bell = jnp.exp2(u * u * -0.7213475204444817)
    return (u * phi, phi + u * bell * 0.3989422804014327)


def normed(x):
    centre = x - jnp.mean(x, axis=1, keepdims=True)
    scale = lax.rsqrt(jnp.mean(centre * centre, axis=1, keepdims=True) + EPSILON)
    return (centre * scale, scale)


def norm_back(u, n, scale):
    return scale * (u - jnp.mean(u, axis=1, keepdims=True) - n * jnp.mean(u * n, axis=1, keepdims=True))


def row_sum(x):
    return jnp.sum(x, axis=0, keepdims=True)


def token_kernel(
    here_ref,
    h_ref,
    ctx_ref,
    cot_own_ref,
    cot_far_ref,
    wo_ref,
    wi_ref,
    wp_ref,
    bi_ref,
    vec_ref,
    out_ref,
    far0_ref,
    far1_ref,
    first_ref,
    act_ref,
    og_ref,
    ig_ref,
    fp_ref,
    ag_ref,
    dctx_ref,
    sums_ref,
    isum_ref,
    slope_ref,
):
    step = pl.program_id(0)
    steps = pl.num_programs(0)

    @pl.when(step == 0)
    def _():
        sums_ref[...] = jnp.zeros_like(sums_ref)
        isum_ref[...] = jnp.zeros_like(isum_ref)

    ff = wi_ref.shape[1]
    chunk = 512
    output_bias, gain1, shift1 = vec_ref[0:1, :], vec_ref[1:2, :], vec_ref[2:3, :]
    outer_bias, gain2, shift2 = vec_ref[3:4, :], vec_ref[4:5, :], vec_ref[5:6, :]
    middle = wo_ref.shape[0] // 2
    near = step < steps // 2

    def part(rows):
        ctx = lanes(ctx_ref[0, rows, :], ctx_ref[1, rows, :])
        x = h_ref[rows, :].astype(F32) + mm(ctx, wo_ref[...], NN) + output_bias
        yield
        n1, r1 = normed(x)
        fn = n1 * gain1 + shift1
        first = fn.astype(BF16)
        first_ref[rows, :] = first
        yield
        for c in range(0, ff, chunk):
            act, slope = gelu_pair(mm(first, wi_ref[:, c : c + chunk], NN) + bi_ref[:, c : c + chunk])
            act_ref[rows, c : c + chunk] = act.astype(BF16)
            slope_ref[rows, c : c + chunk] = slope
            yield
        x = fn + mm(act_ref[rows, :], wp_ref[...], NN) + outer_bias
        yield
        n2, r2 = normed(x)
        out = (n2 * gain2 + shift2).astype(BF16)

        @pl.when(near)
        def _():
            out_ref[0, rows, :] = out

        @pl.when(jnp.logical_not(near))
        def _():
            (far1_ref if rows.start else far0_ref)[...] = out

        e = jnp.where(near, cot_own_ref[0, rows, :], cot_far_ref[rows, :]).astype(F32)
        sums_ref[0:1, :] += row_sum(e * n2)
        sums_ref[1:2, :] += row_sum(e)
        sp = norm_back(e * gain2, n2, r2)
        og = sp.astype(BF16)
        og_ref[rows, :] = og
        sums_ref[2:3, :] += row_sum(og.astype(F32))
        yield
        for c in range(0, ff, chunk):
            ig = (mm(og, wp_ref[c : c + chunk, :], NT) * slope_ref[rows, c : c + chunk]).astype(BF16)
            ig_ref[rows, c : c + chunk] = ig
            isum_ref[:, c : c + chunk] += row_sum(ig.astype(F32))
            yield
        d = sp + mm(ig_ref[rows, :], wi_ref[...], NT)
        yield
        sums_ref[3:4, :] += row_sum(d * n1)
        sums_ref[4:5, :] += row_sum(d)
        fp = norm_back(d * gain1, n1, r1)
        fp_ref[rows, :] = fp
        ag = fp.astype(BF16)
        ag_ref[rows, :] = ag
        sums_ref[5:6, :] += row_sum(ag.astype(F32))
        yield
        dctx = mm(ag, wo_ref[...], NT).astype(BF16)
        dctx_ref[0, rows, :] = dctx[:, :middle]
        dctx_ref[1, rows, :] = dctx[:, middle:]

    size = h_ref.shape[0]
    parts = [part(slice(r, r + TILE)) for r in range(0, size, TILE)]
    live, waiting = [], list(parts)
    while waiting or live:
        if waiting:
            live.append(waiting.pop(0))
        live = [p for p in live if next(p, 0) is None]


def token_pass(here, h, ctx, cot, cot_far, wo, wi, wp, bi, vec):
    length, width = h.shape
    half = length // 2
    ff = wi.shape[1]
    steps = length // TOKENS
    near = steps // 2
    rows = pl.BlockSpec((TOKENS, width), lambda i, b: (i, 0))
    split_rows = pl.BlockSpec((2, TOKENS, width // 2), lambda i, b: (0, i, 0))
    wide_rows = pl.BlockSpec((TOKENS, ff), lambda i, b: (i, 0))
    own_rows = pl.BlockSpec((1, TOKENS, width), lambda i, b: (b[0], jnp.minimum(i, near - 1), 0))
    far_rows = pl.BlockSpec((TOKENS, width), lambda i, b: (jnp.maximum(i - near, 0), 0))
    low = jax.ShapeDtypeStruct((length, width), BF16)
    low_ff = jax.ShapeDtypeStruct((length, ff), BF16)
    return run(
        token_kernel,
        "token_pass",
        (steps,),
        (here, h, ctx, cot, cot_far, wo, wi, wp, bi, vec),
        [
            rows,
            split_rows,
            own_rows,
            far_rows,
            fixed((width, width)),
            fixed((width, ff)),
            fixed((ff, width)),
            fixed((1, ff)),
            fixed((8, width)),
        ],
        (
            jax.ShapeDtypeStruct((2, half, width), BF16),
            jax.ShapeDtypeStruct((half // 2, width), BF16),
            jax.ShapeDtypeStruct((half // 2, width), BF16),
            low,
            low_ff,
            low,
            low_ff,
            jax.ShapeDtypeStruct((length, width), F32),
            low,
            jax.ShapeDtypeStruct((2, length, width // 2), BF16),
            jax.ShapeDtypeStruct((8, width), F32),
            jax.ShapeDtypeStruct((1, ff), F32),
        ),
        (
            own_rows,
            pl.BlockSpec((half // 2, width), lambda i, b: (0, 0)),
            pl.BlockSpec((half // 2, width), lambda i, b: (0, 0)),
            rows,
            wide_rows,
            rows,
            wide_rows,
            rows,
            rows,
            split_rows,
            pl.BlockSpec((8, width), lambda i, b: (0, 0)),
            pl.BlockSpec((1, ff), lambda i, b: (0, 0)),
        ),
        [pltpu.VMEM((TOKENS, ff), F32)],
        scalars=1,
        micros=23,
    )


def put_pairs(res, core_ref, keep_ref, send_ref, columns, rows, count):
    even = core_ref[0] == 0
    for z in range(count):
        for y in range(2):
            base = (z * 2 + y) * 2 * rows
            for x in range(2):
                zero = lanes(*[res[base : base + rows, c] for c in columns[x]])
                one = lanes(*[res[base + rows : base + 2 * rows, c] for c in columns[x]])
                keep_ref[x, y, z, 0] = jnp.where(even, zero, one).astype(BF16)
                send_ref[x, y, z, 0] = jnp.where(even, one, zero).astype(BF16)


HALVES = ((slice(0, 384),), (slice(384, 768),))
VECTOR_ROWS = 32
BIAS_ROWS = 16


def outer_grad_kernel(core_ref, act_ref, og_ref, sums_ref, isum_ref, keep_ref, send_ref, rows_ref):
    res = mm(act_ref[...], og_ref[...], TN)
    middle = res.shape[1] // 2
    rows = res.shape[0] // 4
    even = core_ref[0] == 0
    rows_ref[...] = jnp.zeros_like(rows_ref)
    at = 0
    for r in range(6):
        for x in range(2):
            rows_ref[at : at + 1, :] = sums_ref[r : r + 1, x * middle : (x + 1) * middle]
            at += 1
    for r in range(isum_ref.shape[1] // middle):
        rows_ref[at : at + 1, :] = isum_ref[:, r * middle : (r + 1) * middle]
        at += 1
    extra = rows_ref[...].astype(BF16)
    for y in range(2):
        for x in range(2):
            columns = slice(x * middle, (x + 1) * middle)
            zero = res[2 * y * rows : (2 * y + 1) * rows, columns]
            one = res[(2 * y + 1) * rows : (2 * y + 2) * rows, columns]
            keep_ref[y, x, 0, 0:rows, :] = jnp.where(even, zero, one).astype(BF16)
            send_ref[y, x, 0, 0:rows, :] = jnp.where(even, one, zero).astype(BF16)
            keep_ref[y, x, 0, rows:, :] = extra
            send_ref[y, x, 0, rows:, :] = extra


def pair_out(shape, block, index):
    kind = jax.ShapeDtypeStruct(shape, BF16)
    spec = pl.BlockSpec(block, index)
    return ((kind, kind), (spec, spec))


def outer_grad_call(core, act, og, sums, isum):
    length, ff = act.shape
    width = og.shape[1]
    shape = (2, 2, 4, ff // 16 + VECTOR_ROWS, width // 2)
    kinds, specs = pair_out(shape, (2, 2, 1) + shape[3:], lambda z: (0, 0, z, 0, 0))
    return run(
        outer_grad_kernel,
        "outer_grad",
        (4,),
        (core, act, og, sums, isum),
        [
            SCALAR,
            pl.BlockSpec((length, ff // 4), lambda z: (0, z)),
            fixed((length, width)),
            fixed(sums.shape),
            fixed(isum.shape),
        ],
        kinds,
        specs,
        [pltpu.VMEM((VECTOR_ROWS, width // 2), F32)],
        micros=4.5,
    )


def inner_grad_kernel(
    core_ref, first_ref, low_ref, high_ref, ctx_ref, ag_ref, keep_ref, send_ref
):
    step = pl.program_id(0)
    rows = keep_ref.shape[4]

    @pl.when(step < 4)
    def _():
        res = mm(first_ref[...], lanes(low_ref[...], high_ref[...]), TN)
        put_pairs(res, core_ref, keep_ref, send_ref, HALVES, rows, 4)

    @pl.when(step == 4)
    def _():
        res = mm(lanes(ctx_ref[0], ctx_ref[1]), ag_ref[...], TN)
        put_pairs(res, core_ref, keep_ref, send_ref, HALVES, rows, 4)


def inner_grad_call(core, first, ig, ctx, ag, passes):
    length, width = first.shape
    shape = (2, 2, 4, 5, width // 16, width // 2)
    kinds, specs = pair_out(shape, shape[:3] + (1,) + shape[4:], lambda s: (0, 0, 0, s, 0, 0))
    return run(
        inner_grad_kernel,
        "inner_grad",
        (5,),
        (core, first, ig, ig, ctx, ag),
        [
            SCALAR,
            fixed((length, width)),
            pl.BlockSpec((length, width // 2), lambda s: (0, jnp.minimum(s, 3))),
            pl.BlockSpec((length, width // 2), lambda s: (0, 4 + jnp.minimum(s, 3))),
            fixed((2, length, width // 2)),
            fixed((length, width)),
        ],
        kinds,
        specs,
        passes=passes,
        micros=6,
    )


def rounded(x):
    return x.astype(BF16).astype(F32)


def sum_second(keep, came, came1):
    total = rounded(keep.astype(F32) + came.astype(F32))
    return rounded(total + came1.astype(F32))


def quarter_kernel(plan, at_ref, *refs):
    outs = refs[-4:]
    here = at_ref[2]
    for d in range(4):
        z = lax.bitwise_xor(here, d)
        for first, count, row, column, through in plan:
            keep_ref, came_ref, came1_ref = refs[first : first + 3]
            came2_ref = refs[through]
            rows, part = keep_ref.shape[3:]
            total = sum_second(keep_ref[0, 0, z], came_ref[0, 0, z], came1_ref[0, z])
            came2 = came2_ref[z, :, column : column + part]
            outs[d][row : row + rows, column : column + part] = rounded(
                total + came2.astype(F32)
            ).astype(BF16)


def quarter(at, states, total_rows, total_width, passes, after):
    specs, operands, plan, seen = [], [], [], {}
    for keep, came, came1, came2, axis, row, column in states:
        _, _, depth, rows, part = keep.shape
        if axis == 0:
            both = pl.BlockSpec((1, 1, depth, rows, part), lambda i, s: (s[0], s[1], 0, 0, 0))
            one = pl.BlockSpec((1, depth, rows, part), lambda i, s: (s[1], 0, 0, 0))
        else:
            both = pl.BlockSpec((1, 1, depth, rows, part), lambda i, s: (s[1], s[0], 0, 0, 0))
            one = pl.BlockSpec((1, depth, rows, part), lambda i, s: (s[0], 0, 0, 0))
        first = len(operands)
        specs += [both, both, one]
        operands += [keep, came, came1]
        if id(came2) not in seen:
            seen[id(came2)] = len(operands)
            specs.append(fixed(came2.shape))
            operands.append(came2)
        plan.append((first, 3, row, column, seen[id(came2)]))
    part = jax.ShapeDtypeStruct((total_rows, total_width), BF16)
    return run(
        functools.partial(quarter_kernel, plan),
        "quarter",
        (1,),
        (at, *operands),
        specs,
        (part,) * 4,
        (pl.BlockSpec((total_rows, total_width), lambda i, s: (0, 0)),) * 4,
        scalars=1,
        passes=passes,
        after=after,
    )


def projection_part(core_ref, h_ref, grads, sums, keep_ref, send_ref):
    rows = h_ref.shape[1] // 16
    even = core_ref[0] == 0
    for s in range(3):
        place = slice(s * rows, (s + 1) * rows)
        parts = [mm(h_ref[...], ref[s], TN) for ref in grads]
        for z in range(4):
            for y in range(2):
                base = (z * 2 + y) * 2 * rows
                for x in range(2):
                    unit = slice(x * UNIT, (x + 1) * UNIT)
                    zero = lanes(*[p[base : base + rows, unit] for p in parts])
                    one = lanes(*[p[base + rows : base + 2 * rows, unit] for p in parts])
                    keep_ref[y, x, z, place, :] = jnp.where(even, zero, one).astype(BF16)
                    send_ref[y, x, z, place, :] = jnp.where(even, one, zero).astype(BF16)
    extra = jnp.zeros((BIAS_ROWS, keep_ref.shape[4]), F32)
    at = lax.broadcasted_iota(jnp.int32, extra.shape, 0)
    for r in range(2):
        for g, ref in enumerate(sums):
            for x in range(2):
                part = ref[r : r + 1, x * UNIT : (x + 1) * UNIT]
                extra = jnp.where(at == (r * len(sums) + g) * 2 + x, part, extra)
    for z in range(4):
        for y in range(2):
            for x in range(2):
                keep_ref[y, x, z, 3 * rows :, :] = extra.astype(BF16)
                send_ref[y, x, z, 3 * rows :, :] = extra.astype(BF16)


def attention_backward_kernel(
    others,
    before,
    q_ref,
    k_ref,
    v_ref,
    dctx_pair_ref,
    ctx_pair_ref,
    lse_ref,
    seg_ref,
    *refs,
):
    delta_ref, total_ref, kt_ref, dctx_ref, segc_ref = refs[-5:]
    if others is None:
        grads_ref, sums_ref = refs[:2]
    else:
        core_ref, h_ref = refs[:2]
        other_refs = refs[2 : 2 + others]
        before_refs = refs[2 + others : 2 + others + before]
        grads_ref, sums_ref, keep_ref, send_ref = refs[-9:-5]
    length = q_ref.shape[0]
    dctx_ref[...] = lanes(dctx_pair_ref[0], dctx_pair_ref[1])
    ctx = lanes(ctx_pair_ref[0], ctx_pair_ref[1])
    segr = seg_ref[...].astype(F32)
    segc_ref[...] = column_of(segr)
    prod = dctx_ref[...].astype(F32) * ctx.astype(F32)
    high = prod.astype(BF16)
    rest = (prod - high.astype(F32)).astype(BF16)
    lane = lax.broadcasted_iota(jnp.int32, (8, GROUP), 1)
    head_of = lax.broadcasted_iota(jnp.int32, (8, GROUP), 0)
    chooser = jnp.where(lane // HEAD == head_of, 1.0, 0.0).astype(BF16)
    delta_ref[...] = mm(chooser, high, NT) + mm(chooser, rest, NT)
    total_ref[...] = jnp.zeros_like(total_ref)
    kt_ref[...] = jnp.transpose(k_ref[...])

    def block(j, carry):
        rows = pl.ds(pl.multiple_of(j * TILE, TILE), TILE)
        kb = k_ref[rows, :]
        vb = v_ref[rows, :]
        mask = jnp.where(segc_ref[rows, :] == segr, 0.0, NEGATIVE)
        dk = jnp.zeros((TILE, GROUP), F32)
        dv = jnp.zeros((TILE, GROUP), F32)
        for head in range(PER_GROUP):
            mine = head_lanes((TILE, GROUP), head)
            km = jnp.where(mine, kb, BF16(0)) * BF16(HEAD**-0.5)
            vm = jnp.where(mine, vb, BF16(0))
            s = mm(km, q_ref[...], NT) + mask
            p = jnp.exp(s - lse_ref[head : head + 1, :])
            dp = mm(vm, dctx_ref[...], NT)
            ds = (p * (dp - delta_ref[head : head + 1, :])).astype(BF16)
            dv = jnp.where(mine, mm(p.astype(BF16), dctx_ref[...], NN), dv)
            dk = jnp.where(mine, mm(ds, q_ref[...], NN), dk)
            columns = slice(head * HEAD, (head + 1) * HEAD)
            total_ref[columns, :] += mm(kt_ref[columns, rows], ds, NN)
        dkb = (dk * HEAD**-0.5).astype(BF16)
        dvb = dv.astype(BF16)
        grads_ref[1, rows, :] = dkb
        grads_ref[2, rows, :] = dvb
        return carry + row_sum(dvb.astype(F32))

    dv_sum = lax.fori_loop(0, length // TILE, block, jnp.zeros((1, GROUP), F32), unroll=True)
    dq = jnp.transpose(total_ref[...] * HEAD**-0.5).astype(BF16)
    grads_ref[0] = dq
    sums_ref[...] = jnp.zeros_like(sums_ref)
    sums_ref[0:1, :] = row_sum(dq.astype(F32))
    sums_ref[1:2, :] = dv_sum
    if others is not None:
        sums = (*before_refs, sums_ref) if before else ()
        projection_part(core_ref, h_ref, (*other_refs, grads_ref), sums, keep_ref, send_ref)


def attention_backward(g, q, k, v, dctx, ctx, lse, seg, weights, passes, after):
    length, width = q.shape
    rows = pl.BlockSpec((length, GROUP), lambda i: (0, g))
    pair_rows = pl.BlockSpec((2, length, UNIT), lambda i: (0, 0, g))
    operands = [q, k, v, dctx, ctx, lse, seg]
    specs = [
        rows,
        rows,
        rows,
        pair_rows,
        pair_rows,
        pl.BlockSpec((8, length), lambda i: (g, 0)),
        fixed((1, length)),
    ]
    kinds = [jax.ShapeDtypeStruct((3, length, GROUP), BF16), jax.ShapeDtypeStruct((8, GROUP), F32)]
    outs = [fixed((3, length, GROUP)), fixed((8, GROUP))]
    others, before = None, 0
    if weights:
        core, h, grads, sums = weights
        others, before = len(grads), len(sums)
        operands += [core, h, *grads, *sums]
        specs += [SCALAR] + [fixed(x.shape) for x in (h, *grads, *sums)]
        shape = (2, 2, 4, 3 * width // 16 + BIAS_ROWS, (others + 1) * UNIT)
        kinds += [jax.ShapeDtypeStruct(shape, BF16)] * 2
        outs += [fixed(shape)] * 2
    return run(
        functools.partial(attention_backward_kernel, others, before),
        "attention_backward",
        (1,),
        tuple(operands),
        specs,
        kinds,
        outs,
        [
            pltpu.VMEM((8, length), F32),
            pltpu.VMEM((GROUP, length), F32),
            pltpu.VMEM((GROUP, length), BF16),
            pltpu.VMEM((length, GROUP), BF16),
            pltpu.VMEM((length, 1), F32),
        ],
        passes=passes,
        after=after,
        micros=8,
    )


def hidden_total(fp_ref, d_refs, w_refs):
    total = fp_ref[...]
    for at, w_ref in enumerate(w_refs):
        d = lanes(*[ref[at, :, x * UNIT : (x + 1) * UNIT] for x in range(2) for ref in d_refs])
        total = total + mm(d, w_ref[...], NT)
    return total


def hidden_away_kernel(fp_ref, *refs):
    refs[6][...] = hidden_total(fp_ref, refs[:3], refs[3:6]).astype(BF16)


def hidden_home_kernel(here_ref, fp_ref, *refs):
    came0_ref, came1_ref, out_ref, layer_ref = refs[6:]
    out_ref[0] = hidden_total(fp_ref, refs[:3], refs[3:6])
    layer_ref[0] = jnp.where(pl.program_id(0) == 0, came0_ref[...], came1_ref[...])


def hidden_away(fp, d0, d1, d2, wq, wk, wv, passes, after):
    length, width = fp.shape
    half = length // 2
    steps = half // TILE
    return run(
        hidden_away_kernel,
        "hidden_away",
        (steps,),
        (fp, d0, d1, d2, wq, wk, wv),
        [
            pl.BlockSpec((TILE, width), lambda i: (i + steps, 0)),
        ]
        + [pl.BlockSpec((3, TILE, GROUP), lambda i: (0, i + steps, 0))] * 3
        + [fixed((width, width))] * 3,
        (jax.ShapeDtypeStruct((half, width), BF16),),
        (pl.BlockSpec((TILE, width), lambda i: (i, 0)),),
        passes=passes,
        after=after,
        micros=3,
    )


def hidden_home(here, fp, d0, d1, d2, wq, wk, wv, came0, came1, layer, passes, after):
    length, width = fp.shape
    half = length // 2
    steps = half // TILE
    return run(
        hidden_home_kernel,
        "hidden_home",
        (steps,),
        (here, fp, d0, d1, d2, wq, wk, wv, came0, came1),
        [
            pl.BlockSpec((TILE, width), lambda i, b: (i, 0)),
        ]
        + [pl.BlockSpec((3, TILE, GROUP), lambda i, b: (0, i, 0))] * 3
        + [fixed((width, width))] * 3
        + [fixed((TILE, width))] * 2,
        (
            jax.ShapeDtypeStruct((2, half, width), F32),
            jax.ShapeDtypeStruct((2, half, width), BF16),
        ),
        (
            pl.BlockSpec((1, TILE, width), lambda i, b: (b[0], i, 0)),
            pl.BlockSpec((1, TILE, width), lambda i, b: (1 - b[0], i, 0)),
        ),
        scalars=1,
        held={1: layer},
        passes=passes,
        after=after,
        micros=3,
    )


def place_kernel(here_ref, came_ref, out_ref):
    out_ref[0] = came_ref[...].astype(F32)


def place_far(here, came, grad, passes):
    half, width = came.shape
    return run(
        place_kernel,
        "place_far",
        (2,),
        (here, came),
        [pl.BlockSpec((half // 2, width), lambda i, b: (i, 0))],
        (jax.ShapeDtypeStruct((2, half, width), F32),),
        (pl.BlockSpec((1, half // 2, width), lambda i, b: (1 - b[0], i, 0)),),
        scalars=1,
        held={0: grad},
        passes=passes,
        micros=1,
    )


def fast(
    hidden,
    segments,
    query_matrix,
    query_bias,
    key_matrix,
    value_matrix,
    value_bias,
    output_matrix,
    output_bias,
    first_gain,
    first_shift,
    inner_matrix,
    inner_bias,
    outer_matrix,
    outer_bias,
    second_gain,
    second_shift,
    cotangent,
):
    here = lax.axis_index("blk")
    place = lax.axis_index("seq")
    core, y_at, z_at = place % 2, (place // 2) % 2, place // 4
    here_id = here.astype(jnp.int32)[None]
    core_id = core.astype(jnp.int32)[None]
    half, width = hidden.shape[1:]

    def pick(x, *at):
        start = at + (0,) * (x.ndim - len(at))
        size = (1,) * len(at) + x.shape[len(at) :]
        return lax.dynamic_slice(x, start, size).reshape(x.shape[len(at) :])

    def trade(x):
        return lax.ppermute(x, "blk", [(0, 1), (1, 0)])

    def seq_swap(x, bit):
        return lax.ppermute(x, "seq", [(i, i ^ bit) for i in range(16)])

    def row(x):
        return x.astype(F32)[None, :]

    at = jnp.stack([here, y_at, z_at]).astype(jnp.int32)

    def rounded(x):
        return lax.reduce_precision(x, 8, 7)

    def sum_0(state, *at):
        return rounded(pick(state[0], *at).astype(F32) + pick(state[1], *at).astype(F32))

    def sum_1(state, mine, *at):
        return rounded(sum_0(state, mine, *at) + pick(state[2], *at).astype(F32))

    def sum_2(state, mine, then, *at):
        return rounded(sum_1(state, mine, then, *at) + pick(state[3], *at).astype(F32))

    def send_z(parts):
        return [seq_swap(x, 4 * d) for d, x in zip((1, 2, 3), parts)]

    def add_z(total, parts):
        return (total + parts[0].astype(F32)) + (parts[1].astype(F32) + parts[2].astype(F32))

    seg = jnp.concatenate([pick(segments, here), trade(pick(segments, 1 - here))])[None, :]
    far = trade(pick(hidden, 1 - here))
    cot_far = trade(pick(cotangent, 1 - here + jnp.minimum(seg[0, -1], 0)))
    q, k, v, ctx, lse, h = attention_forward(
        here_id,
        hidden,
        far,
        query_matrix,
        key_matrix,
        value_matrix,
        row(query_bias),
        row(value_bias),
        seg,
    )
    empty = jnp.zeros((2, width), F32)
    vec = jnp.concatenate(
        [
            row(output_bias),
            row(first_gain),
            row(first_shift),
            row(outer_bias),
            row(second_gain),
            row(second_shift),
            empty,
        ],
        axis=0,
    )
    out, out_far0, out_far1, first, act, og, ig, fp, ag, dctx, sums, isum = token_pass(
        here_id, h, ctx, cotangent, cot_far, output_matrix, inner_matrix, outer_matrix, row(inner_bias), vec
    )
    out_came0, out_came1 = trade(out_far0), trade(out_far1)
    x_mine, x_away, y_mine, y_away = here, 1 - here, y_at, 1 - y_at
    a_keep, a_send = outer_grad_call(core_id, act, og, sums, isum)
    a0 = seq_swap(a_send, 1)
    b_keep, b_send, a_keep = inner_grad_call(core_id, first, ig, ctx, ag, (a_keep,))
    b0 = seq_swap(b_send, 1)
    a = (a_keep, a0)
    a_away = sum_0(a, y_away).astype(BF16)
    a1 = seq_swap(a_away, 2)
    b = (b_keep, b0)
    b_away = sum_0(b, x_away).astype(BF16)
    b1 = trade(b_away)
    bwd = (q, k, v, dctx, ctx, lse, seg)
    grads0, bias0 = attention_backward(0, *bwd, (), (), (a_away, b_away))
    grads1, bias1, c_keep, c_send, a_keep, b_keep, out_came0 = attention_backward(
        1, *bwd, (core_id, h, (grads0,), ()), (a_keep, b_keep, out_came0), ()
    )
    c0 = seq_swap(c_send, 1)
    a = (a_keep, a0, a1)
    a_away = sum_1(a, y_mine, x_away).astype(BF16)
    a2 = trade(a_away)
    b = (b_keep, b0, b1)
    b_away = sum_1(b, x_mine, y_away).astype(BF16)
    b2 = seq_swap(b_away, 2)
    grads2, _, d_keep, d_send, a_keep, b_keep, c_keep = attention_backward(
        2, *bwd, (core_id, h, (), (bias0, bias1)), (a_keep, b_keep, c_keep), (a_away, b_away)
    )
    d0 = seq_swap(d_send, 1)
    c = (c_keep, c0)
    c_away = sum_0(c, y_away).astype(BF16)
    c1 = seq_swap(c_away, 2)

    def flat(x):
        return x.reshape(*x.shape[:-3], -1, x.shape[-1])

    a_rows, b_rows = a_keep.shape[3], 5 * width // 16
    states = [
        (a_keep, a0, a1, a2, 1, 0, 0),
        (flat(b_keep), flat(b0), flat(b1), flat(b2), 0, a_rows, 0),
    ]
    ab_mine, *parts, out_came1, d_keep = quarter(
        at, states, a_rows + b_rows, width // 2, (out_came1, d_keep), (c_away,)
    )
    ab3 = send_z(parts)
    args = (fp, grads0, grads1, grads2, query_matrix, key_matrix, value_matrix)
    d = (d_keep, d0)
    d_away = sum_0(d, y_away).astype(BF16)
    d1 = seq_swap(d_away, 2)
    hidden_grad, layer_out, c_keep, d_keep = hidden_home(
        here_id, *args, out_came0, out_came1, out, (c_keep, d_keep), (d_away,)
    )
    c = (c_keep, c0, c1)
    d = (d_keep, d0, d1)

    def lanes_of(*parts):
        return jnp.concatenate(parts, axis=-1)

    def late_1(*at):
        return lanes_of(sum_1(c, y_mine, *at), sum_1(d, y_mine, *at))

    e_away = late_1(x_away).astype(BF16)
    e2 = trade(e_away)
    far_grad, c_keep, d_keep, ab_mine = hidden_away(*args, (c_keep, d_keep, ab_mine), (e_away,))
    came = trade(far_grad)
    c = (c_keep, c0, c1)
    d = (d_keep, d0, d1)

    def late_2(z):
        return rounded(late_1(x_mine, z) + pick(e2, z).astype(F32))

    e3 = send_z([late_2(z_at ^ e).astype(BF16) for e in (1, 2, 3)])
    early = add_z(ab_mine.astype(F32), ab3)
    hidden_grad = place_far(here_id, came, hidden_grad, ())[0]
    late = add_z(late_2(z_at), e3)
    rows = width // 16
    outer_rows = 4 * rows
    outer_grad = early[:outer_rows]
    vectors = early[outer_rows : outer_rows + VECTOR_ROWS].reshape(-1, width)
    inner_all = early[outer_rows + VECTOR_ROWS :].reshape(5, rows, width // 2)
    output_grad = inner_all[4]
    inner_grad = jnp.transpose(inner_all[:4], (1, 0, 2)).reshape(rows, -1)
    units = width // UNIT
    biases = late[3 * rows :, 2 * UNIT :][: 2 * units].reshape(2, units // 2, 2, UNIT)
    biases = jnp.transpose(biases, (0, 2, 1, 3)).reshape(2, width)
    return (
        layer_out,
        hidden_grad,
        late[:rows],
        biases[0],
        late[rows : 2 * rows],
        late[2 * rows : 3 * rows],
        biases[1],
        output_grad,
        vectors[5],
        vectors[3],
        vectors[4],
        inner_grad,
        vectors[6:10].reshape(-1),
        outer_grad,
        vectors[2],
        vectors[0],
        vectors[1],
    )


def choose(sizes, *args):
    seq_count, row_count, width = args[0].shape
    whole_here = sizes[1] == 2 and seq_count == 2 and row_count == 2 * TILE and width == 3 * GROUP
    return fast(*args) if whole_here and sizes[0] == 16 else general(*args)


def solution(mesh):
    sizes = (mesh.shape["seq"], mesh.shape["blk"])
    return jax.shard_map(
        functools.partial(choose, sizes),
        mesh=mesh,
        in_specs=(
            P("seq", "blk", None),
            P("seq", "blk"),
            P(),
            P(),
            P(),
            P(),
            P(),
            P(),
            P(),
            P(),
            P(),
            P(),
            P(),
            P(),
            P(),
            P(),
            P(),
            P("seq", "blk", None),
        ),
        out_specs=(
            P("seq", "blk", None),
            P("seq", "blk", None),
            P("seq", "blk"),
            P(),
            P("seq", "blk"),
            P("seq", "blk"),
            P(),
            P("seq", "blk"),
            P(),
            P(),
            P(),
            P("seq", "blk"),
            P(),
            P("seq", "blk"),
            P(),
            P(),
            P(),
        ),
        check_vma=False,
    )
```

```python
import functools
import math

import jax
import jax.numpy as jnp
from jax import lax
from jax.experimental import pallas as pl
from jax.experimental.pallas import tpu as pltpu
from jax.sharding import PartitionSpec as P

HEADS = 12
HEAD = 64


NEGATIVE = -1e30
EPSILON = 1e-12


def layer_norm(values, norm_gain, norm_shift):
    centre = values - jnp.mean(values, axis=-1, keepdims=True)
    spread = jnp.mean(centre * centre, axis=-1, keepdims=True)
    return centre * lax.rsqrt(spread + EPSILON) * norm_gain + norm_shift


def gelu_exact(values):
    return jax.nn.gelu(values, approximate=False)


def linear(operand, matrix):
    return jnp.dot(operand, matrix, preferred_element_type=jnp.float32)


def split_heads(values):
    return values.reshape(values.shape[0], values.shape[1], HEADS, HEAD)


def block_scores(query_block, key_block, score_scale):
    return (
        jnp.einsum("sqhd,skhd->shqk", query_block, key_block, preferred_element_type=jnp.float32)
        * score_scale
    )


def attention_grads(
    query_block, key_block, value_block, dctx_block, same_doc, log_total, row_delta, score_scale
):
    attn_probs = jnp.where(
        same_doc,
        jnp.exp(block_scores(query_block, key_block, score_scale) - log_total[..., None]),
        0.0,
    )
    slopes = jnp.einsum(
        "sqhd,skhd->shqk", dctx_block, value_block, preferred_element_type=jnp.float32
    )
    return (attn_probs, (attn_probs * (slopes - row_delta[..., None])).astype(jnp.bfloat16))


def over_blocks(length, step, initial):
    block_size = math.gcd(length, 512)

    def scan_step(carried, block_index):
        return (step(carried, block_index * block_size, block_size), None)

    result, unused = lax.scan(scan_step, initial, jnp.arange(length // block_size, dtype=jnp.int32))
    return result


def general(
    hidden,
    segments,
    query_matrix,
    query_bias,
    key_matrix,
    value_matrix,
    value_bias,
    output_matrix,
    output_bias,
    first_gain,
    first_shift,
    inner_matrix,
    inner_bias,
    outer_matrix,
    outer_bias,
    second_gain,
    second_shift,
    cotangent,
):
    seq_count, row_count, model_width = hidden.shape
    score_scale = HEAD ** (-0.5)
    single_float = jnp.float32
    bf16 = jnp.bfloat16
    queries = (linear(hidden, query_matrix) + query_bias.astype(single_float)).astype(bf16)
    key_proj = linear(hidden, key_matrix).astype(bf16)
    value_proj = (linear(hidden, value_matrix) + value_bias.astype(single_float)).astype(bf16)
    seg_all = lax.all_gather(segments, "blk", axis=1, tiled=True)
    keys_all, values_all = (
        lax.all_gather(key_proj, "blk", axis=1, tiled=True),
        lax.all_gather(value_proj, "blk", axis=1, tiled=True),
    )
    length = seg_all.shape[1]
    query_heads = split_heads(queries)
    key_heads = split_heads(keys_all)
    value_heads = split_heads(values_all)

    def key_slices(offset, block_size):
        key_segs = lax.dynamic_slice_in_dim(seg_all, offset, block_size, 1)
        same_doc = (segments[:, :, None] == key_segs[:, None, :])[:, None]
        key_block = lax.dynamic_slice_in_dim(key_heads, offset, block_size, 1)
        value_block = lax.dynamic_slice_in_dim(value_heads, offset, block_size, 1)
        return (same_doc, key_block, value_block)

    def stats_step(carried, offset, block_size):
        same_doc, key_block, value_block = key_slices(offset, block_size)
        running_max, running_sum = carried
        scores = jnp.where(same_doc, block_scores(query_heads, key_block, score_scale), NEGATIVE)
        higher = jnp.maximum(running_max, jnp.max(scores, axis=-1))
        weights = jnp.where(same_doc, jnp.exp(scores - higher[..., None]), 0.0)
        return (higher, running_sum * jnp.exp(running_max - higher) + jnp.sum(weights, axis=-1))

    stat_shape = (seq_count, HEADS, row_count)
    running_max, running_sum = over_blocks(
        length,
        stats_step,
        (jnp.full(stat_shape, NEGATIVE, single_float), jnp.zeros(stat_shape, single_float)),
    )
    log_total = running_max + jnp.log(running_sum)

    def context_step(carried, offset, block_size):
        same_doc, key_block, value_block = key_slices(offset, block_size)
        attn_probs = jnp.where(
            same_doc,
            jnp.exp(block_scores(query_heads, key_block, score_scale) - log_total[..., None]),
            0.0,
        )
        return carried + jnp.einsum(
            "shqk,skhd->sqhd",
            attn_probs.astype(bf16),
            value_block,
            preferred_element_type=single_float,
        )

    head_zeros = jnp.zeros((seq_count, row_count, HEADS, HEAD), single_float)
    context = over_blocks(length, context_step, head_zeros)
    context_reduced = context.reshape(seq_count, row_count, model_width).astype(bf16)
    attn_out = linear(context_reduced, output_matrix) + output_bias.astype(single_float)
    first_pre = hidden.astype(single_float) + attn_out
    first_norm, first_back = jax.vjp(
        layer_norm, first_pre, first_gain.astype(single_float), first_shift.astype(single_float)
    )
    first_reduced = first_norm.astype(bf16)
    inner = linear(first_reduced, inner_matrix) + inner_bias.astype(single_float)
    act_full, gelu_back = jax.vjp(gelu_exact, inner)
    activation_reduced = act_full.astype(bf16)
    outer = linear(activation_reduced, outer_matrix) + outer_bias.astype(single_float)
    layer_full, second_back = jax.vjp(
        layer_norm,
        first_norm + outer,
        second_gain.astype(single_float),
        second_shift.astype(single_float),
    )
    layer_out = layer_full.astype(bf16)
    second_pre_grad, second_gain_grad, second_shift_grad = second_back(
        cotangent.astype(single_float)
    )
    outer_gradient_reduced = second_pre_grad.astype(bf16)
    outer_weight_grad = jnp.einsum(
        "gvx,gvm->xm",
        activation_reduced,
        outer_gradient_reduced,
        preferred_element_type=single_float,
    )
    outer_bias_grad = jnp.sum(outer_gradient_reduced.astype(single_float), axis=(0, 1))
    activation_gradient = jnp.einsum(
        "rzo,uo->rzu", outer_gradient_reduced, outer_matrix, preferred_element_type=single_float
    )
    inner_gradient_reduced = gelu_back(activation_gradient)[0].astype(bf16)
    inner_weight_grad = jnp.einsum(
        "ret,reu->tu", first_reduced, inner_gradient_reduced, preferred_element_type=single_float
    )
    inner_bias_grad = jnp.sum(inner_gradient_reduced.astype(single_float), axis=(0, 1))
    first_norm_grad = second_pre_grad + jnp.einsum(
        "aoi,ni->aon", inner_gradient_reduced, inner_matrix, preferred_element_type=single_float
    )
    first_pre_grad, first_gain_grad, first_shift_grad = first_back(first_norm_grad)
    attention_gradient_reduced = first_pre_grad.astype(bf16)
    output_weight_grad = jnp.einsum(
        "tfm,tfc->mc",
        context_reduced,
        attention_gradient_reduced,
        preferred_element_type=single_float,
    )
    output_bias_grad = jnp.sum(attention_gradient_reduced.astype(single_float), axis=(0, 1))
    dctx_low = jnp.einsum(
        "upx,cx->upc",
        attention_gradient_reduced,
        output_matrix,
        preferred_element_type=single_float,
    ).astype(bf16)
    dctx_heads = split_heads(dctx_low)
    row_delta = jnp.transpose(
        jnp.sum(dctx_heads.astype(single_float) * context, axis=-1), (0, 2, 1)
    )

    def query_step(carried, offset, block_size):
        same_doc, key_block, value_block = key_slices(offset, block_size)
        attn_probs, dscores = attention_grads(
            query_heads,
            key_block,
            value_block,
            dctx_heads,
            same_doc,
            log_total,
            row_delta,
            score_scale,
        )
        return carried + score_scale * jnp.einsum(
            "shqk,skhd->sqhd", dscores, key_block, preferred_element_type=single_float
        )

    query_grad = over_blocks(length, query_step, head_zeros)
    query_all, dctx_all = (
        lax.all_gather(queries, "blk", axis=1, tiled=True),
        lax.all_gather(dctx_low, "blk", axis=1, tiled=True),
    )
    lse_all, delta_all = (
        lax.all_gather(log_total, "blk", axis=2, tiled=True),
        lax.all_gather(row_delta, "blk", axis=2, tiled=True),
    )
    query_all_heads = split_heads(query_all)
    dctx_all_heads = split_heads(dctx_all)
    own_keys = split_heads(key_proj)
    own_values = split_heads(value_proj)

    def key_step(carried, offset, block_size):
        query_segs = lax.dynamic_slice_in_dim(seg_all, offset, block_size, 1)
        same_doc = (query_segs[:, :, None] == segments[:, None, :])[:, None]
        query_block = lax.dynamic_slice_in_dim(query_all_heads, offset, block_size, 1)
        dctx_block = lax.dynamic_slice_in_dim(dctx_all_heads, offset, block_size, 1)
        lse_block = lax.dynamic_slice_in_dim(lse_all, offset, block_size, 2)
        delta_block = lax.dynamic_slice_in_dim(delta_all, offset, block_size, 2)
        key_sum, value_sum = carried
        attn_probs, dscores = attention_grads(
            query_block,
            own_keys,
            own_values,
            dctx_block,
            same_doc,
            lse_block,
            delta_block,
            score_scale,
        )
        key_sum = key_sum + score_scale * jnp.einsum(
            "shqk,sqhd->skhd", dscores, query_block, preferred_element_type=single_float
        )
        value_sum = value_sum + jnp.einsum(
            "shqk,sqhd->skhd",
            attn_probs.astype(bf16),
            dctx_block,
            preferred_element_type=single_float,
        )
        return (key_sum, value_sum)

    key_grad, value_grad = over_blocks(length, key_step, (head_zeros, head_zeros))
    query_gradient_reduced = query_grad.reshape(seq_count, row_count, model_width).astype(bf16)
    key_gradient_reduced = key_grad.reshape(seq_count, row_count, model_width).astype(bf16)
    value_gradient_reduced = value_grad.reshape(seq_count, row_count, model_width).astype(bf16)
    query_weight_grad = jnp.einsum(
        "tfm,tfc->mc", hidden, query_gradient_reduced, preferred_element_type=single_float
    )
    query_bias_grad = jnp.sum(query_gradient_reduced.astype(single_float), axis=(0, 1))
    key_matrix_gradient = jnp.einsum(
        "tfm,tfc->mc", hidden, key_gradient_reduced, preferred_element_type=single_float
    )
    value_weight_grad = jnp.einsum(
        "tfm,tfc->mc", hidden, value_gradient_reduced, preferred_element_type=single_float
    )
    value_bias_grad = jnp.sum(value_gradient_reduced.astype(single_float), axis=(0, 1))
    hidden_grad = first_pre_grad + jnp.einsum(
        "upx,cx->upc", query_gradient_reduced, query_matrix, preferred_element_type=single_float
    )
    hidden_grad = hidden_grad + jnp.einsum(
        "upx,cx->upc", key_gradient_reduced, key_matrix, preferred_element_type=single_float
    )
    hidden_grad = hidden_grad + jnp.einsum(
        "upx,cx->upc", value_gradient_reduced, value_matrix, preferred_element_type=single_float
    )
    partial_sums = (
        lax.psum_scatter(query_weight_grad, "seq", scatter_dimension=0, tiled=True),
        lax.psum_scatter(key_matrix_gradient, "seq", scatter_dimension=0, tiled=True),
        lax.psum_scatter(value_weight_grad, "seq", scatter_dimension=0, tiled=True),
        lax.psum_scatter(output_weight_grad, "seq", scatter_dimension=0, tiled=True),
        lax.psum_scatter(inner_weight_grad, "seq", scatter_dimension=0, tiled=True),
        lax.psum_scatter(outer_weight_grad, "seq", scatter_dimension=0, tiled=True),
    )
    matrices = lax.psum_scatter(tuple(partial_sums), "blk", scatter_dimension=1, tiled=True)
    vectors = lax.psum(
        (
            query_bias_grad,
            value_bias_grad,
            output_bias_grad,
            first_gain_grad,
            first_shift_grad,
            inner_bias_grad,
            outer_bias_grad,
            second_gain_grad,
            second_shift_grad,
        ),
        ("seq", "blk"),
    )
    return (
        layer_out,
        hidden_grad,
        matrices[0],
        vectors[0],
        matrices[1],
        matrices[2],
        vectors[1],
        matrices[3],
        vectors[2],
        vectors[3],
        vectors[4],
        matrices[4],
        vectors[5],
        matrices[5],
        vectors[6],
        vectors[7],
        vectors[8],
    )


BF16 = jnp.bfloat16
F32 = jnp.float32
NN = ((1,), (0,))
NT = ((1,), (1,))
TN = ((0,), (0,))
UNIT = 128
GROUP = 256
PER_GROUP = GROUP // HEAD
TILE = 256
TOKENS = 512
VMEM_LIMIT = 60 * 2**20
SCALAR = pl.BlockSpec(memory_space=pltpu.SMEM)
ANY = pl.BlockSpec(memory_space=pl.ANY)


def mm(a, b, dims):
    return lax.dot_general(a, b, (dims, ((), ())), preferred_element_type=F32)


def fixed(shape):
    return pl.BlockSpec(shape, lambda *_: (0,) * len(shape), pipeline_mode=pl.Buffered(1))


def run(
    kernel,
    name,
    grid,
    operands,
    in_specs,
    out_shape,
    out_specs,
    scratch=(),
    scalars=0,
    held=None,
    passes=(),
    after=(),
    micros=1,
):
    held = held or {}
    out_shape, out_specs = list(out_shape), list(out_specs)
    n_in, n_out, n_held, n_pass = len(operands), len(out_shape), len(held), len(passes)
    aliases = {n_in + i: at for i, at in enumerate(held)}
    aliases |= {n_in + n_held + i: n_out + i for i in range(n_pass)}

    def body(*refs):
        outs = n_in + n_held + n_pass + len(after)
        kernel(*refs[:n_in], *refs[outs : outs + n_out], *refs[outs + n_out + n_pass :])

    result = pl.pallas_call(
        body,
        grid_spec=pltpu.PrefetchScalarGridSpec(
            num_scalar_prefetch=scalars,
            grid=grid,
            in_specs=list(in_specs) + [ANY] * (n_held + n_pass + len(after)),
            out_specs=out_specs + [ANY] * n_pass,
            scratch_shapes=list(scratch),
        ),
        out_shape=out_shape + [jax.ShapeDtypeStruct(x.shape, x.dtype) for x in passes],
        input_output_aliases=aliases,
        compiler_params=pltpu.CompilerParams(
            vmem_limit_bytes=VMEM_LIMIT, dimension_semantics=("arbitrary",) * len(grid)
        ),
        cost_estimate=pl.CostEstimate(
            flops=int(micros * 1e10), bytes_accessed=1, transcendentals=0
        ),
        name=name,
    )(*operands, *held.values(), *passes, *after)
    return result


def head_lanes(shape, head):
    lane = lax.broadcasted_iota(jnp.int32, shape, 1)
    return (lane >= head * HEAD) & (lane < (head + 1) * HEAD)


def lanes(*parts):
    return jnp.concatenate(parts, axis=1)


def column_of(row):
    return jnp.transpose(jnp.broadcast_to(row.astype(F32), (UNIT, row.shape[1])))[:, 0:1]


def same_pair(row, column, rows):
    return jnp.where(column[rows] == row, 0.0, NEGATIVE)


def attention_forward_kernel(
    here_ref,
    own_ref,
    far_ref,
    wq0_ref,
    wq1_ref,
    wk0_ref,
    wk1_ref,
    wv0_ref,
    wv1_ref,
    bq0_ref,
    bq1_ref,
    bv0_ref,
    bv1_ref,
    seg_ref,
    q_ref,
    k_ref,
    v_ref,
    ctx_ref,
    lse_ref,
    h_ref,
    mask_ref,
    vaug_ref,
):
    half = far_ref.shape[0]
    length = 2 * half

    @pl.when(pl.program_id(0) == 0)
    def _():
        segr = seg_ref[...].astype(F32)
        mask_ref[...] = jnp.where(column_of(segr) == segr, 0.0, NEGATIVE)
        h_ref[0:half, :] = own_ref[0]
        h_ref[half:, :] = far_ref[...]

    h = h_ref[...]
    bias_q = lanes(bq0_ref[...], bq1_ref[...])
    bias_v = lanes(bv0_ref[...], bv1_ref[...])
    q_ref[...] = (mm(h, lanes(wq0_ref[...], wq1_ref[...]), NN) + bias_q).astype(BF16)
    k_ref[...] = mm(h, lanes(wk0_ref[...], wk1_ref[...]), NN).astype(BF16)
    v = (mm(h, lanes(wv0_ref[...], wv1_ref[...]), NN) + bias_v).astype(BF16)
    v_ref[...] = v
    lane = lax.broadcasted_iota(jnp.int32, v.shape, 1)
    for head in range(PER_GROUP):
        other = (lane // UNIT) != (head // 2)
        filler = jnp.where(other, 1.0, 0.0).astype(BF16)
        vaug_ref[head] = jnp.where(head_lanes(v.shape, head), v, filler)

    def block(i, carry):
        rows = pl.ds(pl.multiple_of(i * TILE, TILE), TILE)
        qb = q_ref[rows, :] * BF16(HEAD**-0.5)
        halves = [None, None]
        stat_lane = lax.broadcasted_iota(jnp.int32, (TILE, UNIT), 1)
        stats = jnp.zeros((TILE, UNIT), F32)
        for head in range(PER_GROUP):
            qm = jnp.where(head_lanes(qb.shape, head), qb, BF16(0))
            s = mm(qm, k_ref[...], NT) + mask_ref[rows, :]
            top = jnp.max(s, axis=1, keepdims=True)
            e = jnp.exp(s - top).astype(BF16)
            o = mm(e, vaug_ref[head], NN)
            t = head // 2
            total = o[:, (1 - t) * UNIT : (2 - t) * UNIT]
            part = o[:, t * UNIT : (t + 1) * UNIT] / total
            halves[t] = part if halves[t] is None else halves[t] + part
            stats = jnp.where(stat_lane == head, top + jnp.log(total), stats)
        ctx_ref[0, rows, :] = halves[0].astype(BF16)
        ctx_ref[1, rows, :] = halves[1].astype(BF16)
        lse_ref[:, rows] = jnp.transpose(stats)[0:8]
        return carry

    lax.fori_loop(0, length // TILE, block, 0, unroll=True)


def attention_forward(here, hidden, far, wq, wk, wv, bq, bv, seg):
    half, width = far.shape
    length = 2 * half
    groups = width // GROUP
    left = pl.BlockSpec((width, UNIT), lambda g, h: (0, g))
    right = pl.BlockSpec((width, UNIT), lambda g, h: (0, groups + g))
    bias_left = pl.BlockSpec((1, UNIT), lambda g, h: (0, g))
    bias_right = pl.BlockSpec((1, UNIT), lambda g, h: (0, groups + g))
    rows = pl.BlockSpec((length, GROUP), lambda g, h: (0, g))
    wide = jax.ShapeDtypeStruct((length, width), BF16)
    own = pl.BlockSpec((1, half, width), lambda g, h: (h[0], 0, 0), pipeline_mode=pl.Buffered(1))
    return run(
        attention_forward_kernel,
        "attention_forward",
        (groups,),
        (here, hidden, far, wq, wq, wk, wk, wv, wv, bq, bq, bv, bv, seg),
        [own, fixed((half, width))]
        + [left, right] * 3
        + [bias_left, bias_right] * 2
        + [fixed((1, length))],
        (
            wide,
            wide,
            wide,
            jax.ShapeDtypeStruct((2, length, width // 2), BF16),
            jax.ShapeDtypeStruct((8 * groups, length), F32),
            wide,
        ),
        (
            rows,
            rows,
            rows,
            pl.BlockSpec((2, length, UNIT), lambda g, h: (0, 0, g)),
            pl.BlockSpec((8, length), lambda g, h: (g, 0)),
            pl.BlockSpec((length, width), lambda g, h: (0, 0)),
        ),
        [pltpu.VMEM((length, length), F32), pltpu.VMEM((PER_GROUP, length, GROUP), BF16)],
        scalars=1,
        micros=16,
    )


def gelu_pair(u):
    phi = 0.5 + 0.5 * lax.erf(u * 0.7071067811865476)
    bell = jnp.exp2(u * u * -0.7213475204444817)
    return (u * phi, phi + u * bell * 0.3989422804014327)


def normed(x):
    centre = x - jnp.mean(x, axis=1, keepdims=True)
    scale = lax.rsqrt(jnp.mean(centre * centre, axis=1, keepdims=True) + EPSILON)
    return (centre * scale, scale)


def norm_back(u, n, scale):
    return scale * (u - jnp.mean(u, axis=1, keepdims=True) - n * jnp.mean(u * n, axis=1, keepdims=True))


def row_sum(x):
    return jnp.sum(x, axis=0, keepdims=True)


def token_kernel(
    here_ref,
    h_ref,
    ctx_ref,
    cot_own_ref,
    cot_far_ref,
    wo_ref,
    wi_ref,
    wp_ref,
    bi_ref,
    vec_ref,
    out_ref,
    far0_ref,
    far1_ref,
    first_ref,
    act_ref,
    og_ref,
    ig_ref,
    fp_ref,
    ag_ref,
    dctx_ref,
    sums_ref,
    isum_ref,
    slope_ref,
):
    step = pl.program_id(0)
    steps = pl.num_programs(0)

    @pl.when(step == 0)
    def _():
        sums_ref[...] = jnp.zeros_like(sums_ref)
        isum_ref[...] = jnp.zeros_like(isum_ref)

    ff = wi_ref.shape[1]
    chunk = 512
    output_bias, gain1, shift1 = vec_ref[0:1, :], vec_ref[1:2, :], vec_ref[2:3, :]
    outer_bias, gain2, shift2 = vec_ref[3:4, :], vec_ref[4:5, :], vec_ref[5:6, :]
    middle = wo_ref.shape[0] // 2
    near = step < steps // 2

    def part(rows):
        ctx = lanes(ctx_ref[0, rows, :], ctx_ref[1, rows, :])
        x = h_ref[rows, :].astype(F32) + mm(ctx, wo_ref[...], NN) + output_bias
        yield
        n1, r1 = normed(x)
        fn = n1 * gain1 + shift1
        first = fn.astype(BF16)
        first_ref[rows, :] = first
        yield
        for c in range(0, ff, chunk):
            act, slope = gelu_pair(mm(first, wi_ref[:, c : c + chunk], NN) + bi_ref[:, c : c + chunk])
            act_ref[rows, c : c + chunk] = act.astype(BF16)
            slope_ref[rows, c : c + chunk] = slope
            yield
        x = fn + mm(act_ref[rows, :], wp_ref[...], NN) + outer_bias
        yield
        n2, r2 = normed(x)
        out = (n2 * gain2 + shift2).astype(BF16)

        out_ref[0, rows, :] = jnp.where(near, out, out_ref[0, rows, :])
        (far1_ref if rows.start else far0_ref)[...] = out
        e = jnp.where(near, cot_own_ref[0, rows, :], cot_far_ref[rows, :]).astype(F32)
        sums_ref[0:1, :] += row_sum(e * n2)
        sums_ref[1:2, :] += row_sum(e)
        sp = norm_back(e * gain2, n2, r2)
        og = sp.astype(BF16)
        og_ref[rows, :] = og
        sums_ref[2:3, :] += row_sum(og.astype(F32))
        yield
        for c in range(0, ff, chunk):
            ig = (mm(og, wp_ref[c : c + chunk, :], NT) * slope_ref[rows, c : c + chunk]).astype(BF16)
            ig_ref[rows, c : c + chunk] = ig
            isum_ref[:, c : c + chunk] += row_sum(ig.astype(F32))
            yield
        d = sp + mm(ig_ref[rows, :], wi_ref[...], NT)
        yield
        sums_ref[3:4, :] += row_sum(d * n1)
        sums_ref[4:5, :] += row_sum(d)
        fp = norm_back(d * gain1, n1, r1)
        fp_ref[rows, :] = fp
        ag = fp.astype(BF16)
        ag_ref[rows, :] = ag
        sums_ref[5:6, :] += row_sum(ag.astype(F32))
        yield
        dctx = mm(ag, wo_ref[...], NT).astype(BF16)
        dctx_ref[0, rows, :] = dctx[:, :middle]
        dctx_ref[1, rows, :] = dctx[:, middle:]

    size = h_ref.shape[0]
    parts = [part(slice(r, r + TILE)) for r in range(0, size, TILE)]
    live, waiting = [], list(parts)
    while waiting or live:
        if waiting:
            live.append(waiting.pop(0))
        live = [p for p in live if next(p, 0) is None]


def token_pass(here, h, ctx, cot, cot_far, wo, wi, wp, bi, vec):
    length, width = h.shape
    half = length // 2
    ff = wi.shape[1]
    steps = length // TOKENS
    near = steps // 2
    rows = pl.BlockSpec((TOKENS, width), lambda i, b: (i, 0))
    split_rows = pl.BlockSpec((2, TOKENS, width // 2), lambda i, b: (0, i, 0))
    wide_rows = pl.BlockSpec((TOKENS, ff), lambda i, b: (i, 0))
    own_rows = pl.BlockSpec((1, TOKENS, width), lambda i, b: (b[0], jnp.minimum(i, near - 1), 0))
    far_rows = pl.BlockSpec((TOKENS, width), lambda i, b: (jnp.maximum(i - near, 0), 0))
    low = jax.ShapeDtypeStruct((length, width), BF16)
    low_ff = jax.ShapeDtypeStruct((length, ff), BF16)
    return run(
        token_kernel,
        "token_pass",
        (steps,),
        (here, h, ctx, cot, cot_far, wo, wi, wp, bi, vec),
        [
            rows,
            split_rows,
            own_rows,
            far_rows,
            fixed((width, width)),
            fixed((width, ff)),
            fixed((ff, width)),
            fixed((1, ff)),
            fixed((8, width)),
        ],
        (
            jax.ShapeDtypeStruct((2, half, width), BF16),
            jax.ShapeDtypeStruct((half // 2, width), BF16),
            jax.ShapeDtypeStruct((half // 2, width), BF16),
            low,
            low_ff,
            low,
            low_ff,
            jax.ShapeDtypeStruct((length, width), F32),
            low,
            jax.ShapeDtypeStruct((2, length, width // 2), BF16),
            jax.ShapeDtypeStruct((8, width), F32),
            jax.ShapeDtypeStruct((1, ff), F32),
        ),
        (
            own_rows,
            pl.BlockSpec((half // 2, width), lambda i, b: (0, 0)),
            pl.BlockSpec((half // 2, width), lambda i, b: (0, 0)),
            rows,
            wide_rows,
            rows,
            wide_rows,
            rows,
            rows,
            split_rows,
            pl.BlockSpec((8, width), lambda i, b: (0, 0)),
            pl.BlockSpec((1, ff), lambda i, b: (0, 0)),
        ),
        [pltpu.VMEM((TOKENS, ff), F32)],
        scalars=1,
        micros=23,
    )


def put_pairs(a, b, core_ref, keep_ref, send_ref, columns, rows, count):
    even = core_ref[0] == 0
    for z in range(count):
        if z % 2 == 0:
            res = mm(a[:, 4 * z * rows : 4 * (z + 2) * rows], b, TN)
        for y in range(2):
            base = (z % 2 * 2 + y) * 2 * rows
            for x in range(2):
                zero = lanes(*[res[base : base + rows, c] for c in columns[x]])
                one = lanes(*[res[base + rows : base + 2 * rows, c] for c in columns[x]])
                keep_ref[x, y, z, 0] = jnp.where(even, zero, one).astype(BF16)
                send_ref[x, y, z, 0] = jnp.where(even, one, zero).astype(BF16)


HALVES = ((slice(0, 384),), (slice(384, 768),))
VECTOR_ROWS = 32
BIAS_ROWS = 16


def outer_grad_kernel(core_ref, act_ref, og_ref, sums_ref, isum_ref, keep_ref, send_ref, rows_ref):
    middle = og_ref.shape[1] // 2
    rows = act_ref.shape[1] // 4
    even = core_ref[0] == 0
    rows_ref[...] = jnp.zeros_like(rows_ref)
    at = 0
    for r in range(6):
        for x in range(2):
            rows_ref[at : at + 1, :] = sums_ref[r : r + 1, x * middle : (x + 1) * middle]
            at += 1
    for r in range(isum_ref.shape[1] // middle):
        rows_ref[at : at + 1, :] = isum_ref[:, r * middle : (r + 1) * middle]
        at += 1
    extra = rows_ref[...].astype(BF16)
    for y in range(2):
        res = mm(act_ref[:, 2 * y * rows : 2 * (y + 1) * rows], og_ref[...], TN)
        for x in range(2):
            columns = slice(x * middle, (x + 1) * middle)
            zero = res[0:rows, columns]
            one = res[rows:, columns]
            keep_ref[y, x, 0, 0:rows, :] = jnp.where(even, zero, one).astype(BF16)
            send_ref[y, x, 0, 0:rows, :] = jnp.where(even, one, zero).astype(BF16)
            keep_ref[y, x, 0, rows:, :] = extra
            send_ref[y, x, 0, rows:, :] = extra


def pair_out(shape, block, index):
    kind = jax.ShapeDtypeStruct(shape, BF16)
    spec = pl.BlockSpec(block, index)
    return ((kind, kind), (spec, spec))


def outer_grad_call(core, act, og, sums, isum):
    length, ff = act.shape
    width = og.shape[1]
    shape = (2, 2, 4, ff // 16 + VECTOR_ROWS, width // 2)
    kinds, specs = pair_out(shape, (2, 2, 1) + shape[3:], lambda z: (0, 0, z, 0, 0))
    return run(
        outer_grad_kernel,
        "outer_grad",
        (4,),
        (core, act, og, sums, isum),
        [
            SCALAR,
            pl.BlockSpec((length, ff // 4), lambda z: (0, z)),
            fixed((length, width)),
            fixed(sums.shape),
            fixed(isum.shape),
        ],
        kinds,
        specs,
        [pltpu.VMEM((VECTOR_ROWS, width // 2), F32)],
        micros=4.5,
    )


def inner_grad_kernel(
    core_ref, first_ref, low_ref, high_ref, ctx_ref, ag_ref, keep_ref, send_ref
):
    step = pl.program_id(0)
    rows = keep_ref.shape[4]

    @pl.when(step < 4)
    def _():
        both = lanes(low_ref[...], high_ref[...])
        put_pairs(first_ref[...], both, core_ref, keep_ref, send_ref, HALVES, rows, 4)

    @pl.when(step == 4)
    def _():
        ctx = lanes(ctx_ref[0], ctx_ref[1])
        put_pairs(ctx, ag_ref[...], core_ref, keep_ref, send_ref, HALVES, rows, 4)


def inner_grad_call(core, first, ig, ctx, ag, passes):
    length, width = first.shape
    shape = (2, 2, 4, 5, width // 16, width // 2)
    kinds, specs = pair_out(shape, shape[:3] + (1,) + shape[4:], lambda s: (0, 0, 0, s, 0, 0))
    return run(
        inner_grad_kernel,
        "inner_grad",
        (5,),
        (core, first, ig, ig, ctx, ag),
        [
            SCALAR,
            fixed((length, width)),
            pl.BlockSpec((length, width // 2), lambda s: (0, jnp.minimum(s, 3))),
            pl.BlockSpec((length, width // 2), lambda s: (0, 4 + jnp.minimum(s, 3))),
            fixed((2, length, width // 2)),
            fixed((length, width)),
        ],
        kinds,
        specs,
        passes=passes,
        micros=6,
    )


def rounded(x):
    return x.astype(BF16).astype(F32)


def halve_first_kernel(at_ref, keep_ref, came_ref, out_ref):
    out_ref[...] = (keep_ref[0].astype(F32) + came_ref[0].astype(F32)).astype(BF16)


def halve_first(at, axis, keep, came, passes):
    _, _, depth, rows, width = keep.shape
    half = pl.BlockSpec((1, 2, depth, rows, width), lambda i, s: (1 - s[axis], 0, 0, 0, 0))
    return run(
        halve_first_kernel,
        "halve_first",
        (1,),
        (at, keep, came),
        [half, half],
        (jax.ShapeDtypeStruct((2, depth, rows, width), BF16),),
        (fixed((2, depth, rows, width)),),
        scalars=1,
        passes=passes,
    )


def sum_second(keep, came, came1):
    total = rounded(keep.astype(F32) + came.astype(F32))
    return rounded(total + came1.astype(F32))


def quarter_kernel(plan, at_ref, *refs):
    outs = refs[-4:]
    here = at_ref[2]
    for d in range(4):
        z = lax.bitwise_xor(here, d)
        for first, count, row, column, through in plan:
            keep_ref, came_ref, came1_ref = refs[first : first + 3]
            came2_ref = refs[through]
            rows, part = keep_ref.shape[3:]
            total = sum_second(keep_ref[0, 0, z], came_ref[0, 0, z], came1_ref[0, z])
            came2 = came2_ref[z, :, column : column + part]
            outs[d][row : row + rows, column : column + part] = rounded(
                total + came2.astype(F32)
            ).astype(BF16)


def quarter(at, states, total_rows, total_width, passes, after):
    specs, operands, plan, seen = [], [], [], {}
    for keep, came, came1, came2, axis, row, column in states:
        _, _, depth, rows, part = keep.shape
        if axis == 0:
            both = pl.BlockSpec((1, 1, depth, rows, part), lambda i, s: (s[0], s[1], 0, 0, 0))
            one = pl.BlockSpec((1, depth, rows, part), lambda i, s: (s[1], 0, 0, 0))
        else:
            both = pl.BlockSpec((1, 1, depth, rows, part), lambda i, s: (s[1], s[0], 0, 0, 0))
            one = pl.BlockSpec((1, depth, rows, part), lambda i, s: (s[0], 0, 0, 0))
        first = len(operands)
        specs += [both, both, one]
        operands += [keep, came, came1]
        if id(came2) not in seen:
            seen[id(came2)] = len(operands)
            specs.append(fixed(came2.shape))
            operands.append(came2)
        plan.append((first, 3, row, column, seen[id(came2)]))
    part = jax.ShapeDtypeStruct((total_rows, total_width), BF16)
    return run(
        functools.partial(quarter_kernel, plan),
        "quarter",
        (1,),
        (at, *operands),
        specs,
        (part,) * 4,
        (pl.BlockSpec((total_rows, total_width), lambda i, s: (0, 0)),) * 4,
        scalars=1,
        passes=passes,
        after=after,
    )


def projection_part(core_ref, h_ref, grads, sums, keep_ref, send_ref):
    rows = h_ref.shape[1] // 16
    even = core_ref[0] == 0
    for s in range(3):
        place = slice(s * rows, (s + 1) * rows)
        parts = [mm(h_ref[...], ref[s], TN) for ref in grads]
        for z in range(4):
            for y in range(2):
                base = (z * 2 + y) * 2 * rows
                for x in range(2):
                    unit = slice(x * UNIT, (x + 1) * UNIT)
                    zero = lanes(*[p[base : base + rows, unit] for p in parts])
                    one = lanes(*[p[base + rows : base + 2 * rows, unit] for p in parts])
                    keep_ref[y, x, z, place, :] = jnp.where(even, zero, one).astype(BF16)
                    send_ref[y, x, z, place, :] = jnp.where(even, one, zero).astype(BF16)
    extra = jnp.zeros((BIAS_ROWS, keep_ref.shape[4]), F32)
    at = lax.broadcasted_iota(jnp.int32, extra.shape, 0)
    for r in range(2):
        for g, ref in enumerate(sums):
            for x in range(2):
                part = ref[r : r + 1, x * UNIT : (x + 1) * UNIT]
                extra = jnp.where(at == (r * len(sums) + g) * 2 + x, part, extra)
    for z in range(4):
        for y in range(2):
            for x in range(2):
                keep_ref[y, x, z, 3 * rows :, :] = extra.astype(BF16)
                send_ref[y, x, z, 3 * rows :, :] = extra.astype(BF16)


def attention_backward_kernel(
    others,
    before,
    q_ref,
    k_ref,
    v_ref,
    dctx_pair_ref,
    ctx_pair_ref,
    lse_ref,
    seg_ref,
    *refs,
):
    delta_ref, total_ref, kt_ref, dctx_ref, segc_ref = refs[-5:]
    if others is None:
        grads_ref, sums_ref = refs[:2]
    else:
        core_ref, h_ref = refs[:2]
        other_refs = refs[2 : 2 + others]
        before_refs = refs[2 + others : 2 + others + before]
        grads_ref, sums_ref, keep_ref, send_ref = refs[-9:-5]
    length = q_ref.shape[0]
    dctx_ref[...] = lanes(dctx_pair_ref[0], dctx_pair_ref[1])
    ctx = lanes(ctx_pair_ref[0], ctx_pair_ref[1])
    segr = seg_ref[...].astype(F32)
    segc_ref[...] = column_of(segr)
    prod = dctx_ref[...].astype(F32) * ctx.astype(F32)
    high = prod.astype(BF16)
    rest = (prod - high.astype(F32)).astype(BF16)
    lane = lax.broadcasted_iota(jnp.int32, (8, GROUP), 1)
    head_of = lax.broadcasted_iota(jnp.int32, (8, GROUP), 0)
    chooser = jnp.where(lane // HEAD == head_of, 1.0, 0.0).astype(BF16)
    delta_ref[...] = mm(chooser, high, NT) + mm(chooser, rest, NT)
    total_ref[...] = jnp.zeros_like(total_ref)
    kt_ref[...] = jnp.transpose(k_ref[...])

    def block(j, carry):
        rows = pl.ds(pl.multiple_of(j * TILE, TILE), TILE)
        kb = k_ref[rows, :]
        vb = v_ref[rows, :]
        mask = jnp.where(segc_ref[rows, :] == segr, 0.0, NEGATIVE)
        dk = jnp.zeros((TILE, GROUP), F32)
        dv = jnp.zeros((TILE, GROUP), F32)
        for head in range(PER_GROUP):
            mine = head_lanes((TILE, GROUP), head)
            km = jnp.where(mine, kb, BF16(0)) * BF16(HEAD**-0.5)
            vm = jnp.where(mine, vb, BF16(0))
            s = mm(km, q_ref[...], NT) + mask
            p = jnp.exp(s - lse_ref[head : head + 1, :])
            dp = mm(vm, dctx_ref[...], NT)
            ds = (p * (dp - delta_ref[head : head + 1, :])).astype(BF16)
            dv = jnp.where(mine, mm(p.astype(BF16), dctx_ref[...], NN), dv)
            dk = jnp.where(mine, mm(ds, q_ref[...], NN), dk)
            columns = slice(head * HEAD, (head + 1) * HEAD)
            total_ref[columns, :] += mm(kt_ref[columns, rows], ds, NN)
        dkb = (dk * HEAD**-0.5).astype(BF16)
        dvb = dv.astype(BF16)
        grads_ref[1, rows, :] = dkb
        grads_ref[2, rows, :] = dvb
        return carry + row_sum(dvb.astype(F32))

    dv_sum = lax.fori_loop(0, length // TILE, block, jnp.zeros((1, GROUP), F32), unroll=True)
    dq = jnp.transpose(total_ref[...] * HEAD**-0.5).astype(BF16)
    grads_ref[0] = dq
    sums_ref[...] = jnp.zeros_like(sums_ref)
    sums_ref[0:1, :] = row_sum(dq.astype(F32))
    sums_ref[1:2, :] = dv_sum
    if others is not None:
        sums = (*before_refs, sums_ref) if before else ()
        projection_part(core_ref, h_ref, (*other_refs, grads_ref), sums, keep_ref, send_ref)


def attention_backward(g, q, k, v, dctx, ctx, lse, seg, weights, passes, after):
    length, width = q.shape
    rows = pl.BlockSpec((length, GROUP), lambda i: (0, g))
    pair_rows = pl.BlockSpec((2, length, UNIT), lambda i: (0, 0, g))
    operands = [q, k, v, dctx, ctx, lse, seg]
    specs = [
        rows,
        rows,
        rows,
        pair_rows,
        pair_rows,
        pl.BlockSpec((8, length), lambda i: (g, 0)),
        fixed((1, length)),
    ]
    kinds = [jax.ShapeDtypeStruct((3, length, GROUP), BF16), jax.ShapeDtypeStruct((8, GROUP), F32)]
    outs = [fixed((3, length, GROUP)), fixed((8, GROUP))]
    others, before = None, 0
    if weights:
        core, h, grads, sums = weights
        others, before = len(grads), len(sums)
        operands += [core, h, *grads, *sums]
        specs += [SCALAR] + [fixed(x.shape) for x in (h, *grads, *sums)]
        shape = (2, 2, 4, 3 * width // 16 + BIAS_ROWS, (others + 1) * UNIT)
        kinds += [jax.ShapeDtypeStruct(shape, BF16)] * 2
        outs += [fixed(shape)] * 2
    return run(
        functools.partial(attention_backward_kernel, others, before),
        "attention_backward",
        (1,),
        tuple(operands),
        specs,
        kinds,
        outs,
        [
            pltpu.VMEM((8, length), F32),
            pltpu.VMEM((GROUP, length), F32),
            pltpu.VMEM((GROUP, length), BF16),
            pltpu.VMEM((length, GROUP), BF16),
            pltpu.VMEM((length, 1), F32),
        ],
        passes=passes,
        after=after,
        micros=8,
    )


def hidden_total(fp_ref, d_refs, w_refs):
    total = fp_ref[...]
    for at, w_ref in enumerate(w_refs):
        d = lanes(*[ref[at, :, x * UNIT : (x + 1) * UNIT] for x in range(2) for ref in d_refs])
        total = total + mm(d, w_ref[...], NT)
    return total


def hidden_away_kernel(fp_ref, *refs):
    refs[6][...] = hidden_total(fp_ref, refs[:3], refs[3:6]).astype(BF16)


def hidden_home_kernel(here_ref, fp_ref, *refs):
    came0_ref, came1_ref, out_ref, layer_ref = refs[6:]
    out_ref[0] = hidden_total(fp_ref, refs[:3], refs[3:6])
    layer_ref[0] = jnp.where(pl.program_id(0) == 0, came0_ref[...], came1_ref[...])


def hidden_away(fp, d0, d1, d2, wq, wk, wv, passes, after):
    length, width = fp.shape
    half = length // 2
    steps = half // TILE
    return run(
        hidden_away_kernel,
        "hidden_away",
        (steps,),
        (fp, d0, d1, d2, wq, wk, wv),
        [
            pl.BlockSpec((TILE, width), lambda i: (i + steps, 0)),
        ]
        + [pl.BlockSpec((3, TILE, GROUP), lambda i: (0, i + steps, 0))] * 3
        + [fixed((width, width))] * 3,
        (jax.ShapeDtypeStruct((half, width), BF16),),
        (pl.BlockSpec((TILE, width), lambda i: (i, 0)),),
        passes=passes,
        after=after,
        micros=3,
    )


def hidden_home(here, fp, d0, d1, d2, wq, wk, wv, came0, came1, layer, passes, after):
    length, width = fp.shape
    half = length // 2
    steps = half // TILE
    return run(
        hidden_home_kernel,
        "hidden_home",
        (steps,),
        (here, fp, d0, d1, d2, wq, wk, wv, came0, came1),
        [
            pl.BlockSpec((TILE, width), lambda i, b: (i, 0)),
        ]
        + [pl.BlockSpec((3, TILE, GROUP), lambda i, b: (0, i, 0))] * 3
        + [fixed((width, width))] * 3
        + [fixed((TILE, width))] * 2,
        (
            jax.ShapeDtypeStruct((2, half, width), F32),
            jax.ShapeDtypeStruct((2, half, width), BF16),
        ),
        (
            pl.BlockSpec((1, TILE, width), lambda i, b: (b[0], i, 0)),
            pl.BlockSpec((1, TILE, width), lambda i, b: (1 - b[0], i, 0)),
        ),
        scalars=1,
        held={1: layer},
        passes=passes,
        after=after,
        micros=3,
    )


def place_kernel(here_ref, came_ref, out_ref):
    out_ref[0] = came_ref[...].astype(F32)


def place_far(here, came, grad, passes):
    half, width = came.shape
    return run(
        place_kernel,
        "place_far",
        (2,),
        (here, came),
        [pl.BlockSpec((half // 2, width), lambda i, b: (i, 0))],
        (jax.ShapeDtypeStruct((2, half, width), F32),),
        (pl.BlockSpec((1, half // 2, width), lambda i, b: (1 - b[0], i, 0)),),
        scalars=1,
        held={0: grad},
        passes=passes,
        micros=1,
    )


def fast(
    hidden,
    segments,
    query_matrix,
    query_bias,
    key_matrix,
    value_matrix,
    value_bias,
    output_matrix,
    output_bias,
    first_gain,
    first_shift,
    inner_matrix,
    inner_bias,
    outer_matrix,
    outer_bias,
    second_gain,
    second_shift,
    cotangent,
):
    here = lax.axis_index("blk")
    place = lax.axis_index("seq")
    core, y_at, z_at = place % 2, (place // 2) % 2, place // 4
    here_id = here.astype(jnp.int32)[None]
    core_id = core.astype(jnp.int32)[None]
    half, width = hidden.shape[1:]

    def pick(x, *at):
        start = at + (0,) * (x.ndim - len(at))
        size = (1,) * len(at) + x.shape[len(at) :]
        return lax.dynamic_slice(x, start, size).reshape(x.shape[len(at) :])

    def trade(x):
        return lax.ppermute(x, "blk", [(0, 1), (1, 0)])

    def seq_swap(x, bit):
        return lax.ppermute(x, "seq", [(i, i ^ bit) for i in range(16)])

    def row(x):
        return x.astype(F32)[None, :]

    at = jnp.stack([here, y_at, z_at]).astype(jnp.int32)

    def rounded(x):
        return lax.reduce_precision(x, 8, 7)

    def sum_0(state, *at):
        return rounded(pick(state[0], *at).astype(F32) + pick(state[1], *at).astype(F32))

    def sum_1(state, mine, *at):
        return rounded(sum_0(state, mine, *at) + pick(state[2], *at).astype(F32))

    def sum_2(state, mine, then, *at):
        return rounded(sum_1(state, mine, then, *at) + pick(state[3], *at).astype(F32))

    def send_z(parts):
        return [seq_swap(x, 4 * d) for d, x in zip((1, 2, 3), parts)]

    def add_z(total, parts):
        return (total + parts[0].astype(F32)) + (parts[1].astype(F32) + parts[2].astype(F32))

    seg = jnp.concatenate([pick(segments, here), trade(pick(segments, 1 - here))])[None, :]
    far = trade(pick(hidden, 1 - here))
    cot_far = trade(pick(cotangent, 1 - here + jnp.minimum(seg[0, -1], 0)))
    q, k, v, ctx, lse, h = attention_forward(
        here_id,
        hidden,
        far,
        query_matrix,
        key_matrix,
        value_matrix,
        row(query_bias),
        row(value_bias),
        seg,
    )
    empty = jnp.zeros((2, width), F32)
    vec = jnp.concatenate(
        [
            row(output_bias),
            row(first_gain),
            row(first_shift),
            row(outer_bias),
            row(second_gain),
            row(second_shift),
            empty,
        ],
        axis=0,
    )
    out, out_far0, out_far1, first, act, og, ig, fp, ag, dctx, sums, isum = token_pass(
        here_id, h, ctx, cotangent, cot_far, output_matrix, inner_matrix, outer_matrix, row(inner_bias), vec
    )
    x_mine, x_away, y_mine, y_away = here, 1 - here, y_at, 1 - y_at
    a_keep, a_send = outer_grad_call(core_id, act, og, sums, isum)
    a0 = seq_swap(a_send, 1)
    b_keep, b_send, a_keep = inner_grad_call(core_id, first, ig, ctx, ag, (a_keep,))
    b0 = seq_swap(b_send, 1)
    a = (a_keep, a0)
    a_away, out_far0 = halve_first(at, 1, a_keep, a0, (out_far0,))
    a1 = seq_swap(a_away, 2)
    out_came0 = trade(out_far0)
    b = (b_keep, b0)
    b_away = sum_0(b, x_away).astype(BF16)
    b1 = trade(b_away)
    bwd = (q, k, v, dctx, ctx, lse, seg)
    grads0, bias0 = attention_backward(0, *bwd, (), (), (a_away, b_away))
    grads1, bias1, c_keep, c_send, a_keep, b_keep, out_came0, out_far1 = attention_backward(
        1, *bwd, (core_id, h, (grads0,), ()), (a_keep, b_keep, out_came0, out_far1), ()
    )
    out_came1 = trade(out_far1)
    c0 = seq_swap(c_send, 1)
    a = (a_keep, a0, a1)
    a_away = sum_1(a, y_mine, x_away).astype(BF16)
    a2 = trade(a_away)
    b = (b_keep, b0, b1)
    b_away = sum_1(b, x_mine, y_away).astype(BF16)
    b2 = seq_swap(b_away, 2)
    grads2, _, d_keep, d_send, a_keep, b_keep, c_keep = attention_backward(
        2, *bwd, (core_id, h, (), (bias0, bias1)), (a_keep, b_keep, c_keep), (a_away, b_away)
    )
    d0 = seq_swap(d_send, 1)
    c = (c_keep, c0)
    c_away = sum_0(c, y_away).astype(BF16)
    c1 = seq_swap(c_away, 2)

    def flat(x):
        return x.reshape(*x.shape[:-3], -1, x.shape[-1])

    a_rows, b_rows = a_keep.shape[3], 5 * width // 16
    states = [
        (a_keep, a0, a1, a2, 1, 0, 0),
        (flat(b_keep), flat(b0), flat(b1), flat(b2), 0, a_rows, 0),
    ]
    ab_mine, *parts, out_came1, d_keep = quarter(
        at, states, a_rows + b_rows, width // 2, (out_came1, d_keep), (c_away,)
    )
    ab3 = send_z(parts)
    args = (fp, grads0, grads1, grads2, query_matrix, key_matrix, value_matrix)
    d = (d_keep, d0)
    d_away = sum_0(d, y_away).astype(BF16)
    d1 = seq_swap(d_away, 2)
    hidden_grad, layer_out, c_keep, d_keep = hidden_home(
        here_id, *args, out_came0, out_came1, out, (c_keep, d_keep), (d_away,)
    )
    c = (c_keep, c0, c1)
    d = (d_keep, d0, d1)

    def lanes_of(*parts):
        return jnp.concatenate(parts, axis=-1)

    def late_1(*at):
        return lanes_of(sum_1(c, y_mine, *at), sum_1(d, y_mine, *at))

    e_away = late_1(x_away).astype(BF16)
    e2 = trade(e_away)
    far_grad, c_keep, d_keep, ab_mine = hidden_away(*args, (c_keep, d_keep, ab_mine), (e_away,))
    came = trade(far_grad)
    c = (c_keep, c0, c1)
    d = (d_keep, d0, d1)

    def late_2(z):
        return rounded(late_1(x_mine, z) + pick(e2, z).astype(F32))

    e3 = send_z([late_2(z_at ^ e).astype(BF16) for e in (1, 2, 3)])
    early = add_z(ab_mine.astype(F32), ab3)
    hidden_grad = place_far(here_id, came, hidden_grad, ())[0]
    late = add_z(late_2(z_at), e3)
    rows = width // 16
    outer_rows = 4 * rows
    outer_grad = early[:outer_rows]
    vectors = early[outer_rows : outer_rows + VECTOR_ROWS].reshape(-1, width)
    inner_all = early[outer_rows + VECTOR_ROWS :].reshape(5, rows, width // 2)
    output_grad = inner_all[4]
    inner_grad = jnp.transpose(inner_all[:4], (1, 0, 2)).reshape(rows, -1)
    units = width // UNIT
    biases = late[3 * rows :, 2 * UNIT :][: 2 * units].reshape(2, units // 2, 2, UNIT)
    biases = jnp.transpose(biases, (0, 2, 1, 3)).reshape(2, width)
    return (
        layer_out,
        hidden_grad,
        late[:rows],
        biases[0],
        late[rows : 2 * rows],
        late[2 * rows : 3 * rows],
        biases[1],
        output_grad,
        vectors[5],
        vectors[3],
        vectors[4],
        inner_grad,
        vectors[6:10].reshape(-1),
        outer_grad,
        vectors[2],
        vectors[0],
        vectors[1],
    )


def choose(sizes, *args):
    seq_count, row_count, width = args[0].shape
    whole_here = sizes[1] == 2 and seq_count == 2 and row_count == 2 * TILE and width == 3 * GROUP
    return fast(*args) if whole_here and sizes[0] == 16 else general(*args)


def solution(mesh):
    sizes = (mesh.shape["seq"], mesh.shape["blk"])
    return jax.shard_map(
        functools.partial(choose, sizes),
        mesh=mesh,
        in_specs=(
            P("seq", "blk", None),
            P("seq", "blk"),
            P(),
            P(),
            P(),
            P(),
            P(),
            P(),
            P(),
            P(),
            P(),
            P(),
            P(),
            P(),
            P(),
            P(),
            P(),
            P("seq", "blk", None),
        ),
        out_specs=(
            P("seq", "blk", None),
            P("seq", "blk", None),
            P("seq", "blk"),
            P(),
            P("seq", "blk"),
            P("seq", "blk"),
            P(),
            P("seq", "blk"),
            P(),
            P(),
            P(),
            P("seq", "blk"),
            P(),
            P("seq", "blk"),
            P(),
            P(),
            P(),
        ),
        check_vma=False,
    )
```

```python
import functools
import math

import jax
import jax.numpy as jnp
from jax import lax
from jax.experimental import pallas as pl
from jax.experimental.pallas import tpu as pltpu
from jax.sharding import PartitionSpec as P

HEADS = 12
HEAD = 64


NEGATIVE = -1e30
EPSILON = 1e-12


def layer_norm(values, norm_gain, norm_shift):
    centre = values - jnp.mean(values, axis=-1, keepdims=True)
    spread = jnp.mean(centre * centre, axis=-1, keepdims=True)
    return centre * lax.rsqrt(spread + EPSILON) * norm_gain + norm_shift


def gelu_exact(values):
    return jax.nn.gelu(values, approximate=False)


def linear(operand, matrix):
    return jnp.dot(operand, matrix, preferred_element_type=jnp.float32)


def split_heads(values):
    return values.reshape(values.shape[0], values.shape[1], HEADS, HEAD)


def block_scores(query_block, key_block, score_scale):
    return (
        jnp.einsum("sqhd,skhd->shqk", query_block, key_block, preferred_element_type=jnp.float32)
        * score_scale
    )


def attention_grads(
    query_block, key_block, value_block, dctx_block, same_doc, log_total, row_delta, score_scale
):
    attn_probs = jnp.where(
        same_doc,
        jnp.exp(block_scores(query_block, key_block, score_scale) - log_total[..., None]),
        0.0,
    )
    slopes = jnp.einsum(
        "sqhd,skhd->shqk", dctx_block, value_block, preferred_element_type=jnp.float32
    )
    return (attn_probs, (attn_probs * (slopes - row_delta[..., None])).astype(jnp.bfloat16))


def over_blocks(length, step, initial):
    block_size = math.gcd(length, 512)

    def scan_step(carried, block_index):
        return (step(carried, block_index * block_size, block_size), None)

    result, unused = lax.scan(scan_step, initial, jnp.arange(length // block_size, dtype=jnp.int32))
    return result


def general(
    hidden,
    segments,
    query_matrix,
    query_bias,
    key_matrix,
    value_matrix,
    value_bias,
    output_matrix,
    output_bias,
    first_gain,
    first_shift,
    inner_matrix,
    inner_bias,
    outer_matrix,
    outer_bias,
    second_gain,
    second_shift,
    cotangent,
):
    seq_count, row_count, model_width = hidden.shape
    score_scale = HEAD ** (-0.5)
    single_float = jnp.float32
    bf16 = jnp.bfloat16
    queries = (linear(hidden, query_matrix) + query_bias.astype(single_float)).astype(bf16)
    key_proj = linear(hidden, key_matrix).astype(bf16)
    value_proj = (linear(hidden, value_matrix) + value_bias.astype(single_float)).astype(bf16)
    seg_all = lax.all_gather(segments, "blk", axis=1, tiled=True)
    keys_all, values_all = (
        lax.all_gather(key_proj, "blk", axis=1, tiled=True),
        lax.all_gather(value_proj, "blk", axis=1, tiled=True),
    )
    length = seg_all.shape[1]
    query_heads = split_heads(queries)
    key_heads = split_heads(keys_all)
    value_heads = split_heads(values_all)

    def key_slices(offset, block_size):
        key_segs = lax.dynamic_slice_in_dim(seg_all, offset, block_size, 1)
        same_doc = (segments[:, :, None] == key_segs[:, None, :])[:, None]
        key_block = lax.dynamic_slice_in_dim(key_heads, offset, block_size, 1)
        value_block = lax.dynamic_slice_in_dim(value_heads, offset, block_size, 1)
        return (same_doc, key_block, value_block)

    def stats_step(carried, offset, block_size):
        same_doc, key_block, value_block = key_slices(offset, block_size)
        running_max, running_sum = carried
        scores = jnp.where(same_doc, block_scores(query_heads, key_block, score_scale), NEGATIVE)
        higher = jnp.maximum(running_max, jnp.max(scores, axis=-1))
        weights = jnp.where(same_doc, jnp.exp(scores - higher[..., None]), 0.0)
        return (higher, running_sum * jnp.exp(running_max - higher) + jnp.sum(weights, axis=-1))

    stat_shape = (seq_count, HEADS, row_count)
    running_max, running_sum = over_blocks(
        length,
        stats_step,
        (jnp.full(stat_shape, NEGATIVE, single_float), jnp.zeros(stat_shape, single_float)),
    )
    log_total = running_max + jnp.log(running_sum)

    def context_step(carried, offset, block_size):
        same_doc, key_block, value_block = key_slices(offset, block_size)
        attn_probs = jnp.where(
            same_doc,
            jnp.exp(block_scores(query_heads, key_block, score_scale) - log_total[..., None]),
            0.0,
        )
        return carried + jnp.einsum(
            "shqk,skhd->sqhd",
            attn_probs.astype(bf16),
            value_block,
            preferred_element_type=single_float,
        )

    head_zeros = jnp.zeros((seq_count, row_count, HEADS, HEAD), single_float)
    context = over_blocks(length, context_step, head_zeros)
    context_reduced = context.reshape(seq_count, row_count, model_width).astype(bf16)
    attn_out = linear(context_reduced, output_matrix) + output_bias.astype(single_float)
    first_pre = hidden.astype(single_float) + attn_out
    first_norm, first_back = jax.vjp(
        layer_norm, first_pre, first_gain.astype(single_float), first_shift.astype(single_float)
    )
    first_reduced = first_norm.astype(bf16)
    inner = linear(first_reduced, inner_matrix) + inner_bias.astype(single_float)
    act_full, gelu_back = jax.vjp(gelu_exact, inner)
    activation_reduced = act_full.astype(bf16)
    outer = linear(activation_reduced, outer_matrix) + outer_bias.astype(single_float)
    layer_full, second_back = jax.vjp(
        layer_norm,
        first_norm + outer,
        second_gain.astype(single_float),
        second_shift.astype(single_float),
    )
    layer_out = layer_full.astype(bf16)
    second_pre_grad, second_gain_grad, second_shift_grad = second_back(
        cotangent.astype(single_float)
    )
    outer_gradient_reduced = second_pre_grad.astype(bf16)
    outer_weight_grad = jnp.einsum(
        "gvx,gvm->xm",
        activation_reduced,
        outer_gradient_reduced,
        preferred_element_type=single_float,
    )
    outer_bias_grad = jnp.sum(outer_gradient_reduced.astype(single_float), axis=(0, 1))
    activation_gradient = jnp.einsum(
        "rzo,uo->rzu", outer_gradient_reduced, outer_matrix, preferred_element_type=single_float
    )
    inner_gradient_reduced = gelu_back(activation_gradient)[0].astype(bf16)
    inner_weight_grad = jnp.einsum(
        "ret,reu->tu", first_reduced, inner_gradient_reduced, preferred_element_type=single_float
    )
    inner_bias_grad = jnp.sum(inner_gradient_reduced.astype(single_float), axis=(0, 1))
    first_norm_grad = second_pre_grad + jnp.einsum(
        "aoi,ni->aon", inner_gradient_reduced, inner_matrix, preferred_element_type=single_float
    )
    first_pre_grad, first_gain_grad, first_shift_grad = first_back(first_norm_grad)
    attention_gradient_reduced = first_pre_grad.astype(bf16)
    output_weight_grad = jnp.einsum(
        "tfm,tfc->mc",
        context_reduced,
        attention_gradient_reduced,
        preferred_element_type=single_float,
    )
    output_bias_grad = jnp.sum(attention_gradient_reduced.astype(single_float), axis=(0, 1))
    dctx_low = jnp.einsum(
        "upx,cx->upc",
        attention_gradient_reduced,
        output_matrix,
        preferred_element_type=single_float,
    ).astype(bf16)
    dctx_heads = split_heads(dctx_low)
    row_delta = jnp.transpose(
        jnp.sum(dctx_heads.astype(single_float) * context, axis=-1), (0, 2, 1)
    )

    def query_step(carried, offset, block_size):
        same_doc, key_block, value_block = key_slices(offset, block_size)
        attn_probs, dscores = attention_grads(
            query_heads,
            key_block,
            value_block,
            dctx_heads,
            same_doc,
            log_total,
            row_delta,
            score_scale,
        )
        return carried + score_scale * jnp.einsum(
            "shqk,skhd->sqhd", dscores, key_block, preferred_element_type=single_float
        )

    query_grad = over_blocks(length, query_step, head_zeros)
    query_all, dctx_all = (
        lax.all_gather(queries, "blk", axis=1, tiled=True),
        lax.all_gather(dctx_low, "blk", axis=1, tiled=True),
    )
    lse_all, delta_all = (
        lax.all_gather(log_total, "blk", axis=2, tiled=True),
        lax.all_gather(row_delta, "blk", axis=2, tiled=True),
    )
    query_all_heads = split_heads(query_all)
    dctx_all_heads = split_heads(dctx_all)
    own_keys = split_heads(key_proj)
    own_values = split_heads(value_proj)

    def key_step(carried, offset, block_size):
        query_segs = lax.dynamic_slice_in_dim(seg_all, offset, block_size, 1)
        same_doc = (query_segs[:, :, None] == segments[:, None, :])[:, None]
        query_block = lax.dynamic_slice_in_dim(query_all_heads, offset, block_size, 1)
        dctx_block = lax.dynamic_slice_in_dim(dctx_all_heads, offset, block_size, 1)
        lse_block = lax.dynamic_slice_in_dim(lse_all, offset, block_size, 2)
        delta_block = lax.dynamic_slice_in_dim(delta_all, offset, block_size, 2)
        key_sum, value_sum = carried
        attn_probs, dscores = attention_grads(
            query_block,
            own_keys,
            own_values,
            dctx_block,
            same_doc,
            lse_block,
            delta_block,
            score_scale,
        )
        key_sum = key_sum + score_scale * jnp.einsum(
            "shqk,sqhd->skhd", dscores, query_block, preferred_element_type=single_float
        )
        value_sum = value_sum + jnp.einsum(
            "shqk,sqhd->skhd",
            attn_probs.astype(bf16),
            dctx_block,
            preferred_element_type=single_float,
        )
        return (key_sum, value_sum)

    key_grad, value_grad = over_blocks(length, key_step, (head_zeros, head_zeros))
    query_gradient_reduced = query_grad.reshape(seq_count, row_count, model_width).astype(bf16)
    key_gradient_reduced = key_grad.reshape(seq_count, row_count, model_width).astype(bf16)
    value_gradient_reduced = value_grad.reshape(seq_count, row_count, model_width).astype(bf16)
    query_weight_grad = jnp.einsum(
        "tfm,tfc->mc", hidden, query_gradient_reduced, preferred_element_type=single_float
    )
    query_bias_grad = jnp.sum(query_gradient_reduced.astype(single_float), axis=(0, 1))
    key_matrix_gradient = jnp.einsum(
        "tfm,tfc->mc", hidden, key_gradient_reduced, preferred_element_type=single_float
    )
    value_weight_grad = jnp.einsum(
        "tfm,tfc->mc", hidden, value_gradient_reduced, preferred_element_type=single_float
    )
    value_bias_grad = jnp.sum(value_gradient_reduced.astype(single_float), axis=(0, 1))
    hidden_grad = first_pre_grad + jnp.einsum(
        "upx,cx->upc", query_gradient_reduced, query_matrix, preferred_element_type=single_float
    )
    hidden_grad = hidden_grad + jnp.einsum(
        "upx,cx->upc", key_gradient_reduced, key_matrix, preferred_element_type=single_float
    )
    hidden_grad = hidden_grad + jnp.einsum(
        "upx,cx->upc", value_gradient_reduced, value_matrix, preferred_element_type=single_float
    )
    partial_sums = (
        lax.psum_scatter(query_weight_grad, "seq", scatter_dimension=0, tiled=True),
        lax.psum_scatter(key_matrix_gradient, "seq", scatter_dimension=0, tiled=True),
        lax.psum_scatter(value_weight_grad, "seq", scatter_dimension=0, tiled=True),
        lax.psum_scatter(output_weight_grad, "seq", scatter_dimension=0, tiled=True),
        lax.psum_scatter(inner_weight_grad, "seq", scatter_dimension=0, tiled=True),
        lax.psum_scatter(outer_weight_grad, "seq", scatter_dimension=0, tiled=True),
    )
    matrices = lax.psum_scatter(tuple(partial_sums), "blk", scatter_dimension=1, tiled=True)
    vectors = lax.psum(
        (
            query_bias_grad,
            value_bias_grad,
            output_bias_grad,
            first_gain_grad,
            first_shift_grad,
            inner_bias_grad,
            outer_bias_grad,
            second_gain_grad,
            second_shift_grad,
        ),
        ("seq", "blk"),
    )
    return (
        layer_out,
        hidden_grad,
        matrices[0],
        vectors[0],
        matrices[1],
        matrices[2],
        vectors[1],
        matrices[3],
        vectors[2],
        vectors[3],
        vectors[4],
        matrices[4],
        vectors[5],
        matrices[5],
        vectors[6],
        vectors[7],
        vectors[8],
    )


BF16 = jnp.bfloat16
F32 = jnp.float32
NN = ((1,), (0,))
NT = ((1,), (1,))
TN = ((0,), (0,))
UNIT = 128
GROUP = 256
PER_GROUP = GROUP // HEAD
TILE = 256
TOKENS = 512
VMEM_LIMIT = 60 * 2**20
SCALAR = pl.BlockSpec(memory_space=pltpu.SMEM)
ANY = pl.BlockSpec(memory_space=pl.ANY)


def mm(a, b, dims):
    return lax.dot_general(a, b, (dims, ((), ())), preferred_element_type=F32)


def fixed(shape):
    return pl.BlockSpec(shape, lambda *_: (0,) * len(shape), pipeline_mode=pl.Buffered(1))


def run(
    kernel,
    name,
    grid,
    operands,
    in_specs,
    out_shape,
    out_specs,
    scratch=(),
    scalars=0,
    held=None,
    passes=(),
    after=(),
    micros=1,
):
    held = held or {}
    out_shape, out_specs = list(out_shape), list(out_specs)
    n_in, n_out, n_held, n_pass = len(operands), len(out_shape), len(held), len(passes)
    aliases = {n_in + i: at for i, at in enumerate(held)}
    aliases |= {n_in + n_held + i: n_out + i for i in range(n_pass)}

    def body(*refs):
        outs = n_in + n_held + n_pass + len(after)
        kernel(*refs[:n_in], *refs[outs : outs + n_out], *refs[outs + n_out + n_pass :])

    result = pl.pallas_call(
        body,
        grid_spec=pltpu.PrefetchScalarGridSpec(
            num_scalar_prefetch=scalars,
            grid=grid,
            in_specs=list(in_specs) + [ANY] * (n_held + n_pass + len(after)),
            out_specs=out_specs + [ANY] * n_pass,
            scratch_shapes=list(scratch),
        ),
        out_shape=out_shape + [jax.ShapeDtypeStruct(x.shape, x.dtype) for x in passes],
        input_output_aliases=aliases,
        compiler_params=pltpu.CompilerParams(
            vmem_limit_bytes=VMEM_LIMIT, dimension_semantics=("arbitrary",) * len(grid)
        ),
        cost_estimate=pl.CostEstimate(
            flops=int(micros * 1e10), bytes_accessed=1, transcendentals=0
        ),
        name=name,
    )(*operands, *held.values(), *passes, *after)
    return result


def head_lanes(shape, head):
    lane = lax.broadcasted_iota(jnp.int32, shape, 1)
    return (lane >= head * HEAD) & (lane < (head + 1) * HEAD)


def lanes(*parts):
    return jnp.concatenate(parts, axis=1)


def column_of(row):
    return jnp.transpose(jnp.broadcast_to(row.astype(F32), (UNIT, row.shape[1])))[:, 0:1]


def same_pair(row, column, rows):
    return jnp.where(column[rows] == row, 0.0, NEGATIVE)


def attention_forward_kernel(
    here_ref,
    own_ref,
    far_ref,
    wq0_ref,
    wq1_ref,
    wk0_ref,
    wk1_ref,
    wv0_ref,
    wv1_ref,
    bq0_ref,
    bq1_ref,
    bv0_ref,
    bv1_ref,
    seg_ref,
    q_ref,
    k_ref,
    v_ref,
    ctx_ref,
    lse_ref,
    h_ref,
    mask_ref,
    vaug_ref,
):
    half = far_ref.shape[0]
    length = 2 * half

    @pl.when(pl.program_id(0) == 0)
    def _():
        segr = seg_ref[...].astype(F32)
        mask_ref[...] = jnp.where(column_of(segr) == segr, 0.0, NEGATIVE)
        h_ref[0:half, :] = own_ref[0]
        h_ref[half:, :] = far_ref[...]

    h = h_ref[...]
    bias_q = lanes(bq0_ref[...], bq1_ref[...])
    bias_v = lanes(bv0_ref[...], bv1_ref[...])
    q_ref[...] = (mm(h, lanes(wq0_ref[...], wq1_ref[...]), NN) + bias_q).astype(BF16)
    k_ref[...] = mm(h, lanes(wk0_ref[...], wk1_ref[...]), NN).astype(BF16)
    v = (mm(h, lanes(wv0_ref[...], wv1_ref[...]), NN) + bias_v).astype(BF16)
    v_ref[...] = v
    lane = lax.broadcasted_iota(jnp.int32, v.shape, 1)
    for head in range(PER_GROUP):
        other = (lane // UNIT) != (head // 2)
        filler = jnp.where(other, 1.0, 0.0).astype(BF16)
        vaug_ref[head] = jnp.where(head_lanes(v.shape, head), v, filler)

    def block(i, carry):
        rows = pl.ds(pl.multiple_of(i * TILE, TILE), TILE)
        qb = q_ref[rows, :] * BF16(HEAD**-0.5)
        halves = [None, None]
        stat_lane = lax.broadcasted_iota(jnp.int32, (TILE, UNIT), 1)
        stats = jnp.zeros((TILE, UNIT), F32)
        for head in range(PER_GROUP):
            qm = jnp.where(head_lanes(qb.shape, head), qb, BF16(0))
            s = mm(qm, k_ref[...], NT) + mask_ref[rows, :]
            top = jnp.max(s, axis=1, keepdims=True)
            e = jnp.exp(s - top).astype(BF16)
            o = mm(e, vaug_ref[head], NN)
            t = head // 2
            total = o[:, (1 - t) * UNIT : (2 - t) * UNIT]
            part = o[:, t * UNIT : (t + 1) * UNIT] / total
            halves[t] = part if halves[t] is None else halves[t] + part
            stats = jnp.where(stat_lane == head, top + jnp.log(total), stats)
        ctx_ref[0, rows, :] = halves[0].astype(BF16)
        ctx_ref[1, rows, :] = halves[1].astype(BF16)
        lse_ref[:, rows] = jnp.transpose(stats)[0:8]
        return carry

    lax.fori_loop(0, length // TILE, block, 0, unroll=True)


def attention_forward(here, hidden, far, wq, wk, wv, bq, bv, seg):
    half, width = far.shape
    length = 2 * half
    groups = width // GROUP
    left = pl.BlockSpec((width, UNIT), lambda g, h: (0, g))
    right = pl.BlockSpec((width, UNIT), lambda g, h: (0, groups + g))
    bias_left = pl.BlockSpec((1, UNIT), lambda g, h: (0, g))
    bias_right = pl.BlockSpec((1, UNIT), lambda g, h: (0, groups + g))
    rows = pl.BlockSpec((length, GROUP), lambda g, h: (0, g))
    wide = jax.ShapeDtypeStruct((length, width), BF16)
    own = pl.BlockSpec((1, half, width), lambda g, h: (h[0], 0, 0), pipeline_mode=pl.Buffered(1))
    return run(
        attention_forward_kernel,
        "attention_forward",
        (groups,),
        (here, hidden, far, wq, wq, wk, wk, wv, wv, bq, bq, bv, bv, seg),
        [own, fixed((half, width))]
        + [left, right] * 3
        + [bias_left, bias_right] * 2
        + [fixed((1, length))],
        (
            wide,
            wide,
            wide,
            jax.ShapeDtypeStruct((2, length, width // 2), BF16),
            jax.ShapeDtypeStruct((8 * groups, length), F32),
            wide,
        ),
        (
            rows,
            rows,
            rows,
            pl.BlockSpec((2, length, UNIT), lambda g, h: (0, 0, g)),
            pl.BlockSpec((8, length), lambda g, h: (g, 0)),
            pl.BlockSpec((length, width), lambda g, h: (0, 0)),
        ),
        [pltpu.VMEM((length, length), F32), pltpu.VMEM((PER_GROUP, length, GROUP), BF16)],
        scalars=1,
        micros=16,
    )


def gelu_pair(u):
    phi = 0.5 + 0.5 * lax.erf(u * 0.7071067811865476)
    bell = jnp.exp2(u * u * -0.7213475204444817)
    return (u * phi, phi + u * bell * 0.3989422804014327)


def normed(x):
    centre = x - jnp.mean(x, axis=1, keepdims=True)
    scale = lax.rsqrt(jnp.mean(centre * centre, axis=1, keepdims=True) + EPSILON)
    return (centre * scale, scale)


def norm_back(u, n, scale):
    return scale * (u - jnp.mean(u, axis=1, keepdims=True) - n * jnp.mean(u * n, axis=1, keepdims=True))


def row_sum(x):
    return jnp.sum(x, axis=0, keepdims=True)


def token_kernel(
    here_ref,
    h_ref,
    ctx_ref,
    cot_own_ref,
    cot_far_ref,
    wo_ref,
    wi_ref,
    wp_ref,
    bi_ref,
    vec_ref,
    out_ref,
    far0_ref,
    far1_ref,
    first_ref,
    act_ref,
    og_ref,
    ig_ref,
    fp_ref,
    ag_ref,
    dctx_ref,
    sums_ref,
    isum_ref,
    slope_ref,
):
    step = pl.program_id(0)
    steps = pl.num_programs(0)

    @pl.when(step == 0)
    def _():
        sums_ref[...] = jnp.zeros_like(sums_ref)
        isum_ref[...] = jnp.zeros_like(isum_ref)

    ff = wi_ref.shape[1]
    chunk = 512
    output_bias, gain1, shift1 = vec_ref[0:1, :], vec_ref[1:2, :], vec_ref[2:3, :]
    outer_bias, gain2, shift2 = vec_ref[3:4, :], vec_ref[4:5, :], vec_ref[5:6, :]
    middle = wo_ref.shape[0] // 2
    near = step < steps // 2

    def part(rows):
        ctx = lanes(ctx_ref[0, rows, :], ctx_ref[1, rows, :])
        x = h_ref[rows, :].astype(F32) + mm(ctx, wo_ref[...], NN) + output_bias
        yield
        n1, r1 = normed(x)
        fn = n1 * gain1 + shift1
        first = fn.astype(BF16)
        first_ref[rows, :] = first
        yield
        for c in range(0, ff, chunk):
            act, slope = gelu_pair(mm(first, wi_ref[:, c : c + chunk], NN) + bi_ref[:, c : c + chunk])
            act_ref[rows, c : c + chunk] = act.astype(BF16)
            slope_ref[rows, c : c + chunk] = slope
            yield
        x = fn + mm(act_ref[rows, :], wp_ref[...], NN) + outer_bias
        yield
        n2, r2 = normed(x)
        out = (n2 * gain2 + shift2).astype(BF16)

        out_ref[0, rows, :] = jnp.where(near, out, out_ref[0, rows, :])
        (far1_ref if rows.start else far0_ref)[...] = out
        e = jnp.where(near, cot_own_ref[0, rows, :], cot_far_ref[rows, :]).astype(F32)
        sums_ref[0:1, :] += row_sum(e * n2)
        sums_ref[1:2, :] += row_sum(e)
        sp = norm_back(e * gain2, n2, r2)
        og = sp.astype(BF16)
        og_ref[rows, :] = og
        sums_ref[2:3, :] += row_sum(og.astype(F32))
        yield
        for c in range(0, ff, chunk):
            ig = (mm(og, wp_ref[c : c + chunk, :], NT) * slope_ref[rows, c : c + chunk]).astype(BF16)
            ig_ref[rows, c : c + chunk] = ig
            isum_ref[:, c : c + chunk] += row_sum(ig.astype(F32))
            yield
        d = sp + mm(ig_ref[rows, :], wi_ref[...], NT)
        yield
        sums_ref[3:4, :] += row_sum(d * n1)
        sums_ref[4:5, :] += row_sum(d)
        fp = norm_back(d * gain1, n1, r1)
        fp_ref[rows, :] = fp
        ag = fp.astype(BF16)
        ag_ref[rows, :] = ag
        sums_ref[5:6, :] += row_sum(ag.astype(F32))
        yield
        dctx = mm(ag, wo_ref[...], NT).astype(BF16)
        dctx_ref[0, rows, :] = dctx[:, :middle]
        dctx_ref[1, rows, :] = dctx[:, middle:]

    size = h_ref.shape[0]
    parts = [part(slice(r, r + TILE)) for r in range(0, size, TILE)]
    live, waiting = [], list(parts)
    while waiting or live:
        if waiting:
            live.append(waiting.pop(0))
        live = [p for p in live if next(p, 0) is None]


def token_pass(here, h, ctx, cot, cot_far, wo, wi, wp, bi, vec):
    length, width = h.shape
    half = length // 2
    ff = wi.shape[1]
    steps = length // TOKENS
    near = steps // 2
    rows = pl.BlockSpec((TOKENS, width), lambda i, b: (i, 0))
    split_rows = pl.BlockSpec((2, TOKENS, width // 2), lambda i, b: (0, i, 0))
    wide_rows = pl.BlockSpec((TOKENS, ff), lambda i, b: (i, 0))
    own_rows = pl.BlockSpec((1, TOKENS, width), lambda i, b: (b[0], jnp.minimum(i, near - 1), 0))
    far_rows = pl.BlockSpec((TOKENS, width), lambda i, b: (jnp.maximum(i - near, 0), 0))
    low = jax.ShapeDtypeStruct((length, width), BF16)
    low_ff = jax.ShapeDtypeStruct((length, ff), BF16)
    return run(
        token_kernel,
        "token_pass",
        (steps,),
        (here, h, ctx, cot, cot_far, wo, wi, wp, bi, vec),
        [
            rows,
            split_rows,
            own_rows,
            far_rows,
            fixed((width, width)),
            fixed((width, ff)),
            fixed((ff, width)),
            fixed((1, ff)),
            fixed((8, width)),
        ],
        (
            jax.ShapeDtypeStruct((2, half, width), BF16),
            jax.ShapeDtypeStruct((half // 2, width), BF16),
            jax.ShapeDtypeStruct((half // 2, width), BF16),
            low,
            low_ff,
            low,
            low_ff,
            jax.ShapeDtypeStruct((length, width), F32),
            low,
            jax.ShapeDtypeStruct((2, length, width // 2), BF16),
            jax.ShapeDtypeStruct((8, width), F32),
            jax.ShapeDtypeStruct((1, ff), F32),
        ),
        (
            own_rows,
            pl.BlockSpec((half // 2, width), lambda i, b: (0, 0)),
            pl.BlockSpec((half // 2, width), lambda i, b: (0, 0)),
            rows,
            wide_rows,
            rows,
            wide_rows,
            rows,
            rows,
            split_rows,
            pl.BlockSpec((8, width), lambda i, b: (0, 0)),
            pl.BlockSpec((1, ff), lambda i, b: (0, 0)),
        ),
        [pltpu.VMEM((TOKENS, ff), F32)],
        scalars=1,
        micros=23,
    )


def put_pairs(a, b, core_ref, keep_ref, send_ref, columns, rows, count):
    even = core_ref[0] == 0
    for z in range(count):
        if z % 2 == 0:
            res = mm(a[:, 4 * z * rows : 4 * (z + 2) * rows], b, TN)
        for y in range(2):
            base = (z % 2 * 2 + y) * 2 * rows
            for x in range(2):
                zero = lanes(*[res[base : base + rows, c] for c in columns[x]])
                one = lanes(*[res[base + rows : base + 2 * rows, c] for c in columns[x]])
                keep_ref[x, y, z, 0] = jnp.where(even, zero, one).astype(BF16)
                send_ref[x, y, z, 0] = jnp.where(even, one, zero).astype(BF16)


HALVES = ((slice(0, 384),), (slice(384, 768),))
VECTOR_ROWS = 32
BIAS_ROWS = 16


def outer_grad_kernel(core_ref, act_ref, og_ref, sums_ref, isum_ref, keep_ref, send_ref, rows_ref):
    middle = og_ref.shape[1] // 2
    rows = act_ref.shape[1] // 4
    even = core_ref[0] == 0
    rows_ref[...] = jnp.zeros_like(rows_ref)
    at = 0
    for r in range(6):
        for x in range(2):
            rows_ref[at : at + 1, :] = sums_ref[r : r + 1, x * middle : (x + 1) * middle]
            at += 1
    for r in range(isum_ref.shape[1] // middle):
        rows_ref[at : at + 1, :] = isum_ref[:, r * middle : (r + 1) * middle]
        at += 1
    extra = rows_ref[...].astype(BF16)
    for y in range(2):
        res = mm(act_ref[:, 2 * y * rows : 2 * (y + 1) * rows], og_ref[...], TN)
        for x in range(2):
            columns = slice(x * middle, (x + 1) * middle)
            zero = res[0:rows, columns]
            one = res[rows:, columns]
            keep_ref[y, x, 0, 0:rows, :] = jnp.where(even, zero, one).astype(BF16)
            send_ref[y, x, 0, 0:rows, :] = jnp.where(even, one, zero).astype(BF16)
            keep_ref[y, x, 0, rows:, :] = extra
            send_ref[y, x, 0, rows:, :] = extra


def pair_out(shape, block, index):
    kind = jax.ShapeDtypeStruct(shape, BF16)
    spec = pl.BlockSpec(block, index)
    return ((kind, kind), (spec, spec))


def outer_grad_call(core, act, og, sums, isum):
    length, ff = act.shape
    width = og.shape[1]
    shape = (2, 2, 4, ff // 16 + VECTOR_ROWS, width // 2)
    kinds, specs = pair_out(shape, (2, 2, 1) + shape[3:], lambda z: (0, 0, z, 0, 0))
    return run(
        outer_grad_kernel,
        "outer_grad",
        (4,),
        (core, act, og, sums, isum),
        [
            SCALAR,
            pl.BlockSpec((length, ff // 4), lambda z: (0, z)),
            fixed((length, width)),
            fixed(sums.shape),
            fixed(isum.shape),
        ],
        kinds,
        specs,
        [pltpu.VMEM((VECTOR_ROWS, width // 2), F32)],
        micros=4.5,
    )


def inner_grad_kernel(
    core_ref, first_ref, low_ref, high_ref, ctx_ref, ag_ref, keep_ref, send_ref
):
    step = pl.program_id(0)
    rows = keep_ref.shape[4]

    @pl.when(step < 4)
    def _():
        both = lanes(low_ref[...], high_ref[...])
        put_pairs(first_ref[...], both, core_ref, keep_ref, send_ref, HALVES, rows, 4)

    @pl.when(step == 4)
    def _():
        ctx = lanes(ctx_ref[0], ctx_ref[1])
        put_pairs(ctx, ag_ref[...], core_ref, keep_ref, send_ref, HALVES, rows, 4)


def inner_grad_call(core, first, ig, ctx, ag, passes):
    length, width = first.shape
    shape = (2, 2, 4, 5, width // 16, width // 2)
    kinds, specs = pair_out(shape, shape[:3] + (1,) + shape[4:], lambda s: (0, 0, 0, s, 0, 0))
    return run(
        inner_grad_kernel,
        "inner_grad",
        (5,),
        (core, first, ig, ig, ctx, ag),
        [
            SCALAR,
            fixed((length, width)),
            pl.BlockSpec((length, width // 2), lambda s: (0, jnp.minimum(s, 3))),
            pl.BlockSpec((length, width // 2), lambda s: (0, 4 + jnp.minimum(s, 3))),
            fixed((2, length, width // 2)),
            fixed((length, width)),
        ],
        kinds,
        specs,
        passes=passes,
        micros=6,
    )


def rounded(x):
    return x.astype(BF16).astype(F32)


def halve_first_kernel(at_ref, keep_ref, came_ref, out_ref):
    out_ref[...] = (keep_ref[0].astype(F32) + came_ref[0].astype(F32)).astype(BF16)


def halve_first(at, axis, keep, came, passes):
    _, _, depth, rows, width = keep.shape
    half = pl.BlockSpec((1, 2, depth, rows, width), lambda i, s: (1 - s[axis], 0, 0, 0, 0))
    return run(
        halve_first_kernel,
        "halve_first",
        (1,),
        (at, keep, came),
        [half, half],
        (jax.ShapeDtypeStruct((2, depth, rows, width), BF16),),
        (fixed((2, depth, rows, width)),),
        scalars=1,
        passes=passes,
    )


def sum_second(keep, came, came1):
    total = rounded(keep.astype(F32) + came.astype(F32))
    return rounded(total + came1.astype(F32))


def quarter_kernel(plan, at_ref, *refs):
    outs = refs[-4:]
    here = at_ref[2]
    for d in range(4):
        z = lax.bitwise_xor(here, d)
        for first, count, row, column, through in plan:
            keep_ref, came_ref, came1_ref = refs[first : first + 3]
            came2_ref = refs[through]
            rows, part = keep_ref.shape[3:]
            total = sum_second(keep_ref[0, 0, z], came_ref[0, 0, z], came1_ref[0, z])
            came2 = came2_ref[z, :, column : column + part]
            outs[d][row : row + rows, column : column + part] = rounded(
                total + came2.astype(F32)
            ).astype(BF16)


def quarter(at, states, total_rows, total_width, passes, after):
    specs, operands, plan, seen = [], [], [], {}
    for keep, came, came1, came2, axis, row, column in states:
        _, _, depth, rows, part = keep.shape
        if axis == 0:
            both = pl.BlockSpec((1, 1, depth, rows, part), lambda i, s: (s[0], s[1], 0, 0, 0))
            one = pl.BlockSpec((1, depth, rows, part), lambda i, s: (s[1], 0, 0, 0))
        else:
            both = pl.BlockSpec((1, 1, depth, rows, part), lambda i, s: (s[1], s[0], 0, 0, 0))
            one = pl.BlockSpec((1, depth, rows, part), lambda i, s: (s[0], 0, 0, 0))
        first = len(operands)
        specs += [both, both, one]
        operands += [keep, came, came1]
        if id(came2) not in seen:
            seen[id(came2)] = len(operands)
            specs.append(fixed(came2.shape))
            operands.append(came2)
        plan.append((first, 3, row, column, seen[id(came2)]))
    part = jax.ShapeDtypeStruct((total_rows, total_width), BF16)
    return run(
        functools.partial(quarter_kernel, plan),
        "quarter",
        (1,),
        (at, *operands),
        specs,
        (part,) * 4,
        (pl.BlockSpec((total_rows, total_width), lambda i, s: (0, 0)),) * 4,
        scalars=1,
        passes=passes,
        after=after,
    )


def projection_part(core_ref, h_ref, grads, sums, keep_ref, send_ref):
    rows = h_ref.shape[1] // 16
    even = core_ref[0] == 0
    for s in range(3):
        place = slice(s * rows, (s + 1) * rows)
        parts = [mm(h_ref[...], ref[s], TN) for ref in grads]
        for z in range(4):
            for y in range(2):
                base = (z * 2 + y) * 2 * rows
                for x in range(2):
                    unit = slice(x * UNIT, (x + 1) * UNIT)
                    zero = lanes(*[p[base : base + rows, unit] for p in parts])
                    one = lanes(*[p[base + rows : base + 2 * rows, unit] for p in parts])
                    keep_ref[y, x, z, place, :] = jnp.where(even, zero, one).astype(BF16)
                    send_ref[y, x, z, place, :] = jnp.where(even, one, zero).astype(BF16)
    extra = jnp.zeros((BIAS_ROWS, keep_ref.shape[4]), F32)
    at = lax.broadcasted_iota(jnp.int32, extra.shape, 0)
    for r in range(2):
        for g, ref in enumerate(sums):
            for x in range(2):
                part = ref[r : r + 1, x * UNIT : (x + 1) * UNIT]
                extra = jnp.where(at == (2 * r + x) * len(sums) + g, part, extra)
    for z in range(4):
        for y in range(2):
            for x in range(2):
                keep_ref[y, x, z, 3 * rows :, :] = extra.astype(BF16)
                send_ref[y, x, z, 3 * rows :, :] = extra.astype(BF16)


def attention_backward_kernel(
    others,
    before,
    q_ref,
    k_ref,
    v_ref,
    dctx_pair_ref,
    ctx_pair_ref,
    lse_ref,
    seg_ref,
    *refs,
):
    delta_ref, total_ref, kt_ref, dctx_ref, segc_ref = refs[-5:]
    if others is None:
        grads_ref, sums_ref = refs[:2]
    else:
        core_ref, h_ref = refs[:2]
        other_refs = refs[2 : 2 + others]
        before_refs = refs[2 + others : 2 + others + before]
        grads_ref, sums_ref, keep_ref, send_ref = refs[-9:-5]
    length = q_ref.shape[0]
    dctx_ref[...] = lanes(dctx_pair_ref[0], dctx_pair_ref[1])
    ctx = lanes(ctx_pair_ref[0], ctx_pair_ref[1])
    segr = seg_ref[...].astype(F32)
    segc_ref[...] = column_of(segr)
    prod = dctx_ref[...].astype(F32) * ctx.astype(F32)
    high = prod.astype(BF16)
    rest = (prod - high.astype(F32)).astype(BF16)
    lane = lax.broadcasted_iota(jnp.int32, (8, GROUP), 1)
    head_of = lax.broadcasted_iota(jnp.int32, (8, GROUP), 0)
    chooser = jnp.where(lane // HEAD == head_of, 1.0, 0.0).astype(BF16)
    delta_ref[...] = mm(chooser, high, NT) + mm(chooser, rest, NT)
    total_ref[...] = jnp.zeros_like(total_ref)
    kt_ref[...] = jnp.transpose(k_ref[...])

    def block(j, carry):
        rows = pl.ds(pl.multiple_of(j * TILE, TILE), TILE)
        kb = k_ref[rows, :]
        vb = v_ref[rows, :]
        mask = jnp.where(segc_ref[rows, :] == segr, 0.0, NEGATIVE)
        dk = jnp.zeros((TILE, GROUP), F32)
        dv = jnp.zeros((TILE, GROUP), F32)
        for head in range(PER_GROUP):
            mine = head_lanes((TILE, GROUP), head)
            km = jnp.where(mine, kb, BF16(0)) * BF16(HEAD**-0.5)
            vm = jnp.where(mine, vb, BF16(0))
            s = mm(km, q_ref[...], NT) + mask
            p = jnp.exp(s - lse_ref[head : head + 1, :])
            dp = mm(vm, dctx_ref[...], NT)
            ds = (p * (dp - delta_ref[head : head + 1, :])).astype(BF16)
            dv = jnp.where(mine, mm(p.astype(BF16), dctx_ref[...], NN), dv)
            dk = jnp.where(mine, mm(ds, q_ref[...], NN), dk)
            columns = slice(head * HEAD, (head + 1) * HEAD)
            total_ref[columns, :] += mm(kt_ref[columns, rows], ds, NN)
        dkb = (dk * HEAD**-0.5).astype(BF16)
        dvb = dv.astype(BF16)
        grads_ref[1, rows, :] = dkb
        grads_ref[2, rows, :] = dvb
        return carry + row_sum(dvb.astype(F32))

    dv_sum = lax.fori_loop(0, length // TILE, block, jnp.zeros((1, GROUP), F32), unroll=True)
    dq = jnp.transpose(total_ref[...] * HEAD**-0.5).astype(BF16)
    grads_ref[0] = dq
    sums_ref[...] = jnp.zeros_like(sums_ref)
    sums_ref[0:1, :] = row_sum(dq.astype(F32))
    sums_ref[1:2, :] = dv_sum
    if others is not None:
        sums = (*before_refs, sums_ref) if before else ()
        projection_part(core_ref, h_ref, (*other_refs, grads_ref), sums, keep_ref, send_ref)


def attention_backward(g, q, k, v, dctx, ctx, lse, seg, weights, passes, after):
    length, width = q.shape
    rows = pl.BlockSpec((length, GROUP), lambda i: (0, g))
    pair_rows = pl.BlockSpec((2, length, UNIT), lambda i: (0, 0, g))
    operands = [q, k, v, dctx, ctx, lse, seg]
    specs = [
        rows,
        rows,
        rows,
        pair_rows,
        pair_rows,
        pl.BlockSpec((8, length), lambda i: (g, 0)),
        fixed((1, length)),
    ]
    kinds = [jax.ShapeDtypeStruct((3, length, GROUP), BF16), jax.ShapeDtypeStruct((8, GROUP), F32)]
    outs = [fixed((3, length, GROUP)), fixed((8, GROUP))]
    others, before = None, 0
    if weights:
        core, h, grads, sums = weights
        others, before = len(grads), len(sums)
        operands += [core, h, *grads, *sums]
        specs += [SCALAR] + [fixed(x.shape) for x in (h, *grads, *sums)]
        shape = (2, 2, 4, 3 * width // 16 + BIAS_ROWS, (others + 1) * UNIT)
        kinds += [jax.ShapeDtypeStruct(shape, BF16)] * 2
        outs += [fixed(shape)] * 2
    return run(
        functools.partial(attention_backward_kernel, others, before),
        "attention_backward",
        (1,),
        tuple(operands),
        specs,
        kinds,
        outs,
        [
            pltpu.VMEM((8, length), F32),
            pltpu.VMEM((GROUP, length), F32),
            pltpu.VMEM((GROUP, length), BF16),
            pltpu.VMEM((length, GROUP), BF16),
            pltpu.VMEM((length, 1), F32),
        ],
        passes=passes,
        after=after,
        micros=8,
    )


def hidden_total(fp_ref, d_refs, w_refs):
    total = fp_ref[...]
    for at, w_ref in enumerate(w_refs):
        d = lanes(*[ref[at, :, x * UNIT : (x + 1) * UNIT] for x in range(2) for ref in d_refs])
        total = total + mm(d, w_ref[...], NT)
    return total


def hidden_away_kernel(fp_ref, *refs):
    refs[6][...] = hidden_total(fp_ref, refs[:3], refs[3:6]).astype(BF16)


def hidden_home_kernel(here_ref, fp_ref, *refs):
    came0_ref, came1_ref, out_ref, layer_ref = refs[6:]
    out_ref[0] = hidden_total(fp_ref, refs[:3], refs[3:6])
    layer_ref[0] = jnp.where(pl.program_id(0) == 0, came0_ref[...], came1_ref[...])


def hidden_away(fp, d0, d1, d2, wq, wk, wv, passes, after):
    length, width = fp.shape
    half = length // 2
    steps = half // TILE
    return run(
        hidden_away_kernel,
        "hidden_away",
        (steps,),
        (fp, d0, d1, d2, wq, wk, wv),
        [
            pl.BlockSpec((TILE, width), lambda i: (i + steps, 0)),
        ]
        + [pl.BlockSpec((3, TILE, GROUP), lambda i: (0, i + steps, 0))] * 3
        + [fixed((width, width))] * 3,
        (jax.ShapeDtypeStruct((half, width), BF16),),
        (pl.BlockSpec((TILE, width), lambda i: (i, 0)),),
        passes=passes,
        after=after,
        micros=3,
    )


def hidden_home(here, fp, d0, d1, d2, wq, wk, wv, came0, came1, layer, passes, after):
    length, width = fp.shape
    half = length // 2
    steps = half // TILE
    return run(
        hidden_home_kernel,
        "hidden_home",
        (steps,),
        (here, fp, d0, d1, d2, wq, wk, wv, came0, came1),
        [
            pl.BlockSpec((TILE, width), lambda i, b: (i, 0)),
        ]
        + [pl.BlockSpec((3, TILE, GROUP), lambda i, b: (0, i, 0))] * 3
        + [fixed((width, width))] * 3
        + [fixed((TILE, width))] * 2,
        (
            jax.ShapeDtypeStruct((2, half, width), F32),
            jax.ShapeDtypeStruct((2, half, width), BF16),
        ),
        (
            pl.BlockSpec((1, TILE, width), lambda i, b: (b[0], i, 0)),
            pl.BlockSpec((1, TILE, width), lambda i, b: (1 - b[0], i, 0)),
        ),
        scalars=1,
        held={1: layer},
        passes=passes,
        after=after,
        micros=3,
    )


def place_kernel(here_ref, came_ref, out_ref):
    out_ref[0] = came_ref[...].astype(F32)


def place_far(here, came, grad, passes):
    half, width = came.shape
    return run(
        place_kernel,
        "place_far",
        (2,),
        (here, came),
        [pl.BlockSpec((half // 2, width), lambda i, b: (i, 0))],
        (jax.ShapeDtypeStruct((2, half, width), F32),),
        (pl.BlockSpec((1, half // 2, width), lambda i, b: (1 - b[0], i, 0)),),
        scalars=1,
        held={0: grad},
        passes=passes,
        micros=1,
    )


def fast(
    hidden,
    segments,
    query_matrix,
    query_bias,
    key_matrix,
    value_matrix,
    value_bias,
    output_matrix,
    output_bias,
    first_gain,
    first_shift,
    inner_matrix,
    inner_bias,
    outer_matrix,
    outer_bias,
    second_gain,
    second_shift,
    cotangent,
):
    here = lax.axis_index("blk")
    place = lax.axis_index("seq")
    core, y_at, z_at = place % 2, (place // 2) % 2, place // 4
    here_id = here.astype(jnp.int32)[None]
    core_id = core.astype(jnp.int32)[None]
    half, width = hidden.shape[1:]

    def pick(x, *at):
        start = at + (0,) * (x.ndim - len(at))
        size = (1,) * len(at) + x.shape[len(at) :]
        return lax.dynamic_slice(x, start, size).reshape(x.shape[len(at) :])

    def trade(x):
        return lax.ppermute(x, "blk", [(0, 1), (1, 0)])

    def seq_swap(x, bit):
        return lax.ppermute(x, "seq", [(i, i ^ bit) for i in range(16)])

    def row(x):
        return x.astype(F32)[None, :]

    at = jnp.stack([here, y_at, z_at]).astype(jnp.int32)

    def rounded(x):
        return lax.reduce_precision(x, 8, 7)

    def sum_0(state, *at):
        return rounded(pick(state[0], *at).astype(F32) + pick(state[1], *at).astype(F32))

    def sum_1(state, mine, *at):
        return rounded(sum_0(state, mine, *at) + pick(state[2], *at).astype(F32))

    def sum_2(state, mine, then, *at):
        return rounded(sum_1(state, mine, then, *at) + pick(state[3], *at).astype(F32))

    def send_z(parts):
        return [seq_swap(x, 4 * d) for d, x in zip((1, 2, 3), parts)]

    def add_z(total, parts):
        return (total + parts[0].astype(F32)) + (parts[1].astype(F32) + parts[2].astype(F32))

    seg = jnp.concatenate([pick(segments, here), trade(pick(segments, 1 - here))])[None, :]
    far = trade(pick(hidden, 1 - here))
    cot_far = trade(pick(cotangent, 1 - here + jnp.minimum(seg[0, -1], 0)))
    q, k, v, ctx, lse, h = attention_forward(
        here_id,
        hidden,
        far,
        query_matrix,
        key_matrix,
        value_matrix,
        row(query_bias),
        row(value_bias),
        seg,
    )
    empty = jnp.zeros((2, width), F32)
    vec = jnp.concatenate(
        [
            row(output_bias),
            row(first_gain),
            row(first_shift),
            row(outer_bias),
            row(second_gain),
            row(second_shift),
            empty,
        ],
        axis=0,
    )
    out, out_far0, out_far1, first, act, og, ig, fp, ag, dctx, sums, isum = token_pass(
        here_id, h, ctx, cotangent, cot_far, output_matrix, inner_matrix, outer_matrix, row(inner_bias), vec
    )
    x_mine, x_away, y_mine, y_away = here, 1 - here, y_at, 1 - y_at
    a_keep, a_send = outer_grad_call(core_id, act, og, sums, isum)
    a0 = seq_swap(a_send, 1)
    b_keep, b_send, a_keep = inner_grad_call(core_id, first, ig, ctx, ag, (a_keep,))
    b0 = seq_swap(b_send, 1)
    a = (a_keep, a0)
    a_away, out_far0 = halve_first(at, 1, a_keep, a0, (out_far0,))
    a1 = seq_swap(a_away, 2)
    out_came0 = trade(out_far0)
    b = (b_keep, b0)
    b_away = sum_0(b, x_away).astype(BF16)
    b1 = trade(b_away)
    bwd = (q, k, v, dctx, ctx, lse, seg)
    grads0, bias0 = attention_backward(0, *bwd, (), (), (a_away, b_away))
    grads1, bias1, c_keep, c_send, a_keep, b_keep, out_came0, out_far1 = attention_backward(
        1, *bwd, (core_id, h, (grads0,), ()), (a_keep, b_keep, out_came0, out_far1), ()
    )
    out_came1 = trade(out_far1)
    c0 = seq_swap(c_send, 1)
    a = (a_keep, a0, a1)
    a_away = sum_1(a, y_mine, x_away).astype(BF16)
    a2 = trade(a_away)
    b = (b_keep, b0, b1)
    b_away = sum_1(b, x_mine, y_away).astype(BF16)
    b2 = seq_swap(b_away, 2)
    grads2, _, d_keep, d_send, a_keep, b_keep, c_keep = attention_backward(
        2, *bwd, (core_id, h, (), (bias0, bias1)), (a_keep, b_keep, c_keep), (a_away, b_away)
    )
    d0 = seq_swap(d_send, 1)
    c = (c_keep, c0)
    c_away = sum_0(c, y_away).astype(BF16)
    c1 = seq_swap(c_away, 2)

    def flat(x):
        return x.reshape(*x.shape[:-3], -1, x.shape[-1])

    a_rows, b_rows = a_keep.shape[3], 5 * width // 16
    states = [
        (a_keep, a0, a1, a2, 1, 0, 0),
        (flat(b_keep), flat(b0), flat(b1), flat(b2), 0, a_rows, 0),
    ]
    ab_mine, *parts, out_came1, d_keep = quarter(
        at, states, a_rows + b_rows, width // 2, (out_came1, d_keep), (c_away,)
    )
    ab3 = send_z(parts)
    args = (fp, grads0, grads1, grads2, query_matrix, key_matrix, value_matrix)
    d = (d_keep, d0)
    d_away = sum_0(d, y_away).astype(BF16)
    d1 = seq_swap(d_away, 2)
    hidden_grad, layer_out, c_keep, d_keep = hidden_home(
        here_id, *args, out_came0, out_came1, out, (c_keep, d_keep), (d_away,)
    )
    c = (c_keep, c0, c1)
    d = (d_keep, d0, d1)

    def lanes_of(*parts):
        return jnp.concatenate(parts, axis=-1)

    def late_1(*at):
        return lanes_of(sum_1(c, y_mine, *at), sum_1(d, y_mine, *at))

    e_away = late_1(x_away).astype(BF16)
    e2 = trade(e_away)
    far_grad, c_keep, d_keep, ab_mine = hidden_away(*args, (c_keep, d_keep, ab_mine), (e_away,))
    came = trade(far_grad)
    c = (c_keep, c0, c1)
    d = (d_keep, d0, d1)

    def late_2(z):
        return rounded(late_1(x_mine, z) + pick(e2, z).astype(F32))

    e3 = send_z([late_2(z_at ^ e).astype(BF16) for e in (1, 2, 3)])
    early = add_z(ab_mine.astype(F32), ab3)
    hidden_grad = place_far(here_id, came, hidden_grad, ())[0]
    late = add_z(late_2(z_at), e3)
    rows = width // 16
    outer_rows = 4 * rows
    outer_grad = early[:outer_rows]
    vectors = early[outer_rows : outer_rows + VECTOR_ROWS].reshape(-1, width)
    inner_all = early[outer_rows + VECTOR_ROWS :].reshape(5, rows, width // 2)
    output_grad = inner_all[4]
    inner_grad = jnp.transpose(inner_all[:4], (1, 0, 2)).reshape(rows, -1)
    units = width // UNIT
    biases = late[3 * rows :, 2 * UNIT :][: 2 * units].reshape(2, width)
    return (
        layer_out,
        hidden_grad,
        late[:rows],
        biases[0],
        late[rows : 2 * rows],
        late[2 * rows : 3 * rows],
        biases[1],
        output_grad,
        vectors[5],
        vectors[3],
        vectors[4],
        inner_grad,
        vectors[6:10].reshape(-1),
        outer_grad,
        vectors[2],
        vectors[0],
        vectors[1],
    )


def choose(sizes, *args):
    seq_count, row_count, width = args[0].shape
    whole_here = sizes[1] == 2 and seq_count == 2 and row_count == 2 * TILE and width == 3 * GROUP
    return fast(*args) if whole_here and sizes[0] == 16 else general(*args)


def solution(mesh):
    sizes = (mesh.shape["seq"], mesh.shape["blk"])
    return jax.shard_map(
        functools.partial(choose, sizes),
        mesh=mesh,
        in_specs=(
            P("seq", "blk", None),
            P("seq", "blk"),
            P(),
            P(),
            P(),
            P(),
            P(),
            P(),
            P(),
            P(),
            P(),
            P(),
            P(),
            P(),
            P(),
            P(),
            P(),
            P("seq", "blk", None),
        ),
        out_specs=(
            P("seq", "blk", None),
            P("seq", "blk", None),
            P("seq", "blk"),
            P(),
            P("seq", "blk"),
            P("seq", "blk"),
            P(),
            P("seq", "blk"),
            P(),
            P(),
            P(),
            P("seq", "blk"),
            P(),
            P("seq", "blk"),
            P(),
            P(),
            P(),
        ),
        check_vma=False,
    )
```

```python
import functools
import math

import jax
import jax.numpy as jnp
from jax import lax
from jax.experimental import pallas as pl
from jax.experimental.pallas import tpu as pltpu
from jax.sharding import PartitionSpec as P

HEADS = 12
HEAD = 64


NEGATIVE = -1e30
EPSILON = 1e-12


def layer_norm(values, norm_gain, norm_shift):
    centre = values - jnp.mean(values, axis=-1, keepdims=True)
    spread = jnp.mean(centre * centre, axis=-1, keepdims=True)
    return centre * lax.rsqrt(spread + EPSILON) * norm_gain + norm_shift


def gelu_exact(values):
    return jax.nn.gelu(values, approximate=False)


def linear(operand, matrix):
    return jnp.dot(operand, matrix, preferred_element_type=jnp.float32)


def split_heads(values):
    return values.reshape(values.shape[0], values.shape[1], HEADS, HEAD)


def block_scores(query_block, key_block, score_scale):
    return (
        jnp.einsum("sqhd,skhd->shqk", query_block, key_block, preferred_element_type=jnp.float32)
        * score_scale
    )


def attention_grads(
    query_block, key_block, value_block, dctx_block, same_doc, log_total, row_delta, score_scale
):
    attn_probs = jnp.where(
        same_doc,
        jnp.exp(block_scores(query_block, key_block, score_scale) - log_total[..., None]),
        0.0,
    )
    slopes = jnp.einsum(
        "sqhd,skhd->shqk", dctx_block, value_block, preferred_element_type=jnp.float32
    )
    return (attn_probs, (attn_probs * (slopes - row_delta[..., None])).astype(jnp.bfloat16))


def over_blocks(length, step, initial):
    block_size = math.gcd(length, 512)

    def scan_step(carried, block_index):
        return (step(carried, block_index * block_size, block_size), None)

    result, unused = lax.scan(scan_step, initial, jnp.arange(length // block_size, dtype=jnp.int32))
    return result


def general(
    hidden,
    segments,
    query_matrix,
    query_bias,
    key_matrix,
    value_matrix,
    value_bias,
    output_matrix,
    output_bias,
    first_gain,
    first_shift,
    inner_matrix,
    inner_bias,
    outer_matrix,
    outer_bias,
    second_gain,
    second_shift,
    cotangent,
):
    seq_count, row_count, model_width = hidden.shape
    score_scale = HEAD ** (-0.5)
    single_float = jnp.float32
    bf16 = jnp.bfloat16
    queries = (linear(hidden, query_matrix) + query_bias.astype(single_float)).astype(bf16)
    key_proj = linear(hidden, key_matrix).astype(bf16)
    value_proj = (linear(hidden, value_matrix) + value_bias.astype(single_float)).astype(bf16)
    seg_all = lax.all_gather(segments, "blk", axis=1, tiled=True)
    keys_all, values_all = (
        lax.all_gather(key_proj, "blk", axis=1, tiled=True),
        lax.all_gather(value_proj, "blk", axis=1, tiled=True),
    )
    length = seg_all.shape[1]
    query_heads = split_heads(queries)
    key_heads = split_heads(keys_all)
    value_heads = split_heads(values_all)

    def key_slices(offset, block_size):
        key_segs = lax.dynamic_slice_in_dim(seg_all, offset, block_size, 1)
        same_doc = (segments[:, :, None] == key_segs[:, None, :])[:, None]
        key_block = lax.dynamic_slice_in_dim(key_heads, offset, block_size, 1)
        value_block = lax.dynamic_slice_in_dim(value_heads, offset, block_size, 1)
        return (same_doc, key_block, value_block)

    def stats_step(carried, offset, block_size):
        same_doc, key_block, value_block = key_slices(offset, block_size)
        running_max, running_sum = carried
        scores = jnp.where(same_doc, block_scores(query_heads, key_block, score_scale), NEGATIVE)
        higher = jnp.maximum(running_max, jnp.max(scores, axis=-1))
        weights = jnp.where(same_doc, jnp.exp(scores - higher[..., None]), 0.0)
        return (higher, running_sum * jnp.exp(running_max - higher) + jnp.sum(weights, axis=-1))

    stat_shape = (seq_count, HEADS, row_count)
    running_max, running_sum = over_blocks(
        length,
        stats_step,
        (jnp.full(stat_shape, NEGATIVE, single_float), jnp.zeros(stat_shape, single_float)),
    )
    log_total = running_max + jnp.log(running_sum)

    def context_step(carried, offset, block_size):
        same_doc, key_block, value_block = key_slices(offset, block_size)
        attn_probs = jnp.where(
            same_doc,
            jnp.exp(block_scores(query_heads, key_block, score_scale) - log_total[..., None]),
            0.0,
        )
        return carried + jnp.einsum(
            "shqk,skhd->sqhd",
            attn_probs.astype(bf16),
            value_block,
            preferred_element_type=single_float,
        )

    head_zeros = jnp.zeros((seq_count, row_count, HEADS, HEAD), single_float)
    context = over_blocks(length, context_step, head_zeros)
    context_reduced = context.reshape(seq_count, row_count, model_width).astype(bf16)
    attn_out = linear(context_reduced, output_matrix) + output_bias.astype(single_float)
    first_pre = hidden.astype(single_float) + attn_out
    first_norm, first_back = jax.vjp(
        layer_norm, first_pre, first_gain.astype(single_float), first_shift.astype(single_float)
    )
    first_reduced = first_norm.astype(bf16)
    inner = linear(first_reduced, inner_matrix) + inner_bias.astype(single_float)
    act_full, gelu_back = jax.vjp(gelu_exact, inner)
    activation_reduced = act_full.astype(bf16)
    outer = linear(activation_reduced, outer_matrix) + outer_bias.astype(single_float)
    layer_full, second_back = jax.vjp(
        layer_norm,
        first_norm + outer,
        second_gain.astype(single_float),
        second_shift.astype(single_float),
    )
    layer_out = layer_full.astype(bf16)
    second_pre_grad, second_gain_grad, second_shift_grad = second_back(
        cotangent.astype(single_float)
    )
    outer_gradient_reduced = second_pre_grad.astype(bf16)
    outer_weight_grad = jnp.einsum(
        "gvx,gvm->xm",
        activation_reduced,
        outer_gradient_reduced,
        preferred_element_type=single_float,
    )
    outer_bias_grad = jnp.sum(outer_gradient_reduced.astype(single_float), axis=(0, 1))
    activation_gradient = jnp.einsum(
        "rzo,uo->rzu", outer_gradient_reduced, outer_matrix, preferred_element_type=single_float
    )
    inner_gradient_reduced = gelu_back(activation_gradient)[0].astype(bf16)
    inner_weight_grad = jnp.einsum(
        "ret,reu->tu", first_reduced, inner_gradient_reduced, preferred_element_type=single_float
    )
    inner_bias_grad = jnp.sum(inner_gradient_reduced.astype(single_float), axis=(0, 1))
    first_norm_grad = second_pre_grad + jnp.einsum(
        "aoi,ni->aon", inner_gradient_reduced, inner_matrix, preferred_element_type=single_float
    )
    first_pre_grad, first_gain_grad, first_shift_grad = first_back(first_norm_grad)
    attention_gradient_reduced = first_pre_grad.astype(bf16)
    output_weight_grad = jnp.einsum(
        "tfm,tfc->mc",
        context_reduced,
        attention_gradient_reduced,
        preferred_element_type=single_float,
    )
    output_bias_grad = jnp.sum(attention_gradient_reduced.astype(single_float), axis=(0, 1))
    dctx_low = jnp.einsum(
        "upx,cx->upc",
        attention_gradient_reduced,
        output_matrix,
        preferred_element_type=single_float,
    ).astype(bf16)
    dctx_heads = split_heads(dctx_low)
    row_delta = jnp.transpose(
        jnp.sum(dctx_heads.astype(single_float) * context, axis=-1), (0, 2, 1)
    )

    def query_step(carried, offset, block_size):
        same_doc, key_block, value_block = key_slices(offset, block_size)
        attn_probs, dscores = attention_grads(
            query_heads,
            key_block,
            value_block,
            dctx_heads,
            same_doc,
            log_total,
            row_delta,
            score_scale,
        )
        return carried + score_scale * jnp.einsum(
            "shqk,skhd->sqhd", dscores, key_block, preferred_element_type=single_float
        )

    query_grad = over_blocks(length, query_step, head_zeros)
    query_all, dctx_all = (
        lax.all_gather(queries, "blk", axis=1, tiled=True),
        lax.all_gather(dctx_low, "blk", axis=1, tiled=True),
    )
    lse_all, delta_all = (
        lax.all_gather(log_total, "blk", axis=2, tiled=True),
        lax.all_gather(row_delta, "blk", axis=2, tiled=True),
    )
    query_all_heads = split_heads(query_all)
    dctx_all_heads = split_heads(dctx_all)
    own_keys = split_heads(key_proj)
    own_values = split_heads(value_proj)

    def key_step(carried, offset, block_size):
        query_segs = lax.dynamic_slice_in_dim(seg_all, offset, block_size, 1)
        same_doc = (query_segs[:, :, None] == segments[:, None, :])[:, None]
        query_block = lax.dynamic_slice_in_dim(query_all_heads, offset, block_size, 1)
        dctx_block = lax.dynamic_slice_in_dim(dctx_all_heads, offset, block_size, 1)
        lse_block = lax.dynamic_slice_in_dim(lse_all, offset, block_size, 2)
        delta_block = lax.dynamic_slice_in_dim(delta_all, offset, block_size, 2)
        key_sum, value_sum = carried
        attn_probs, dscores = attention_grads(
            query_block,
            own_keys,
            own_values,
            dctx_block,
            same_doc,
            lse_block,
            delta_block,
            score_scale,
        )
        key_sum = key_sum + score_scale * jnp.einsum(
            "shqk,sqhd->skhd", dscores, query_block, preferred_element_type=single_float
        )
        value_sum = value_sum + jnp.einsum(
            "shqk,sqhd->skhd",
            attn_probs.astype(bf16),
            dctx_block,
            preferred_element_type=single_float,
        )
        return (key_sum, value_sum)

    key_grad, value_grad = over_blocks(length, key_step, (head_zeros, head_zeros))
    query_gradient_reduced = query_grad.reshape(seq_count, row_count, model_width).astype(bf16)
    key_gradient_reduced = key_grad.reshape(seq_count, row_count, model_width).astype(bf16)
    value_gradient_reduced = value_grad.reshape(seq_count, row_count, model_width).astype(bf16)
    query_weight_grad = jnp.einsum(
        "tfm,tfc->mc", hidden, query_gradient_reduced, preferred_element_type=single_float
    )
    query_bias_grad = jnp.sum(query_gradient_reduced.astype(single_float), axis=(0, 1))
    key_matrix_gradient = jnp.einsum(
        "tfm,tfc->mc", hidden, key_gradient_reduced, preferred_element_type=single_float
    )
    value_weight_grad = jnp.einsum(
        "tfm,tfc->mc", hidden, value_gradient_reduced, preferred_element_type=single_float
    )
    value_bias_grad = jnp.sum(value_gradient_reduced.astype(single_float), axis=(0, 1))
    hidden_grad = first_pre_grad + jnp.einsum(
        "upx,cx->upc", query_gradient_reduced, query_matrix, preferred_element_type=single_float
    )
    hidden_grad = hidden_grad + jnp.einsum(
        "upx,cx->upc", key_gradient_reduced, key_matrix, preferred_element_type=single_float
    )
    hidden_grad = hidden_grad + jnp.einsum(
        "upx,cx->upc", value_gradient_reduced, value_matrix, preferred_element_type=single_float
    )
    partial_sums = (
        lax.psum_scatter(query_weight_grad, "seq", scatter_dimension=0, tiled=True),
        lax.psum_scatter(key_matrix_gradient, "seq", scatter_dimension=0, tiled=True),
        lax.psum_scatter(value_weight_grad, "seq", scatter_dimension=0, tiled=True),
        lax.psum_scatter(output_weight_grad, "seq", scatter_dimension=0, tiled=True),
        lax.psum_scatter(inner_weight_grad, "seq", scatter_dimension=0, tiled=True),
        lax.psum_scatter(outer_weight_grad, "seq", scatter_dimension=0, tiled=True),
    )
    matrices = lax.psum_scatter(tuple(partial_sums), "blk", scatter_dimension=1, tiled=True)
    vectors = lax.psum(
        (
            query_bias_grad,
            value_bias_grad,
            output_bias_grad,
            first_gain_grad,
            first_shift_grad,
            inner_bias_grad,
            outer_bias_grad,
            second_gain_grad,
            second_shift_grad,
        ),
        ("seq", "blk"),
    )
    return (
        layer_out,
        hidden_grad,
        matrices[0],
        vectors[0],
        matrices[1],
        matrices[2],
        vectors[1],
        matrices[3],
        vectors[2],
        vectors[3],
        vectors[4],
        matrices[4],
        vectors[5],
        matrices[5],
        vectors[6],
        vectors[7],
        vectors[8],
    )


BF16 = jnp.bfloat16
F32 = jnp.float32
NN = ((1,), (0,))
NT = ((1,), (1,))
TN = ((0,), (0,))
UNIT = 128
GROUP = 256
PER_GROUP = GROUP // HEAD
TILE = 256
KEYS = 512
TOKENS = 512
VMEM_LIMIT = 60 * 2**20
SCALAR = pl.BlockSpec(memory_space=pltpu.SMEM)
ANY = pl.BlockSpec(memory_space=pl.ANY)


def mm(a, b, dims):
    return lax.dot_general(a, b, (dims, ((), ())), preferred_element_type=F32)


def fixed(shape):
    return pl.BlockSpec(shape, lambda *_: (0,) * len(shape), pipeline_mode=pl.Buffered(1))


def run(
    kernel,
    name,
    grid,
    operands,
    in_specs,
    out_shape,
    out_specs,
    scratch=(),
    scalars=0,
    held=None,
    passes=(),
    after=(),
    micros=1,
):
    held = held or {}
    out_shape, out_specs = list(out_shape), list(out_specs)
    n_in, n_out, n_held, n_pass = len(operands), len(out_shape), len(held), len(passes)
    aliases = {n_in + i: at for i, at in enumerate(held)}
    aliases |= {n_in + n_held + i: n_out + i for i in range(n_pass)}

    def body(*refs):
        outs = n_in + n_held + n_pass + len(after)
        kernel(*refs[:n_in], *refs[outs : outs + n_out], *refs[outs + n_out + n_pass :])

    result = pl.pallas_call(
        body,
        grid_spec=pltpu.PrefetchScalarGridSpec(
            num_scalar_prefetch=scalars,
            grid=grid,
            in_specs=list(in_specs) + [ANY] * (n_held + n_pass + len(after)),
            out_specs=out_specs + [ANY] * n_pass,
            scratch_shapes=list(scratch),
        ),
        out_shape=out_shape + [jax.ShapeDtypeStruct(x.shape, x.dtype) for x in passes],
        input_output_aliases=aliases,
        compiler_params=pltpu.CompilerParams(
            vmem_limit_bytes=VMEM_LIMIT, dimension_semantics=("arbitrary",) * len(grid)
        ),
        cost_estimate=pl.CostEstimate(
            flops=int(micros * 1e10), bytes_accessed=1, transcendentals=0
        ),
        name=name,
    )(*operands, *held.values(), *passes, *after)
    return result


def head_lanes(shape, head):
    lane = lax.broadcasted_iota(jnp.int32, shape, 1)
    return (lane >= head * HEAD) & (lane < (head + 1) * HEAD)


def lanes(*parts):
    return jnp.concatenate(parts, axis=1)


def column_of(row):
    return jnp.transpose(jnp.broadcast_to(row.astype(F32), (UNIT, row.shape[1])))[:, 0:1]


def same_pair(row, column, rows):
    return jnp.where(column[rows] == row, 0.0, NEGATIVE)


def attention_forward_kernel(
    here_ref,
    own_ref,
    far_ref,
    wq0_ref,
    wq1_ref,
    wk0_ref,
    wk1_ref,
    wv0_ref,
    wv1_ref,
    bq0_ref,
    bq1_ref,
    bv0_ref,
    bv1_ref,
    seg_ref,
    q_ref,
    k_ref,
    v_ref,
    ctx_ref,
    lse_ref,
    h_ref,
    mask_ref,
    vaug_ref,
):
    half = far_ref.shape[0]
    length = 2 * half

    @pl.when(pl.program_id(0) == 0)
    def _():
        segr = seg_ref[...].astype(F32)
        mask_ref[...] = jnp.where(column_of(segr) == segr, 0.0, NEGATIVE)
        h_ref[0:half, :] = own_ref[0]
        h_ref[half:, :] = far_ref[...]

    h = h_ref[...]
    bias_q = lanes(bq0_ref[...], bq1_ref[...])
    bias_v = lanes(bv0_ref[...], bv1_ref[...])
    q_ref[...] = (mm(h, lanes(wq0_ref[...], wq1_ref[...]), NN) + bias_q).astype(BF16)
    k_ref[...] = mm(h, lanes(wk0_ref[...], wk1_ref[...]), NN).astype(BF16)
    v = (mm(h, lanes(wv0_ref[...], wv1_ref[...]), NN) + bias_v).astype(BF16)
    v_ref[...] = v
    lane = lax.broadcasted_iota(jnp.int32, v.shape, 1)
    for head in range(PER_GROUP):
        other = (lane // UNIT) != (head // 2)
        filler = jnp.where(other, 1.0, 0.0).astype(BF16)
        vaug_ref[head] = jnp.where(head_lanes(v.shape, head), v, filler)

    def block(i, carry):
        rows = pl.ds(pl.multiple_of(i * TILE, TILE), TILE)
        qb = q_ref[rows, :] * BF16(HEAD**-0.5)
        halves = [None, None]
        stat_lane = lax.broadcasted_iota(jnp.int32, (TILE, UNIT), 1)
        stats = jnp.zeros((TILE, UNIT), F32)
        for head in range(PER_GROUP):
            qm = jnp.where(head_lanes(qb.shape, head), qb, BF16(0))
            s = mm(qm, k_ref[...], NT) + mask_ref[rows, :]
            top = jnp.max(s, axis=1, keepdims=True)
            e = jnp.exp(s - top).astype(BF16)
            o = mm(e, vaug_ref[head], NN)
            t = head // 2
            total = o[:, (1 - t) * UNIT : (2 - t) * UNIT]
            part = o[:, t * UNIT : (t + 1) * UNIT] / total
            halves[t] = part if halves[t] is None else halves[t] + part
            stats = jnp.where(stat_lane == head, top + jnp.log(total), stats)
        ctx_ref[0, rows, :] = halves[0].astype(BF16)
        ctx_ref[1, rows, :] = halves[1].astype(BF16)
        lse_ref[:, rows] = jnp.transpose(stats)[0:8]
        return carry

    lax.fori_loop(0, length // TILE, block, 0, unroll=True)


def attention_forward(here, hidden, far, wq, wk, wv, bq, bv, seg):
    half, width = far.shape
    length = 2 * half
    groups = width // GROUP
    left = pl.BlockSpec((width, UNIT), lambda g, h: (0, g))
    right = pl.BlockSpec((width, UNIT), lambda g, h: (0, groups + g))
    bias_left = pl.BlockSpec((1, UNIT), lambda g, h: (0, g))
    bias_right = pl.BlockSpec((1, UNIT), lambda g, h: (0, groups + g))
    rows = pl.BlockSpec((length, GROUP), lambda g, h: (0, g))
    wide = jax.ShapeDtypeStruct((length, width), BF16)
    own = pl.BlockSpec((1, half, width), lambda g, h: (h[0], 0, 0), pipeline_mode=pl.Buffered(1))
    return run(
        attention_forward_kernel,
        "attention_forward",
        (groups,),
        (here, hidden, far, wq, wq, wk, wk, wv, wv, bq, bq, bv, bv, seg),
        [own, fixed((half, width))]
        + [left, right] * 3
        + [bias_left, bias_right] * 2
        + [fixed((1, length))],
        (
            wide,
            wide,
            wide,
            jax.ShapeDtypeStruct((2, length, width // 2), BF16),
            jax.ShapeDtypeStruct((8 * groups, length), F32),
            wide,
        ),
        (
            rows,
            rows,
            rows,
            pl.BlockSpec((2, length, UNIT), lambda g, h: (0, 0, g)),
            pl.BlockSpec((8, length), lambda g, h: (g, 0)),
            pl.BlockSpec((length, width), lambda g, h: (0, 0)),
        ),
        [pltpu.VMEM((length, length), F32), pltpu.VMEM((PER_GROUP, length, GROUP), BF16)],
        scalars=1,
        micros=16,
    )


def gelu_pair(u):
    phi = 0.5 + 0.5 * lax.erf(u * 0.7071067811865476)
    bell = jnp.exp2(u * u * -0.7213475204444817)
    return (u * phi, phi + u * bell * 0.3989422804014327)


def normed(x):
    centre = x - jnp.mean(x, axis=1, keepdims=True)
    scale = lax.rsqrt(jnp.mean(centre * centre, axis=1, keepdims=True) + EPSILON)
    return (centre * scale, scale)


def norm_back(u, n, scale):
    return scale * (u - jnp.mean(u, axis=1, keepdims=True) - n * jnp.mean(u * n, axis=1, keepdims=True))


def row_sum(x):
    return jnp.sum(x, axis=0, keepdims=True)


def token_kernel(
    here_ref,
    h_ref,
    ctx_ref,
    cot_own_ref,
    cot_far_ref,
    wo_ref,
    wi_ref,
    wp_ref,
    bi_ref,
    vec_ref,
    out_ref,
    far0_ref,
    far1_ref,
    first_ref,
    act_ref,
    og_ref,
    ig_ref,
    fp_ref,
    ag_ref,
    dctx_ref,
    sums_ref,
    isum_ref,
    slope_ref,
):
    step = pl.program_id(0)
    steps = pl.num_programs(0)

    @pl.when(step == 0)
    def _():
        sums_ref[...] = jnp.zeros_like(sums_ref)
        isum_ref[...] = jnp.zeros_like(isum_ref)

    ff = wi_ref.shape[1]
    chunk = 512
    output_bias, gain1, shift1 = vec_ref[0:1, :], vec_ref[1:2, :], vec_ref[2:3, :]
    outer_bias, gain2, shift2 = vec_ref[3:4, :], vec_ref[4:5, :], vec_ref[5:6, :]
    middle = wo_ref.shape[0] // 2
    near = step < steps // 2

    def part(rows):
        ctx = lanes(ctx_ref[0, rows, :], ctx_ref[1, rows, :])
        x = h_ref[rows, :].astype(F32) + mm(ctx, wo_ref[...], NN) + output_bias
        yield
        n1, r1 = normed(x)
        fn = n1 * gain1 + shift1
        first = fn.astype(BF16)
        first_ref[rows, :] = first
        yield
        for c in range(0, ff, chunk):
            act, slope = gelu_pair(mm(first, wi_ref[:, c : c + chunk], NN) + bi_ref[:, c : c + chunk])
            act_ref[rows, c : c + chunk] = act.astype(BF16)
            slope_ref[rows, c : c + chunk] = slope
            yield
        x = fn + mm(act_ref[rows, :], wp_ref[...], NN) + outer_bias
        yield
        n2, r2 = normed(x)
        out = (n2 * gain2 + shift2).astype(BF16)

        out_ref[0, rows, :] = jnp.where(near, out, out_ref[0, rows, :])
        (far1_ref if rows.start else far0_ref)[...] = out
        e = jnp.where(near, cot_own_ref[0, rows, :], cot_far_ref[rows, :]).astype(F32)
        sums_ref[0:1, :] += row_sum(e * n2)
        sums_ref[1:2, :] += row_sum(e)
        sp = norm_back(e * gain2, n2, r2)
        og = sp.astype(BF16)
        og_ref[rows, :] = og
        sums_ref[2:3, :] += row_sum(og.astype(F32))
        yield
        for c in range(0, ff, chunk):
            ig = (mm(og, wp_ref[c : c + chunk, :], NT) * slope_ref[rows, c : c + chunk]).astype(BF16)
            ig_ref[rows, c : c + chunk] = ig
            isum_ref[:, c : c + chunk] += row_sum(ig.astype(F32))
            yield
        d = sp + mm(ig_ref[rows, :], wi_ref[...], NT)
        yield
        sums_ref[3:4, :] += row_sum(d * n1)
        sums_ref[4:5, :] += row_sum(d)
        fp = norm_back(d * gain1, n1, r1)
        fp_ref[rows, :] = fp
        ag = fp.astype(BF16)
        ag_ref[rows, :] = ag
        sums_ref[5:6, :] += row_sum(ag.astype(F32))
        yield
        dctx = mm(ag, wo_ref[...], NT).astype(BF16)
        dctx_ref[0, rows, :] = dctx[:, :middle]
        dctx_ref[1, rows, :] = dctx[:, middle:]

    size = h_ref.shape[0]
    parts = [part(slice(r, r + TILE)) for r in range(0, size, TILE)]
    live, waiting = [], list(parts)
    while waiting or live:
        if waiting:
            live.append(waiting.pop(0))
        live = [p for p in live if next(p, 0) is None]


def token_pass(here, h, ctx, cot, cot_far, wo, wi, wp, bi, vec):
    length, width = h.shape
    half = length // 2
    ff = wi.shape[1]
    steps = length // TOKENS
    near = steps // 2
    rows = pl.BlockSpec((TOKENS, width), lambda i, b: (i, 0))
    split_rows = pl.BlockSpec((2, TOKENS, width // 2), lambda i, b: (0, i, 0))
    wide_rows = pl.BlockSpec((TOKENS, ff), lambda i, b: (i, 0))
    own_rows = pl.BlockSpec((1, TOKENS, width), lambda i, b: (b[0], jnp.minimum(i, near - 1), 0))
    far_rows = pl.BlockSpec((TOKENS, width), lambda i, b: (jnp.maximum(i - near, 0), 0))
    low = jax.ShapeDtypeStruct((length, width), BF16)
    low_ff = jax.ShapeDtypeStruct((length, ff), BF16)
    return run(
        token_kernel,
        "token_pass",
        (steps,),
        (here, h, ctx, cot, cot_far, wo, wi, wp, bi, vec),
        [
            rows,
            split_rows,
            own_rows,
            far_rows,
            fixed((width, width)),
            fixed((width, ff)),
            fixed((ff, width)),
            fixed((1, ff)),
            fixed((8, width)),
        ],
        (
            jax.ShapeDtypeStruct((2, half, width), BF16),
            jax.ShapeDtypeStruct((half // 2, width), BF16),
            jax.ShapeDtypeStruct((half // 2, width), BF16),
            low,
            low_ff,
            low,
            low_ff,
            jax.ShapeDtypeStruct((length, width), F32),
            low,
            jax.ShapeDtypeStruct((2, length, width // 2), BF16),
            jax.ShapeDtypeStruct((8, width), F32),
            jax.ShapeDtypeStruct((1, ff), F32),
        ),
        (
            own_rows,
            pl.BlockSpec((half // 2, width), lambda i, b: (0, 0)),
            pl.BlockSpec((half // 2, width), lambda i, b: (0, 0)),
            rows,
            wide_rows,
            rows,
            wide_rows,
            rows,
            rows,
            split_rows,
            pl.BlockSpec((8, width), lambda i, b: (0, 0)),
            pl.BlockSpec((1, ff), lambda i, b: (0, 0)),
        ),
        [pltpu.VMEM((TOKENS, ff), F32)],
        scalars=1,
        micros=23,
    )


def put_pairs(a, b, core_ref, keep_ref, send_ref, columns, rows, count):
    even = core_ref[0] == 0
    for z in range(count):
        if z % 2 == 0:
            res = mm(a[:, 4 * z * rows : 4 * (z + 2) * rows], b, TN)
        for y in range(2):
            base = (z % 2 * 2 + y) * 2 * rows
            for x in range(2):
                zero = lanes(*[res[base : base + rows, c] for c in columns[x]])
                one = lanes(*[res[base + rows : base + 2 * rows, c] for c in columns[x]])
                keep_ref[x, y, z, 0] = jnp.where(even, zero, one).astype(BF16)
                send_ref[x, y, z, 0] = jnp.where(even, one, zero).astype(BF16)


HALVES = ((slice(0, 384),), (slice(384, 768),))
VECTOR_ROWS = 32
BIAS_ROWS = 16


def outer_grad_kernel(core_ref, act_ref, og_ref, sums_ref, isum_ref, keep_ref, send_ref, rows_ref):
    middle = og_ref.shape[1] // 2
    rows = act_ref.shape[1] // 4
    even = core_ref[0] == 0
    rows_ref[...] = jnp.zeros_like(rows_ref)
    at = 0
    for r in range(6):
        for x in range(2):
            rows_ref[at : at + 1, :] = sums_ref[r : r + 1, x * middle : (x + 1) * middle]
            at += 1
    for r in range(isum_ref.shape[1] // middle):
        rows_ref[at : at + 1, :] = isum_ref[:, r * middle : (r + 1) * middle]
        at += 1
    extra = rows_ref[...].astype(BF16)
    for y in range(2):
        res = mm(act_ref[:, 2 * y * rows : 2 * (y + 1) * rows], og_ref[...], TN)
        for x in range(2):
            columns = slice(x * middle, (x + 1) * middle)
            zero = res[0:rows, columns]
            one = res[rows:, columns]
            keep_ref[y, x, 0, 0:rows, :] = jnp.where(even, zero, one).astype(BF16)
            send_ref[y, x, 0, 0:rows, :] = jnp.where(even, one, zero).astype(BF16)
            keep_ref[y, x, 0, rows:, :] = extra
            send_ref[y, x, 0, rows:, :] = extra


def pair_out(shape, block, index):
    kind = jax.ShapeDtypeStruct(shape, BF16)
    spec = pl.BlockSpec(block, index)
    return ((kind, kind), (spec, spec))


def outer_grad_call(core, act, og, sums, isum):
    length, ff = act.shape
    width = og.shape[1]
    shape = (2, 2, 4, ff // 16 + VECTOR_ROWS, width // 2)
    kinds, specs = pair_out(shape, (2, 2, 1) + shape[3:], lambda z: (0, 0, z, 0, 0))
    return run(
        outer_grad_kernel,
        "outer_grad",
        (4,),
        (core, act, og, sums, isum),
        [
            SCALAR,
            pl.BlockSpec((length, ff // 4), lambda z: (0, z)),
            fixed((length, width)),
            fixed(sums.shape),
            fixed(isum.shape),
        ],
        kinds,
        specs,
        [pltpu.VMEM((VECTOR_ROWS, width // 2), F32)],
        micros=4.5,
    )


def inner_grad_kernel(
    core_ref, first_ref, low_ref, high_ref, ctx_ref, ag_ref, keep_ref, send_ref
):
    step = pl.program_id(0)
    rows = keep_ref.shape[4]

    @pl.when(step < 4)
    def _():
        both = lanes(low_ref[...], high_ref[...])
        put_pairs(first_ref[...], both, core_ref, keep_ref, send_ref, HALVES, rows, 4)

    @pl.when(step == 4)
    def _():
        ctx = lanes(ctx_ref[0], ctx_ref[1])
        put_pairs(ctx, ag_ref[...], core_ref, keep_ref, send_ref, HALVES, rows, 4)


def inner_grad_call(core, first, ig, ctx, ag, passes):
    length, width = first.shape
    shape = (2, 2, 4, 5, width // 16, width // 2)
    kinds, specs = pair_out(shape, shape[:3] + (1,) + shape[4:], lambda s: (0, 0, 0, s, 0, 0))
    return run(
        inner_grad_kernel,
        "inner_grad",
        (5,),
        (core, first, ig, ig, ctx, ag),
        [
            SCALAR,
            fixed((length, width)),
            pl.BlockSpec((length, width // 2), lambda s: (0, jnp.minimum(s, 3))),
            pl.BlockSpec((length, width // 2), lambda s: (0, 4 + jnp.minimum(s, 3))),
            fixed((2, length, width // 2)),
            fixed((length, width)),
        ],
        kinds,
        specs,
        passes=passes,
        micros=6,
    )


def rounded(x):
    return x.astype(BF16).astype(F32)


def halve_first_kernel(at_ref, keep_ref, came_ref, out_ref):
    out_ref[...] = (keep_ref[0].astype(F32) + came_ref[0].astype(F32)).astype(BF16)


def halve_first(at, axis, keep, came, passes):
    _, _, depth, rows, width = keep.shape
    half = pl.BlockSpec((1, 2, depth, rows, width), lambda i, s: (1 - s[axis], 0, 0, 0, 0))
    return run(
        halve_first_kernel,
        "halve_first",
        (1,),
        (at, keep, came),
        [half, half],
        (jax.ShapeDtypeStruct((2, depth, rows, width), BF16),),
        (fixed((2, depth, rows, width)),),
        scalars=1,
        passes=passes,
    )


def sum_second(keep, came, came1):
    total = rounded(keep.astype(F32) + came.astype(F32))
    return rounded(total + came1.astype(F32))


def quarter_kernel(plan, at_ref, *refs):
    outs = refs[-4:]
    here = at_ref[2]
    for d in range(4):
        z = lax.bitwise_xor(here, d)
        for first, count, row, column, through in plan:
            keep_ref, came_ref, came1_ref = refs[first : first + 3]
            came2_ref = refs[through]
            rows, part = keep_ref.shape[3:]
            total = sum_second(keep_ref[0, 0, z], came_ref[0, 0, z], came1_ref[0, z])
            came2 = came2_ref[z, :, column : column + part]
            outs[d][row : row + rows, column : column + part] = rounded(
                total + came2.astype(F32)
            ).astype(BF16)


def quarter(at, states, total_rows, total_width, passes, after):
    specs, operands, plan, seen = [], [], [], {}
    for keep, came, came1, came2, axis, row, column in states:
        _, _, depth, rows, part = keep.shape
        if axis == 0:
            both = pl.BlockSpec((1, 1, depth, rows, part), lambda i, s: (s[0], s[1], 0, 0, 0))
            one = pl.BlockSpec((1, depth, rows, part), lambda i, s: (s[1], 0, 0, 0))
        else:
            both = pl.BlockSpec((1, 1, depth, rows, part), lambda i, s: (s[1], s[0], 0, 0, 0))
            one = pl.BlockSpec((1, depth, rows, part), lambda i, s: (s[0], 0, 0, 0))
        first = len(operands)
        specs += [both, both, one]
        operands += [keep, came, came1]
        if id(came2) not in seen:
            seen[id(came2)] = len(operands)
            specs.append(fixed(came2.shape))
            operands.append(came2)
        plan.append((first, 3, row, column, seen[id(came2)]))
    part = jax.ShapeDtypeStruct((total_rows, total_width), BF16)
    return run(
        functools.partial(quarter_kernel, plan),
        "quarter",
        (1,),
        (at, *operands),
        specs,
        (part,) * 4,
        (pl.BlockSpec((total_rows, total_width), lambda i, s: (0, 0)),) * 4,
        scalars=1,
        passes=passes,
        after=after,
    )


def projection_part(core_ref, h_ref, grads, sums, keep_ref, send_ref):
    rows = h_ref.shape[1] // 16
    even = core_ref[0] == 0
    for s in range(3):
        place = slice(s * rows, (s + 1) * rows)
        parts = [mm(h_ref[...], ref[s], TN) for ref in grads]
        for z in range(4):
            for y in range(2):
                base = (z * 2 + y) * 2 * rows
                for x in range(2):
                    unit = slice(x * UNIT, (x + 1) * UNIT)
                    zero = lanes(*[p[base : base + rows, unit] for p in parts])
                    one = lanes(*[p[base + rows : base + 2 * rows, unit] for p in parts])
                    keep_ref[y, x, z, place, :] = jnp.where(even, zero, one).astype(BF16)
                    send_ref[y, x, z, place, :] = jnp.where(even, one, zero).astype(BF16)
    extra = jnp.zeros((BIAS_ROWS, keep_ref.shape[4]), F32)
    at = lax.broadcasted_iota(jnp.int32, extra.shape, 0)
    for r in range(2):
        for g, ref in enumerate(sums):
            for x in range(2):
                part = ref[r : r + 1, x * UNIT : (x + 1) * UNIT]
                extra = jnp.where(at == (2 * r + x) * len(sums) + g, part, extra)
    for z in range(4):
        for y in range(2):
            for x in range(2):
                keep_ref[y, x, z, 3 * rows :, :] = extra.astype(BF16)
                send_ref[y, x, z, 3 * rows :, :] = extra.astype(BF16)


def attention_backward_kernel(
    others,
    before,
    q_ref,
    k_ref,
    v_ref,
    dctx_pair_ref,
    ctx_pair_ref,
    lse_ref,
    seg_ref,
    *refs,
):
    delta_ref, total_ref, kt_ref, dctx_ref, segc_ref = refs[-5:]
    if others is None:
        grads_ref, sums_ref = refs[:2]
    else:
        core_ref, h_ref = refs[:2]
        other_refs = refs[2 : 2 + others]
        before_refs = refs[2 + others : 2 + others + before]
        grads_ref, sums_ref, keep_ref, send_ref = refs[-9:-5]
    length = q_ref.shape[0]
    dctx_ref[...] = lanes(dctx_pair_ref[0], dctx_pair_ref[1])
    ctx = lanes(ctx_pair_ref[0], ctx_pair_ref[1])
    segr = seg_ref[...].astype(F32)
    segc_ref[...] = column_of(segr)
    prod = dctx_ref[...].astype(F32) * ctx.astype(F32)
    high = prod.astype(BF16)
    rest = (prod - high.astype(F32)).astype(BF16)
    lane = lax.broadcasted_iota(jnp.int32, (8, GROUP), 1)
    head_of = lax.broadcasted_iota(jnp.int32, (8, GROUP), 0)
    chooser = jnp.where(lane // HEAD == head_of, 1.0, 0.0).astype(BF16)
    delta_ref[...] = mm(chooser, high, NT) + mm(chooser, rest, NT)
    total_ref[...] = jnp.zeros_like(total_ref)
    kt_ref[...] = jnp.transpose(k_ref[...])

    def block(j, carry):
        rows = pl.ds(pl.multiple_of(j * KEYS, KEYS), KEYS)
        kb = k_ref[rows, :]
        vb = v_ref[rows, :]
        mask = jnp.where(segc_ref[rows, :] == segr, 0.0, NEGATIVE)
        dk = jnp.zeros((KEYS, GROUP), F32)
        dv = jnp.zeros((KEYS, GROUP), F32)
        for head in range(PER_GROUP):
            mine = head_lanes((KEYS, GROUP), head)
            km = jnp.where(mine, kb, BF16(0)) * BF16(HEAD**-0.5)
            vm = jnp.where(mine, vb, BF16(0))
            s = mm(km, q_ref[...], NT) + mask
            p = jnp.exp(s - lse_ref[head : head + 1, :])
            dp = mm(vm, dctx_ref[...], NT)
            ds = (p * (dp - delta_ref[head : head + 1, :])).astype(BF16)
            dv = jnp.where(mine, mm(p.astype(BF16), dctx_ref[...], NN), dv)
            dk = jnp.where(mine, mm(ds, q_ref[...], NN), dk)
            columns = slice(head * HEAD, (head + 1) * HEAD)
            total_ref[columns, :] += mm(kt_ref[columns, rows], ds, NN)
        dkb = (dk * HEAD**-0.5).astype(BF16)
        dvb = dv.astype(BF16)
        grads_ref[1, rows, :] = dkb
        grads_ref[2, rows, :] = dvb
        return carry + row_sum(dvb.astype(F32))

    dv_sum = lax.fori_loop(0, length // KEYS, block, jnp.zeros((1, GROUP), F32), unroll=True)
    dq = jnp.transpose(total_ref[...] * HEAD**-0.5).astype(BF16)
    grads_ref[0] = dq
    sums_ref[...] = jnp.zeros_like(sums_ref)
    sums_ref[0:1, :] = row_sum(dq.astype(F32))
    sums_ref[1:2, :] = dv_sum
    if others is not None:
        sums = (*before_refs, sums_ref) if before else ()
        projection_part(core_ref, h_ref, (*other_refs, grads_ref), sums, keep_ref, send_ref)


def attention_backward(g, q, k, v, dctx, ctx, lse, seg, weights, passes, after):
    length, width = q.shape
    rows = pl.BlockSpec((length, GROUP), lambda i: (0, g))
    pair_rows = pl.BlockSpec((2, length, UNIT), lambda i: (0, 0, g))
    operands = [q, k, v, dctx, ctx, lse, seg]
    specs = [
        rows,
        rows,
        rows,
        pair_rows,
        pair_rows,
        pl.BlockSpec((8, length), lambda i: (g, 0)),
        fixed((1, length)),
    ]
    kinds = [jax.ShapeDtypeStruct((3, length, GROUP), BF16), jax.ShapeDtypeStruct((8, GROUP), F32)]
    outs = [fixed((3, length, GROUP)), fixed((8, GROUP))]
    others, before = None, 0
    if weights:
        core, h, grads, sums = weights
        others, before = len(grads), len(sums)
        operands += [core, h, *grads, *sums]
        specs += [SCALAR] + [fixed(x.shape) for x in (h, *grads, *sums)]
        shape = (2, 2, 4, 3 * width // 16 + BIAS_ROWS, (others + 1) * UNIT)
        kinds += [jax.ShapeDtypeStruct(shape, BF16)] * 2
        outs += [fixed(shape)] * 2
    return run(
        functools.partial(attention_backward_kernel, others, before),
        "attention_backward",
        (1,),
        tuple(operands),
        specs,
        kinds,
        outs,
        [
            pltpu.VMEM((8, length), F32),
            pltpu.VMEM((GROUP, length), F32),
            pltpu.VMEM((GROUP, length), BF16),
            pltpu.VMEM((length, GROUP), BF16),
            pltpu.VMEM((length, 1), F32),
        ],
        passes=passes,
        after=after,
        micros=8,
    )


def hidden_total(fp_ref, d_refs, w_refs):
    total = fp_ref[...]
    for at, w_ref in enumerate(w_refs):
        d = lanes(*[ref[at, :, x * UNIT : (x + 1) * UNIT] for x in range(2) for ref in d_refs])
        total = total + mm(d, w_ref[...], NT)
    return total


def hidden_away_kernel(fp_ref, *refs):
    refs[6][...] = hidden_total(fp_ref, refs[:3], refs[3:6]).astype(BF16)


def hidden_home_kernel(here_ref, fp_ref, *refs):
    came0_ref, came1_ref, out_ref, layer_ref = refs[6:]
    out_ref[0] = hidden_total(fp_ref, refs[:3], refs[3:6])
    layer_ref[0] = jnp.where(pl.program_id(0) == 0, came0_ref[...], came1_ref[...])


def hidden_away(fp, d0, d1, d2, wq, wk, wv, passes, after):
    length, width = fp.shape
    half = length // 2
    steps = half // TILE
    return run(
        hidden_away_kernel,
        "hidden_away",
        (steps,),
        (fp, d0, d1, d2, wq, wk, wv),
        [
            pl.BlockSpec((TILE, width), lambda i: (i + steps, 0)),
        ]
        + [pl.BlockSpec((3, TILE, GROUP), lambda i: (0, i + steps, 0))] * 3
        + [fixed((width, width))] * 3,
        (jax.ShapeDtypeStruct((half, width), BF16),),
        (pl.BlockSpec((TILE, width), lambda i: (i, 0)),),
        passes=passes,
        after=after,
        micros=3,
    )


def hidden_home(here, fp, d0, d1, d2, wq, wk, wv, came0, came1, layer, passes, after):
    length, width = fp.shape
    half = length // 2
    steps = half // TILE
    return run(
        hidden_home_kernel,
        "hidden_home",
        (steps,),
        (here, fp, d0, d1, d2, wq, wk, wv, came0, came1),
        [
            pl.BlockSpec((TILE, width), lambda i, b: (i, 0)),
        ]
        + [pl.BlockSpec((3, TILE, GROUP), lambda i, b: (0, i, 0))] * 3
        + [fixed((width, width))] * 3
        + [fixed((TILE, width))] * 2,
        (
            jax.ShapeDtypeStruct((2, half, width), F32),
            jax.ShapeDtypeStruct((2, half, width), BF16),
        ),
        (
            pl.BlockSpec((1, TILE, width), lambda i, b: (b[0], i, 0)),
            pl.BlockSpec((1, TILE, width), lambda i, b: (1 - b[0], i, 0)),
        ),
        scalars=1,
        held={1: layer},
        passes=passes,
        after=after,
        micros=3,
    )


def place_kernel(here_ref, came_ref, out_ref):
    out_ref[0] = came_ref[...].astype(F32)


def place_far(here, came, grad, passes):
    half, width = came.shape
    return run(
        place_kernel,
        "place_far",
        (2,),
        (here, came),
        [pl.BlockSpec((half // 2, width), lambda i, b: (i, 0))],
        (jax.ShapeDtypeStruct((2, half, width), F32),),
        (pl.BlockSpec((1, half // 2, width), lambda i, b: (1 - b[0], i, 0)),),
        scalars=1,
        held={0: grad},
        passes=passes,
        micros=1,
    )


def fast(
    hidden,
    segments,
    query_matrix,
    query_bias,
    key_matrix,
    value_matrix,
    value_bias,
    output_matrix,
    output_bias,
    first_gain,
    first_shift,
    inner_matrix,
    inner_bias,
    outer_matrix,
    outer_bias,
    second_gain,
    second_shift,
    cotangent,
):
    here = lax.axis_index("blk")
    place = lax.axis_index("seq")
    core, y_at, z_at = place % 2, (place // 2) % 2, place // 4
    here_id = here.astype(jnp.int32)[None]
    core_id = core.astype(jnp.int32)[None]
    half, width = hidden.shape[1:]

    def pick(x, *at):
        start = at + (0,) * (x.ndim - len(at))
        size = (1,) * len(at) + x.shape[len(at) :]
        return lax.dynamic_slice(x, start, size).reshape(x.shape[len(at) :])

    def trade(x):
        return lax.ppermute(x, "blk", [(0, 1), (1, 0)])

    def seq_swap(x, bit):
        return lax.ppermute(x, "seq", [(i, i ^ bit) for i in range(16)])

    def row(x):
        return x.astype(F32)[None, :]

    at = jnp.stack([here, y_at, z_at]).astype(jnp.int32)

    def rounded(x):
        return lax.reduce_precision(x, 8, 7)

    def sum_0(state, *at):
        return rounded(pick(state[0], *at).astype(F32) + pick(state[1], *at).astype(F32))

    def sum_1(state, mine, *at):
        return rounded(sum_0(state, mine, *at) + pick(state[2], *at).astype(F32))

    def sum_2(state, mine, then, *at):
        return rounded(sum_1(state, mine, then, *at) + pick(state[3], *at).astype(F32))

    def send_z(parts):
        return [seq_swap(x, 4 * d) for d, x in zip((1, 2, 3), parts)]

    def add_z(total, parts):
        return (total + parts[0].astype(F32)) + (parts[1].astype(F32) + parts[2].astype(F32))

    seg = jnp.concatenate([pick(segments, here), trade(pick(segments, 1 - here))])[None, :]
    far = trade(pick(hidden, 1 - here))
    cot_far = trade(pick(cotangent, 1 - here + jnp.minimum(seg[0, -1], 0)))
    q, k, v, ctx, lse, h = attention_forward(
        here_id,
        hidden,
        far,
        query_matrix,
        key_matrix,
        value_matrix,
        row(query_bias),
        row(value_bias),
        seg,
    )
    empty = jnp.zeros((2, width), F32)
    vec = jnp.concatenate(
        [
            row(output_bias),
            row(first_gain),
            row(first_shift),
            row(outer_bias),
            row(second_gain),
            row(second_shift),
            empty,
        ],
        axis=0,
    )
    out, out_far0, out_far1, first, act, og, ig, fp, ag, dctx, sums, isum = token_pass(
        here_id, h, ctx, cotangent, cot_far, output_matrix, inner_matrix, outer_matrix, row(inner_bias), vec
    )
    x_mine, x_away, y_mine, y_away = here, 1 - here, y_at, 1 - y_at
    a_keep, a_send = outer_grad_call(core_id, act, og, sums, isum)
    a0 = seq_swap(a_send, 1)
    b_keep, b_send, a_keep = inner_grad_call(core_id, first, ig, ctx, ag, (a_keep,))
    b0 = seq_swap(b_send, 1)
    a = (a_keep, a0)
    a_away, out_far0 = halve_first(at, 1, a_keep, a0, (out_far0,))
    a1 = seq_swap(a_away, 2)
    out_came0 = trade(out_far0)
    b = (b_keep, b0)
    b_away = sum_0(b, x_away).astype(BF16)
    b1 = trade(b_away)
    bwd = (q, k, v, dctx, ctx, lse, seg)
    grads0, bias0 = attention_backward(0, *bwd, (), (), (a_away, b_away))
    grads1, bias1, c_keep, c_send, a_keep, b_keep, out_came0, out_far1 = attention_backward(
        1, *bwd, (core_id, h, (grads0,), ()), (a_keep, b_keep, out_came0, out_far1), ()
    )
    out_came1 = trade(out_far1)
    c0 = seq_swap(c_send, 1)
    a = (a_keep, a0, a1)
    a_away = sum_1(a, y_mine, x_away).astype(BF16)
    a2 = trade(a_away)
    b = (b_keep, b0, b1)
    b_away = sum_1(b, x_mine, y_away).astype(BF16)
    b2 = seq_swap(b_away, 2)
    grads2, _, d_keep, d_send, a_keep, b_keep, c_keep = attention_backward(
        2, *bwd, (core_id, h, (), (bias0, bias1)), (a_keep, b_keep, c_keep), (a_away, b_away)
    )
    d0 = seq_swap(d_send, 1)
    c = (c_keep, c0)
    c_away = sum_0(c, y_away).astype(BF16)
    c1 = seq_swap(c_away, 2)

    def flat(x):
        return x.reshape(*x.shape[:-3], -1, x.shape[-1])

    a_rows, b_rows = a_keep.shape[3], 5 * width // 16
    states = [
        (a_keep, a0, a1, a2, 1, 0, 0),
        (flat(b_keep), flat(b0), flat(b1), flat(b2), 0, a_rows, 0),
    ]
    ab_mine, *parts, out_came1, d_keep = quarter(
        at, states, a_rows + b_rows, width // 2, (out_came1, d_keep), (c_away,)
    )
    ab3 = send_z(parts)
    args = (fp, grads0, grads1, grads2, query_matrix, key_matrix, value_matrix)
    d = (d_keep, d0)
    d_away = sum_0(d, y_away).astype(BF16)
    d1 = seq_swap(d_away, 2)
    hidden_grad, layer_out, c_keep, d_keep = hidden_home(
        here_id, *args, out_came0, out_came1, out, (c_keep, d_keep), (d_away,)
    )
    c = (c_keep, c0, c1)
    d = (d_keep, d0, d1)

    def lanes_of(*parts):
        return jnp.concatenate(parts, axis=-1)

    def late_1(*at):
        return lanes_of(sum_1(c, y_mine, *at), sum_1(d, y_mine, *at))

    e_away = late_1(x_away).astype(BF16)
    e2 = trade(e_away)
    far_grad, c_keep, d_keep, ab_mine = hidden_away(*args, (c_keep, d_keep, ab_mine), (e_away,))
    came = trade(far_grad)
    c = (c_keep, c0, c1)
    d = (d_keep, d0, d1)

    def late_2(z):
        return rounded(late_1(x_mine, z) + pick(e2, z).astype(F32))

    e3 = send_z([late_2(z_at ^ e).astype(BF16) for e in (1, 2, 3)])
    early = add_z(ab_mine.astype(F32), ab3)
    hidden_grad = place_far(here_id, came, hidden_grad, ())[0]
    late = add_z(late_2(z_at), e3)
    rows = width // 16
    outer_rows = 4 * rows
    outer_grad = early[:outer_rows]
    vectors = early[outer_rows : outer_rows + VECTOR_ROWS].reshape(-1, width)
    inner_all = early[outer_rows + VECTOR_ROWS :].reshape(5, rows, width // 2)
    output_grad = inner_all[4]
    inner_grad = jnp.transpose(inner_all[:4], (1, 0, 2)).reshape(rows, -1)
    units = width // UNIT
    biases = late[3 * rows :, 2 * UNIT :][: 2 * units].reshape(2, width)
    return (
        layer_out,
        hidden_grad,
        late[:rows],
        biases[0],
        late[rows : 2 * rows],
        late[2 * rows : 3 * rows],
        biases[1],
        output_grad,
        vectors[5],
        vectors[3],
        vectors[4],
        inner_grad,
        vectors[6:10].reshape(-1),
        outer_grad,
        vectors[2],
        vectors[0],
        vectors[1],
    )


def choose(sizes, *args):
    seq_count, row_count, width = args[0].shape
    whole_here = sizes[1] == 2 and seq_count == 2 and row_count == 2 * TILE and width == 3 * GROUP
    return fast(*args) if whole_here and sizes[0] == 16 else general(*args)


def solution(mesh):
    sizes = (mesh.shape["seq"], mesh.shape["blk"])
    return jax.shard_map(
        functools.partial(choose, sizes),
        mesh=mesh,
        in_specs=(
            P("seq", "blk", None),
            P("seq", "blk"),
            P(),
            P(),
            P(),
            P(),
            P(),
            P(),
            P(),
            P(),
            P(),
            P(),
            P(),
            P(),
            P(),
            P(),
            P(),
            P("seq", "blk", None),
        ),
        out_specs=(
            P("seq", "blk", None),
            P("seq", "blk", None),
            P("seq", "blk"),
            P(),
            P("seq", "blk"),
            P("seq", "blk"),
            P(),
            P("seq", "blk"),
            P(),
            P(),
            P(),
            P("seq", "blk"),
            P(),
            P("seq", "blk"),
            P(),
            P(),
            P(),
        ),
        check_vma=False,
    )
```
